32 devices in a mesh: wide: 8 (over z, y), narrow: 4 (over x, core).
Axes of the slice: x: 2, y: 2, z: 4, core: 2. Of those that a mesh axis runs over, the one named last changes fastest.
Arguments:
- tokens: bfloat16 [4, 1024, 1024], P(None, 'wide'), may hold values from -6 to 6
- documents: int32 [4, 1024], replicated, may hold values from 0 to 5, as said below
- prenorm: bfloat16 [1024], P('wide'), may hold values from 0.5 to 1.5
- qheads: bfloat16 [1024, 96], P('wide', 'narrow'), may hold values from -0.25 to 0.25
- qshared: bfloat16 [1024, 384], P('wide', 'narrow'), may hold values from -0.25 to 0.25
- kheads: bfloat16 [1024, 32], P('wide', 'narrow'), may hold values from -0.25 to 0.25
- kshared: bfloat16 [1024, 128], P('wide', 'narrow'), may hold values from -0.25 to 0.25
- vheads: bfloat16 [1024, 32], P('wide', 'narrow'), may hold values from -0.1875 to 0.1875
- vshared: bfloat16 [1024, 128], P('wide', 'narrow'), may hold values from -0.1875 to 0.1875
- project: bfloat16 [1024, 1024], P('narrow', 'wide'), may hold values from -1.5 to 1.5
- midnorm: bfloat16 [1024], P('wide'), may hold values from 0.5 to 1.5
- gating: bfloat16 [1024, 2816], P('wide', 'narrow'), may hold values from -0.1875 to 0.1875
- upward: bfloat16 [1024, 2816], P('wide', 'narrow'), may hold values from -0.1875 to 0.1875
- downward: bfloat16 [2816, 1024], P('narrow', 'wide'), may hold values from -0.109375 to 0.109375
- cotangent: bfloat16 [4, 1024, 1024], P(None, 'wide'), may hold values from -6 to 6
Outputs:
- output: bfloat16 [4, 1024, 1024], P(None, 'wide')
- tokens_gradient: float32 [4, 1024, 1024], P(None, 'wide')
- prenorm_gradient: float32 [1024], P('wide')
- qheads_gradient: float32 [1024, 96], P('wide', 'narrow')
- qshared_gradient: float32 [1024, 384], P('wide', 'narrow')
- kheads_gradient: float32 [1024, 32], P('wide', 'narrow')
- kshared_gradient: float32 [1024, 128], P('wide', 'narrow')
- vheads_gradient: float32 [1024, 32], P('wide', 'narrow')
- vshared_gradient: float32 [1024, 128], P('wide', 'narrow')
- project_gradient: float32 [1024, 1024], P('narrow', 'wide')
- midnorm_gradient: float32 [1024], P('wide')
- gating_gradient: float32 [1024, 2816], P('wide', 'narrow')
- upward_gradient: float32 [1024, 2816], P('wide', 'narrow')
- downward_gradient: float32 [2816, 1024], P('narrow', 'wide')
The draws below stay inside these ranges and needn't reach their ends.
Inputs may be any that keep to these rules, and one draw needn't show every extreme that they name: Along each row the ids start at 0 and rise by one at each document boundary. One row, drawn from the seed, holds a single document; every other row holds 4 to 6 documents of 128 tokens or more, and the row after the single-document row (the first row after the last) holds 6.
All inputs are finite; a program needn't handle non-finite values.
Results may differ from the reference program's by a relative error of at most 0.024.
Values may be sent and summed in bfloat16 or wider, within the bound.
A program may use at most 128 MiB of HBM per device.

```python
import math
import jax
import jax.numpy as jnp
from jax import lax

D = 1024
HEADS = 16
DH = 64
QR = 6
KR = 2
VR = 2
FF = 2816
ROWS = 4
LENGTH = 1024


def draw_documents(key, part):
    key = jax.random.fold_in(key, 11)
    single_key, count_key, jitter_key = jax.random.split(key, 3)
    single = jax.random.randint(single_key, (), 0, ROWS, dtype=jnp.int32)
    row_index = jnp.arange(ROWS, dtype=jnp.int32)
    counts = jax.random.randint(count_key, (ROWS,), 4, 7, dtype=jnp.int32)
    counts = jnp.where(row_index == (single + 1) % ROWS, 6, counts)
    counts = jnp.where(row_index == single, 1, counts)
    spacing = LENGTH // counts
    spread = (spacing - LENGTH // 8) // 2
    ordinal = jnp.arange(1, 6, dtype=jnp.int32)[None, :]
    jitter = jax.random.randint(jitter_key, (ROWS, 5), -spread[:, None], spread[:, None] + 1, dtype=jnp.int32)
    bounds = ordinal * spacing[:, None] + jitter
    bounds = jnp.where(ordinal < counts[:, None], bounds, LENGTH)
    places = jnp.arange(LENGTH, dtype=jnp.int32)
    return jnp.sum((places[None, :, None] >= bounds[:, None, :]).astype(jnp.int32), axis=-1)


def shard_levels(own_key, dims, shards, smallest, high):
    level, own = 1.0, jax.random.fold_in(own_key, 6)
    for dim, parts in shards:
        steps = jnp.exp(jax.random.uniform(jax.random.fold_in(own, dim), (parts,), jnp.float32, smallest / len(shards), high / len(shards)))
        level = level * jnp.repeat(steps, dims[dim] // parts).reshape([-1 if axis == dim else 1 for axis in range(len(dims))])
    return level


def bell_draw(rng, dims, scale, most, shards=(), kind=jnp.bfloat16):
    level = shard_levels(rng, dims, shards, -0.22, 0.18) if shards else 1.0
    drawn = jax.random.normal(rng, dims, jnp.float32) * scale * level
    return jnp.minimum(jnp.maximum(drawn, -most), most).astype(kind)


def setup_inputs(seed: int = 0) -> dict:
    arg_keys = jax.random.split(jax.random.key(seed), 16)
    tokens = bell_draw(arg_keys[0], (ROWS, LENGTH, D), 1.0, 6.0, ((1, 8),))
    documents = draw_documents(jax.random.fold_in(arg_keys[15], 71), 0)
    prenorm = jnp.clip(1.0 + 0.1 * jax.random.normal(arg_keys[2], (D,), jnp.float32), 0.5, 1.5).astype(jnp.bfloat16)
    qheads = bell_draw(arg_keys[3], (D, HEADS * QR), (D // 2) ** -0.5, 0.25, ((0, 8), (1, 4)))
    qshared = bell_draw(arg_keys[4], (D, QR * DH), (D // 2) ** -0.5, 0.25, ((0, 8), (1, 4)))
    kheads = bell_draw(arg_keys[5], (D, HEADS * KR), (D // 2) ** -0.5, 0.25, ((0, 8), (1, 4)))
    kshared = bell_draw(arg_keys[6], (D, KR * DH), (D // 2) ** -0.5, 0.25, ((0, 8), (1, 4)))
    vheads = bell_draw(arg_keys[7], (D, HEADS * VR), D ** -0.5, 0.1875, ((0, 8), (1, 4)))
    vshared = bell_draw(arg_keys[8], (D, VR * DH), D ** -0.5, 0.1875, ((0, 8), (1, 4)))
    project = bell_draw(arg_keys[9], (HEADS * DH, D), (max(1, HEADS * DH * 16 // LENGTH)) ** -0.5, 1.5, ((0, 4), (1, 8)))
    midnorm = jnp.clip(1.0 + 0.1 * jax.random.normal(arg_keys[10], (D,), jnp.float32), 0.5, 1.5).astype(jnp.bfloat16)
    gating = bell_draw(arg_keys[11], (D, FF), D ** -0.5, 0.1875, ((0, 8), (1, 4)))
    upward = bell_draw(arg_keys[12], (D, FF), D ** -0.5, 0.1875, ((0, 8), (1, 4)))
    downward = bell_draw(arg_keys[13], (FF, D), FF ** -0.5, 0.109375, ((0, 4), (1, 8)))
    cotangent = bell_draw(arg_keys[14], (ROWS, LENGTH, D), 1.0, 6.0, ((1, 8),))
    return dict(tokens=tokens, documents=documents, prenorm=prenorm, qheads=qheads, qshared=qshared, kheads=kheads, kshared=kshared, vheads=vheads, vshared=vshared, project=project, midnorm=midnorm, gating=gating, upward=upward, downward=downward, cotangent=cotangent)


epsilon = 1e-06
masked_score = -1e+30
highest = lax.Precision.HIGHEST

@jax.custom_vjp
def low(v):
    return lax.optimization_barrier(v.astype(jnp.bfloat16)).astype(jnp.float32)

@jax.custom_vjp
def low_back(v):
    return v

def low_keep(v):
    return (low(v), None)

def low_pass(kept, grad):
    return (grad,)

def back_keep(v):
    return (v, None)

def back_low(kept, grad):
    return (low(grad),)
low.defvjp(low_keep, low_pass)
low_back.defvjp(back_keep, back_low)

def product(left, right):
    return jnp.dot(left, right, precision=highest, preferred_element_type=jnp.float32)

def normalize(source, scales):
    return source * lax.rsqrt(lax.optimization_barrier(jnp.mean(source * source, axis=-1, keepdims=True)) + epsilon) * scales

def rotate(tensor, positions, direction):
    half_width = tensor.shape[-1] // 2
    frequency = 10000.0 ** (-jnp.arange(half_width, dtype=jnp.float32) / half_width)
    angles = positions.astype(jnp.float32)[:, None] * frequency[None, :]
    cosines = jnp.cos(angles)[:, None, :]
    sines_all = direction * jnp.sin(angles)[:, None, :]
    front_half = tensor[..., :half_width]
    back_half = tensor[..., half_width:]
    return jnp.concatenate([front_half * cosines - back_half * sines_all, back_half * cosines + front_half * sines_all], axis=-1)

def row_forward(params, tokens_row, documents_row):
    prenorm, qheads, qshared, kheads, kshared, vheads, vshared, project, midnorm, gating, upward, downward = params
    length = tokens_row.shape[0]
    places = jnp.arange(length, dtype=jnp.int32)
    normed = low(normalize(tokens_row, prenorm))
    query_heads = low_back(product(normed, qheads)).reshape(length, HEADS, QR)
    query_rotated = rotate(low_back(product(normed, qshared)).reshape(length, QR, DH), places, 1.0)
    queries = low(jnp.einsum('lhr,lrd->lhd', query_heads, query_rotated, precision=highest) / QR)
    key_heads = low(low_back(product(normed, kheads))).reshape(length, HEADS, KR)
    key_shared = low(rotate(low_back(product(normed, kshared)).reshape(length, KR, DH), places, 1.0))
    key_rows = low(jnp.einsum('lhr,lrd->lhd', key_heads, key_shared, precision=highest) / KR)
    value_heads = low(low_back(product(normed, vheads))).reshape(length, HEADS, VR)
    value_shared = low(low_back(product(normed, vshared))).reshape(length, VR, DH)
    value_rows = low(jnp.einsum('lhr,lrd->lhd', value_heads, value_shared, precision=highest) / VR)
    block_rows = math.gcd(length, 512)

    def attend(block_index):
        first_row = block_index * block_rows
        query_block = lax.dynamic_slice_in_dim(queries, first_row, block_rows, 0)
        query_places = first_row + jnp.arange(block_rows, dtype=jnp.int32)
        query_docs = lax.dynamic_slice_in_dim(documents_row, first_row, block_rows, 0)
        scores = low_back(jnp.einsum('qhd,khd->hqk', query_block, key_rows, precision=highest) * DH ** (-0.5))
        allowed = ((places[None, :] <= query_places[:, None]) & (documents_row[None, :] == query_docs[:, None]))[None]
        scores = jnp.where(allowed, scores, masked_score)
        shifted = jnp.where(allowed, jnp.exp(scores - lax.optimization_barrier(jnp.max(scores, axis=-1, keepdims=True))), 0.0)
        probability = shifted / lax.optimization_barrier(jnp.sum(shifted, axis=-1, keepdims=True))
        return jnp.einsum('hqk,khd->qhd', low(probability), value_rows, precision=highest)
    attended = lax.map(jax.checkpoint(attend), jnp.arange(length // block_rows, dtype=jnp.int32))
    mixture = low(low_back(attended.reshape(length, HEADS * DH)))
    middle = tokens_row + low_back(product(mixture, project))
    normed_mid = low(normalize(middle, midnorm))
    gate_values = low_back(product(normed_mid, gating))
    up_values = low_back(product(normed_mid, upward))
    hidden = low(jax.nn.silu(gate_values) * up_values)
    return middle + low_back(product(hidden, downward))

def reference(tokens, documents, prenorm, qheads, qshared, kheads, kshared, vheads, vshared, project, midnorm, gating, upward, downward, cotangent):
    params = tuple((weight.astype(jnp.float32) for weight in (prenorm, qheads, qshared, kheads, kshared, vheads, vshared, project, midnorm, gating, upward, downward)))

    def forward(weights, rows_all):

        def one_row(running, paired):
            return (running, jax.checkpoint(row_forward)(weights, paired[0], paired[1]))
        _, outputs = lax.scan(one_row, jnp.zeros((), jnp.float32), (rows_all, documents))
        return outputs
    result, pullback = jax.vjp(forward, params, tokens.astype(jnp.float32))
    weight_gradients, token_gradients = pullback(cotangent.astype(jnp.float32))
    return (result.astype(jnp.bfloat16), token_gradients, weight_gradients[0], weight_gradients[1], weight_gradients[2], weight_gradients[3], weight_gradients[4], weight_gradients[5], weight_gradients[6], weight_gradients[7], weight_gradients[8], weight_gradients[9], weight_gradients[10], weight_gradients[11])
```

```python
import math
from types import SimpleNamespace

import jax
import jax.numpy as jnp
from jax import lax
from jax.experimental import pallas as pl
from jax.experimental.pallas import tpu as pltpu
from jax.sharding import PartitionSpec as P

DH = 64
QR = 6
KR = 2
VR = 2
LANES = 128

epsilon = 1e-06
masked_score = -1e30
MESH = pl.DeviceIdType.MESH
f32 = jnp.float32
bf16 = jnp.bfloat16


def dot_nn(a, b):
    return lax.dot_general(a, b, (((1,), (0,)), ((), ())), preferred_element_type=f32)


def dot_nt(a, b):
    return lax.dot_general(a, b, (((1,), (1,)), ((), ())), preferred_element_type=f32)


def dot_tn(a, b):
    return lax.dot_general(a, b, (((0,), (0,)), ((), ())), preferred_element_type=f32)


def lane_iota(rows, cols=LANES):
    return lax.broadcasted_iota(jnp.int32, (rows, cols), 1)


def row_iota(rows, cols=LANES):
    return lax.broadcasted_iota(jnp.int32, (rows, cols), 0)


def place_lanes(pieces):
    rows = pieces[0][0].shape[0]
    lane = lane_iota(rows)
    result = jnp.zeros((rows, LANES), f32)
    for tile, start, to, count in pieces:
        shift = (to - start) % LANES
        moved = pltpu.roll(tile, shift, 1) if shift else tile
        result = jnp.where((lane >= to) & (lane < to + count), moved, result)
    return result


def canonical_pieces(tiles, width, first, count, start, to):
    pieces = []
    while count:
        part, inside = divmod(first, width)
        take = min(count, width - inside)
        pieces.append((tiles[part], start + inside, to, take))
        first, to, count = first + take, to + take, count - take
    return pieces


def both_halves(tile):
    low = lane_iota(tile.shape[0]) < DH
    turned = pltpu.roll(tile, DH, 1)
    return jnp.where(low, tile, turned), jnp.where(low, turned, tile)


def swap_quarters(tile):
    low = lane_iota(tile.shape[0]) % DH < DH // 2
    return jnp.where(low, pltpu.roll(tile, LANES - DH // 2, 1), pltpu.roll(tile, DH // 2, 1))


def stack_pair(tile):
    low = lane_iota(tile.shape[0]) < DH
    zero = jnp.zeros_like(tile)
    return jnp.concatenate([jnp.where(low, tile, zero), jnp.where(low, zero, tile)], axis=0)


def unstack_pair(rows):
    half = rows.shape[0] // 2
    low = lane_iota(half) < DH
    return jnp.where(low, rows[:half], rows[half:])


def fold_halves(tile):
    return tile + pltpu.roll(tile, DH, 1)


def row_scale(values):
    return lax.rsqrt(jnp.mean(values * values, axis=-1, keepdims=True) + epsilon)


def make_layout(W, N, T, D, F, L, heads):
    lay = SimpleNamespace()
    lay.W, lay.N, lay.T, lay.D, lay.F, lay.L, lay.heads = W, N, T, D, F, L, heads
    lay.A = W // 2
    lay.RW = D // W
    lay.M = N * T
    lay.FM = F // LANES * LANES
    lay.FP = lay.FM + LANES
    lay.pairs = heads // 2
    lay.KB = L if L <= 1024 else 512
    lay.NB = L // lay.KB
    lay.SQ = QR * DH // N
    lay.SK = KR * DH // N
    lay.HQ = heads * QR // N
    lay.HK = heads * KR // N
    lay.oK, lay.oV = 0, lay.SK
    lay.oq = 2 * lay.SK
    lay.ok = lay.oq + lay.HQ
    lay.ov = lay.ok + lay.HK
    lay.og = lay.ov + lay.HK
    assert N == 4 and W % 8 == 0 and T == LANES and D == heads * DH == 1024
    assert F % LANES == DH and lay.SQ <= LANES and lay.og + 2 <= LANES
    return lay


def scratch_list(y):
    W, N, T, D, L, A, RW, M = y.W, y.N, y.T, y.D, y.L, y.A, y.RW, y.M
    vm = lambda *shape, kind=bf16: pltpu.VMEM(shape, kind)
    GUc = 2 * y.FM + LANES
    return dict(
        WQ=vm(N, D, 256),
        PT=vm(N, D, 256),
        GU=vm(D, GUc),
        DT=vm(D, y.FP),
        KVF=vm(L, 384),
        KP=vm(y.pairs, y.KB, LANES),
        VP=vm(y.pairs, y.KB, LANES),
        EQ=vm(QR, 256, D),
        EK=vm(4, LANES, D),
        BIAS=vm(T, y.KB, kind=f32),
        DOC=vm(T, LANES, kind=f32),
        ROPE=vm(2, T, LANES, kind=f32),
        GAIN=vm(8, D, kind=f32),
        QROT=vm(QR, T, LANES, kind=f32),
        QH=vm(T, 256),
        QP=vm(y.pairs, T, LANES),
        ATT=vm(y.pairs, T, LANES, kind=f32),
        LSE=vm(y.pairs, 2 * T, LANES, kind=f32),
        RUN=vm(y.pairs, 2 * T, LANES, kind=f32),
        MIX=vm(M, D),
        NORM=vm(M, D),
        MID=vm(M, D, kind=f32),
        NM=vm(M, D),
        R2=vm(M, LANES, kind=f32),
        HID=vm(M, y.FP),
        GG=vm(M, GUc),
        MB=vm(M, D),
        MBC=vm(2, T, D),
        MBX=vm(T, D),
        MBS=vm(T, D),
        OP=vm(M, D),
        OPC=vm(2, T, D),
        OPX=vm(T, D),
        OPS=vm(T, D),
        BG=vm(M, D),
        MG=vm(T, D, kind=f32),
        DO=vm(y.pairs, T, LANES),
        QB=vm(y.pairs, T, LANES, kind=f32),
        DKS=vm(4, y.KB, LANES, kind=f32),
        DHD=vm(y.KB, LANES, kind=f32),
        DKVY=vm(A * T, 384),
        DKVR=vm((A - 1) * T, 384),
        DKVO=vm(T, 384, kind=f32),
        QGS=vm(N, T, 256),
        QGR=vm(N, T, 256),
        GS=vm(8, D, kind=f32),
        GR=vm(3, 8, D, kind=f32),
        YGU=vm(A * RW, GUc),
        RGU=vm((A - 1) * RW, GUc),
        PDT=vm(D, y.FP),
        YDT=vm(A * RW, y.FP),
        RDT=vm((A - 1) * RW, y.FP),
        PPT=vm(D, 256),
        YPT=vm(A * RW, 256),
        RPT=vm((A - 1) * RW, 256),
        PQ=vm(D, 256),
        YQ=vm(A * RW, 256),
        RQ=vm((A - 1) * RW, 256),
    )


def block_kernel(y, names, *refs):
    tok, docs, wq_own, gu_own, dt_own, pt_own, cot = refs[:7]
    o_out, o_tok, o_gu, o_dt, o_pt, o_q = refs[7:13]
    s = SimpleNamespace(**dict(zip(names, refs[13:])))
    ssem, rsem = refs[13 + len(names) :]
    W, N, T, D, F, L, A, RW, M = y.W, y.N, y.T, y.D, y.F, y.L, y.A, y.RW, y.M
    FM, FP, KB, pairs = y.FM, y.FP, y.KB, y.pairs
    w = lax.axis_index("wide")
    n = lax.axis_index("narrow")
    zi, yi = w // 2, w % 2
    xo, co = n // 2, n % 2
    y_peer = (zi * 2 + 1 - yi, n)
    c_peer = (w, xo * 2 + 1 - co)
    x_peer = (w, (1 - xo) * 2 + co)
    d_peer = (w, (1 - xo) * 2 + 1 - co)
    turn = lambda step: (zi + step) % A
    z_peer = lambda step: (turn(step) * 2 + yi, n)
    narrow_peers = (c_peer, x_peer, d_peer)
    taken = [0]

    def take(count=1):
        first = taken[0]
        taken[0] += count
        assert taken[0] <= ssem.shape[0]
        return first

    def remote(src, dst, k, peer):
        return pltpu.make_async_remote_copy(
            src_ref=src,
            dst_ref=dst,
            send_sem=ssem.at[k],
            recv_sem=rsem.at[k],
            device_id=peer,
            device_id_type=MESH,
        )

    pending = []

    def send(src, dst, k, peer, started=pending):
        copy = remote(src, dst, k, peer)
        copy.start()
        started.append(copy)

    def arrive(dst, k):
        remote(dst, dst, k, y_peer).wait_recv()

    def rows(ref, first, count):
        return ref.at[pl.ds(pl.multiple_of(first, 16), count)]

    barrier = pltpu.get_barrier_semaphore()
    peers = [y_peer, *narrow_peers] + [z_peer(step) for step in range(1, A)]
    for peer in peers:
        pl.semaphore_signal(barrier, inc=1, device_id=peer, device_id_type=MESH)
    pl.semaphore_wait(barrier, len(peers))

    class Gather:
        def __init__(self, ref, count, first=0, size=None):
            self.ref, self.count, self.first = ref, count, first
            self.size = count if size is None else size
            self.kz, self.ky = take(A), take(A)
            self.started = []

        def sent(self):
            for copy in self.started:
                copy.wait_send()

        def part(self, wide):
            return rows(self.ref, wide * self.count + self.first, self.size)

        def start(self):
            for step in range(1, A):
                send(self.part(w), self.part(w), self.kz + step, z_peer(step), self.started)

        def start_y(self, step):
            part = self.part(turn(-step) * 2 + yi)
            send(part, part, self.ky + step, y_peer, self.started)

        def forward(self, step):
            arrive(self.part(turn(-step) * 2 + yi), self.kz + step)
            self.start_y(step)

        def forward_all(self):
            for step in range(1, A):
                self.forward(step)

        def landed(self, step):
            arrive(self.part(turn(-step) * 2 + 1 - yi), self.ky + step)

        def landed_all(self):
            for step in range(A):
                self.landed(step)

    class Spread:
        def __init__(self, ref):
            self.ref = ref
            self.kx, self.kc, self.kd = take(A), take(A), take(A)

        def part(self, owner, step):
            return rows(self.ref.at[owner], turn(-step) * 2 * RW, 2 * RW)

        def start(self, step):
            send(self.part(n, step), self.part(n, step), self.kx + step, x_peer)
            send(self.part(n, step), self.part(n, step), self.kc + step, c_peer)

        def forward(self, step):
            part = self.part(x_peer[1], step)
            arrive(part, self.kx + step)
            send(part, part, self.kd + step, c_peer)

        def landed(self, step):
            arrive(self.part(c_peer[1], step), self.kc + step)
            arrive(self.part(d_peer[1], step), self.kd + step)

    class Share:
        def __init__(self, ref, chunks):
            self.ref, self.chunks = ref, chunks
            self.kx, self.kc, self.kd = take(chunks), take(chunks), take(chunks)
            self.width = D // chunks

        def part(self, owner, chunk):
            lanes = pl.ds(pl.multiple_of(chunk * self.width, LANES), self.width)
            return self.ref.at[pl.ds(pl.multiple_of(owner * T, T), T), lanes]

        def start(self, chunk):
            send(self.part(n, chunk), self.part(n, chunk), self.kx + chunk, x_peer)
            send(self.part(n, chunk), self.part(n, chunk), self.kc + chunk, c_peer)

        def forward(self, chunk):
            part = self.part(x_peer[1], chunk)
            arrive(part, self.kx + chunk)
            send(part, part, self.kd + chunk, c_peer)

        def landed(self, chunk):
            arrive(self.part(c_peer[1], chunk), self.kc + chunk)
            arrive(self.part(d_peer[1], chunk), self.kd + chunk)

        def finish(self):
            for chunk in range(self.chunks):
                self.forward(chunk)
            for chunk in range(self.chunks):
                self.landed(chunk)

    class NarrowSum:
        def __init__(self, part_ref, core_ref, x_ref, send_ref):
            self.ref, self.core, self.x, self.out = part_ref, core_ref, x_ref, send_ref
            self.kc, self.kx = take(2), take(1)

        def part(self, owner):
            return rows(self.ref, owner * T, T)

        def start(self, far):
            owner = ((1 - xo) if far else xo) * 2 + 1 - co
            send(self.part(owner), self.core.at[int(far)], self.kc + int(far), c_peer)

        def pass_on(self):
            arrive(self.core.at[1], self.kc + 1)
            total = self.part((1 - xo) * 2 + co)[...].astype(f32) + self.core[1].astype(f32)
            self.out[...] = total.astype(bf16)
            send(self.out, self.x, self.kx, x_peer)

        def result(self):
            arrive(self.core.at[0], self.kc)
            arrive(self.x, self.kx)
            return (
                self.part(n)[...].astype(f32) + self.core[0].astype(f32) + self.x[...].astype(f32)
            )

    class WideSum:
        def __init__(self, part_ref, y_ref, z_ref, out_ref, count):
            self.ref, self.y, self.z, self.total = part_ref, y_ref, z_ref, out_ref
            self.count = count
            self.ky, self.kz = take(A), take(A)

        def start(self, group):
            step = (group - zi + A) % A
            send(
                rows(self.ref, (group * 2 + 1 - yi) * self.count, self.count),
                rows(self.y, group * self.count, self.count),
                self.ky + step,
                y_peer,
            )

        def start_all(self):
            for step in range(A):
                self.start(turn(step + 1))

        def pass_on(self, step):
            group = turn(step)
            got = rows(self.y, group * self.count, self.count)
            arrive(got, self.ky + step)
            mine = rows(self.ref, (group * 2 + yi) * self.count, self.count)
            total = mine[...].astype(f32) + got[...].astype(f32)
            if step == 0:
                self.total[...] = total
                return
            mine[...] = total.astype(bf16)
            send(
                mine,
                rows(self.z, (step - 1) * self.count, self.count),
                self.kz + step,
                z_peer(step),
            )

        def finish(self):
            total = self.total[...]
            for step in range(1, A):
                got = rows(self.z, (step - 1) * self.count, self.count)
                arrive(got, self.kz + step)
                total = total + got[...].astype(f32)
            self.total[...] = total

    halves = 2 if RW % 32 == 0 else 1
    part_size = RW // halves
    g_wq = Gather(s.WQ.at[n], RW)
    g_pt = Gather(s.PT.at[n], RW)
    g_kv = Gather(s.KVF, T)
    g_dt = [Gather(s.DT, RW, i * part_size, part_size) for i in range(halves)]
    g_gu = [Gather(s.GU, RW, i * part_size, part_size) for i in range(halves)]
    f_wq, f_pt = Spread(s.WQ), Spread(s.PT)
    h_mix, h_bg, h_og, h_tg = Share(s.MIX, 4), Share(s.BG, 1), Share(o_out, 1), Share(o_tok, 2)
    n_mb = NarrowSum(s.MB, s.MBC, s.MBX, s.MBS)
    n_op = NarrowSum(s.OP, s.OPC, s.OPX, s.OPS)
    w_kv = WideSum(s.KVF, s.DKVY, s.DKVR, s.DKVO, T)
    w_gu = WideSum(s.GU, s.YGU, s.RGU, o_gu, RW)
    w_dt = WideSum(s.PDT, s.YDT, s.RDT, o_dt, RW)
    w_pt = WideSum(s.PPT, s.YPT, s.RPT, o_pt, RW)
    w_q = WideSum(s.PQ, s.YQ, s.RQ, o_q, RW)
    k_a2a, k_gain = take(3), take(3)

    own = pl.ds(pl.multiple_of(w * RW, RW), RW)
    s.WQ[n, own, :] = wq_own[...]
    g_wq.start()
    g_wq.start_y(0)
    s.PT[n, own, :] = pt_own[...]
    s.GU[own, :] = gu_own[...]
    s.DT[own, :] = dt_own[...]

    column, head = row_iota(256, D) & (LANES - 1), lane_iota(256, D) >> 6
    for r in range(QR):
        s.EQ[r] = jnp.where(column == head * QR + r, 1.0, 0.0).astype(bf16)
    column, head = row_iota(LANES, D), lane_iota(LANES, D) >> 6
    for r in range(KR):
        s.EK[r] = jnp.where(column == head * KR + r, 1.0, 0.0).astype(bf16)
        s.EK[KR + r] = jnp.where(column == y.heads * KR + head * VR + r, 1.0, 0.0).astype(bf16)
    place = (w * T + row_iota(T)).astype(f32)
    lane = lane_iota(T)
    angle = place * jnp.exp((lane % (DH // 2)).astype(f32) * (-math.log(10000.0) / (DH // 2)))
    s.ROPE[0] = jnp.cos(angle)
    s.ROPE[1] = jnp.where(lane % DH < DH // 2, -jnp.sin(angle), jnp.sin(angle))

    def own_row(values):
        mine = row_iota(N, values.shape[1]) == n
        return jnp.sum(jnp.where(mine, values.astype(f32), 0.0), axis=0, keepdims=True)

    own_docs = own_row(docs[:, pl.ds(pl.multiple_of(w * T, T), T)])
    own_docs = jnp.transpose(jnp.broadcast_to(own_docs, (T, T)))
    s.DOC[...] = own_docs

    def mask_block(block):
        first = block * KB
        key_docs = own_row(docs[:, pl.ds(pl.multiple_of(first, KB), KB)])
        allowed = (lane_iota(T, KB) + first <= row_iota(T, KB) + w * T) & (
            key_docs == s.DOC[:, :1]
        )
        s.BIAS[...] = jnp.where(allowed, 0.0, masked_score)

    mask_block(0)

    g_wq.forward_all()
    g_pt.start()
    g_pt.start_y(0)
    g_dt[0].start()
    for step in range(A):
        g_wq.landed(step)
        f_wq.start(step)
    for step in range(A):
        f_wq.forward(step)
    for step in range(A):
        f_wq.landed(step)

    gains = s.WQ[0, :, LANES:].astype(f32).T
    s.GAIN[0:1, :] = gains[y.og : y.og + 1]
    s.GAIN[1:2, :] = gains[y.og + 1 : y.og + 2]

    def rotated(tile, back=False):
        turned = swap_quarters(tile) * s.ROPE[1]
        return tile * s.ROPE[0] - turned if back else tile * s.ROPE[0] + turned

    own_rows = pl.ds(pl.multiple_of(n * T, T), T)
    x_own = tok[own_rows, :].astype(f32)
    r1_own = row_scale(x_own)
    normed_own = (x_own * r1_own * s.GAIN[0:1, :]).astype(bf16)
    factors = [dot_nn(normed_own, s.WQ[p]) for p in range(N)]
    first_tiles = [part[:, :LANES] for part in factors]
    second_tiles = [part[:, LANES:] for part in factors]

    def collect(start, width):
        pieces = []
        for p in range(N):
            pieces += [(second_tiles[p], start, p * width, width)]
        return place_lanes(pieces)

    kv_own = pl.ds(pl.multiple_of(w * T, T), T)
    s.KVF[kv_own, 0:128] = rotated(collect(y.oK, y.SK)).astype(bf16)
    s.KVF[kv_own, 128:256] = collect(y.oV, y.SK).astype(bf16)
    s.KVF[kv_own, 256:384] = place_lanes(
        [(second_tiles[p], y.ok, p * y.HK, y.HK) for p in range(N)]
        + [(second_tiles[p], y.ov, (N + p) * y.HK, y.HK) for p in range(N)]
    ).astype(bf16)
    g_kv.start()
    g_kv.start_y(0)

    query_heads = collect(y.oq, y.HQ)
    heads_high = query_heads.astype(bf16)
    s.QH[:, :LANES] = heads_high
    s.QH[:, LANES:] = (query_heads - heads_high.astype(f32)).astype(bf16)
    queries = jnp.zeros((T, D), f32)
    for r in range(QR):
        pieces = canonical_pieces(first_tiles, y.SQ, r * DH, DH, 0, 0)
        pieces += canonical_pieces(first_tiles, y.SQ, r * DH, DH, 0, DH)
        turned = rotated(place_lanes(pieces))
        s.QROT[r] = turned
        queries = queries + dot_nn(s.QH[...], s.EQ[r]) * jnp.concatenate([turned] * pairs, axis=1)
    for i in range(pairs):
        tile = (queries[:, i * LANES : (i + 1) * LANES] * (1.0 / QR)).astype(bf16)
        s.QP[i] = tile * jnp.asarray(DH**-0.5, bf16)

    def norm_rows(block, _):
        at = pl.ds(pl.multiple_of(block * T, T), T)
        values = tok[at, :].astype(f32)
        s.NORM[at, :] = (values * row_scale(values) * s.GAIN[0:1, :]).astype(bf16)
        return 0

    lax.fori_loop(0, N, norm_rows, 0)

    g_kv.forward_all()
    bulk = g_dt[1:] + g_gu
    g_pt.forward_all()
    for g in bulk:
        g.start()
    g_dt[0].start_y(0)
    g_dt[0].forward_all()
    for g in bulk:
        g.start_y(0)
    g_kv.landed_all()

    def expand_block(block):
        chunk_rows = 256

        def expand(chunk, _):
            at = pl.ds(pl.multiple_of(block * KB + chunk * chunk_rows, chunk_rows), chunk_rows)
            to = pl.ds(pl.multiple_of(chunk * chunk_rows, chunk_rows), chunk_rows)
            heads = s.KVF[at, 256:384]
            for ref, lanes, e in ((s.KP, 0, 0), (s.VP, 128, KR)):
                one, two = both_halves(s.KVF[at, lanes : lanes + 128].astype(f32))
                left = dot_nn(heads, s.EK[e])
                right = dot_nn(heads, s.EK[e + 1])
                for i in range(pairs):
                    cut = slice(i * LANES, (i + 1) * LANES)
                    ref[i, to, :] = ((left[:, cut] * one + right[:, cut] * two) * 0.5).astype(bf16)
            return 0

        lax.fori_loop(0, KB // chunk_rows, expand, 0)

    def pair_bias():
        bias = s.BIAS[...]
        return jnp.concatenate([bias, bias], axis=0)

    def forward_pair(i):
        scores = dot_nt(stack_pair(s.QP[i]), s.KP[i]) + pair_bias()
        top = jnp.max(scores, axis=1, keepdims=True)
        if y.NB > 1:
            old_top = s.LSE[i][:, :1]
            top = jnp.maximum(top, old_top)
        weights = jnp.exp(scores - top)
        total = jnp.sum(weights, axis=1, keepdims=True)
        rows_out = dot_nn(weights.astype(bf16), s.VP[i])
        if y.NB > 1:
            factor = jnp.exp(old_top - top)
            total = total + s.RUN[i][:, :1] * factor
            s.LSE[i] = jnp.broadcast_to(top, (2 * T, LANES))
            s.RUN[i] = jnp.broadcast_to(total, (2 * T, LANES))
            keep = stack_pair(s.ATT[i]) * factor
            s.ATT[i] = unstack_pair(rows_out + keep)
        return top, total, rows_out

    def store_mixture(i, attended, top, total):
        s.ATT[i] = attended
        s.LSE[i] = jnp.broadcast_to(top + jnp.log(total), (2 * T, LANES))
        s.MIX[own_rows, pl.ds(pl.multiple_of(i * LANES, LANES), LANES)] = attended.astype(bf16)

    if y.NB == 1:
        expand_block(0)

        def forward_step(i, _):
            top, total, rows_out = forward_pair(i)
            store_mixture(i, unstack_pair(rows_out / total), top, total)
            return 0

        per = pairs // h_mix.chunks
        for chunk in range(h_mix.chunks):
            lax.fori_loop(chunk * per, (chunk + 1) * per, forward_step, 0)
            h_mix.start(chunk)
    else:
        s.LSE[...] = jnp.full(s.LSE.shape, masked_score, f32)
        s.RUN[...] = jnp.zeros(s.RUN.shape, f32)
        s.ATT[...] = jnp.zeros(s.ATT.shape, f32)

        def forward_block(block, _):
            mask_block(block)
            expand_block(block)

            def step(i, _):
                forward_pair(i)
                return 0

            lax.fori_loop(0, pairs, step, 0)
            return 0

        lax.fori_loop(0, y.NB, forward_block, 0)

        def finish_step(i, _):
            total = s.RUN[i][:, :1]
            store_mixture(i, unstack_pair(stack_pair(s.ATT[i]) / total), s.LSE[i][:, :1], total)
            return 0

        lax.fori_loop(0, pairs, finish_step, 0)
        for chunk in range(h_mix.chunks):
            h_mix.start(chunk)

    for step in range(A):
        g_pt.landed(step)
        f_pt.start(step)
    h_mix.finish()
    for step in range(A):
        f_pt.forward(step)
    for g in bulk:
        g.forward_all()
    for step in range(A):
        f_pt.landed(step)

    def middle_rows(block, _):
        at = pl.ds(pl.multiple_of(block * 2 * T, 2 * T), 2 * T)
        values = tok[at, :].astype(f32)
        for p in range(N):
            values = values + dot_nt(s.MIX[at, p * 256 : (p + 1) * 256], s.PT[p])
        scale = row_scale(values)
        s.MID[at, :] = values
        s.R2[at, :] = jnp.broadcast_to(scale, (2 * T, LANES))
        s.NM[at, :] = (values * scale * s.GAIN[1:2, :]).astype(bf16)
        return 0

    lax.fori_loop(0, 2, middle_rows, 0)
    for g in g_dt + g_gu:
        g.landed_all()

    tail_low = lane_iota(2 * T) < DH

    def dense_rows(far):
        block = (1 - xo) if far else xo
        at = pl.ds(pl.multiple_of(block * 2 * T, 2 * T), 2 * T)
        both = dot_nn(s.NM[at, :], s.GU[...])
        back = dot_nn(cot[at, :], s.DT[...])
        tail = both[:, 2 * FM :]
        up_tail = pltpu.roll(tail, DH, 1)

        def gates(gate, up, pushed):
            chance = 1.0 / (1.0 + jnp.exp(-gate))
            silu = gate * chance
            return (
                silu * up,
                pushed * up * chance * (1.0 + gate * (1.0 - chance)),
                pushed * silu,
            )

        hidden, gate_gradient, up_gradient = gates(both[:, :FM], both[:, FM : 2 * FM], back[:, :FM])
        s.HID[at, :FM] = hidden.astype(bf16)
        s.GG[at, :FM] = gate_gradient.astype(bf16)
        s.GG[at, FM : 2 * FM] = up_gradient.astype(bf16)
        hidden, gate_gradient, up_gradient = gates(tail, up_tail, back[:, FM:])
        s.HID[at, FM:] = jnp.where(tail_low, hidden, 0.0).astype(bf16)
        s.GG[at, 2 * FM :] = jnp.where(
            tail_low, gate_gradient, pltpu.roll(up_gradient, DH, 1)
        ).astype(bf16)
        s.MB[at, :] = dot_nt(s.GG[at, :], s.GU[...]).astype(bf16)

    dense_rows(True)
    n_mb.start(True)
    dense_rows(False)
    n_mb.start(False)
    n_mb.pass_on()

    def grad_blocks(target, left, right, exchange):
        per = A // 4
        for j in range(4):
            block = (zi // per + 1 + j) % 4
            lanes = pl.ds(pl.multiple_of(block * 256, 256), 256)
            value = dot_tn(left[:, lanes], right[...]).astype(bf16)
            target[pl.ds(pl.multiple_of(block * 256, 256), 256), :] = value
            for q in range(per):
                exchange.start(block * per + q)

    for g in g_gu:
        g.sent()
    grad_blocks(s.GU, s.NM, s.GG, w_gu)

    mid_back = n_mb.result()
    mid_own = s.MID[own_rows, :]
    r2_own = s.R2[own_rows, :][:, :1]
    scaled = mid_back * s.GAIN[1:2, :]
    s.GS[1:2, :] = jnp.sum(mid_back * mid_own * r2_own, axis=0, keepdims=True)
    middle_gradient = (
        cot[own_rows, :].astype(f32)
        + r2_own * scaled
        - mid_own * (r2_own * r2_own * r2_own) * jnp.mean(scaled * mid_own, axis=-1, keepdims=True)
    )
    s.MG[...] = middle_gradient
    branch = middle_gradient.astype(bf16)
    s.BG[own_rows, :] = branch
    h_bg.start(0)
    for p in range(N):
        part = dot_nn(branch, s.PT[p]).astype(bf16)
        s.DO[2 * p] = part[:, :LANES]
        s.DO[2 * p + 1] = part[:, LANES:]

    def backward_block(block):
        s.DKS[...] = jnp.zeros(s.DKS.shape, f32)
        s.DHD[...] = jnp.zeros(s.DHD.shape, f32)

        def step(i, _):
            query, pushed = s.QP[i], s.DO[i]
            query2, pushed2 = stack_pair(query), stack_pair(pushed)
            product = pushed.astype(f32) * s.ATT[i]
            delta = jnp.sum(stack_pair(product), axis=1, keepdims=True)
            scores = dot_nt(query2, s.KP[i]) + pair_bias()
            chance = jnp.exp(scores - s.LSE[i][:, :1])
            gradient = (chance * (dot_nt(pushed2, s.VP[i]) - delta)).astype(bf16)
            s.QB[i] = s.QB[i] + unstack_pair(dot_nn(gradient, s.KP[i])) * DH**-0.5
            key_back = dot_tn(gradient, query2)
            value_back = dot_tn(chance.astype(bf16), pushed2)
            at = pl.ds(pl.multiple_of(block * KB, KB), KB)
            lanes = pl.ds(pl.multiple_of(i * LANES, LANES), LANES)
            heads = s.KVF[at, 256:384]
            found = s.DHD[...]
            for back, first, e in ((key_back, 0, 0), (value_back, 128, KR)):
                one, two = both_halves(s.KVF[at, first : first + 128].astype(f32))
                spread = jnp.concatenate([s.EK[e, :, lanes], s.EK[e + 1, :, lanes]], axis=1)
                joined = jnp.concatenate([back * one, back * two], axis=1).astype(bf16)
                found = found + dot_nt(joined, spread)
                wide = dot_nn(heads, spread)
                s.DKS[e] = s.DKS[e] + wide[:, :LANES] * back
                s.DKS[e + 1] = s.DKS[e + 1] + wide[:, LANES:] * back
            s.DHD[...] = found
            return 0

        lax.fori_loop(0, pairs, step, 0)
        at = pl.ds(pl.multiple_of(block * KB, KB), KB)
        low = lane_iota(KB) < DH
        for e in (0, KR):
            both = jnp.where(low, fold_halves(s.DKS[e]), fold_halves(s.DKS[e + 1])) * 0.5
            s.KVF[at, e * DH : e * DH + 128] = both.astype(bf16)
        s.KVF[at, 256:384] = (s.DHD[...] * 0.5).astype(bf16)

    s.QB[...] = jnp.zeros(s.QB.shape, f32)
    g_kv.sent()
    if y.NB == 1:
        backward_block(0)
    else:

        def backward_step(block, _):
            mask_block(block)
            expand_block(block)
            backward_block(block)
            return 0

        lax.fori_loop(0, y.NB, backward_step, 0)
    w_kv.start_all()
    grad_blocks(s.PDT, cot, s.HID, w_dt)

    query_back = jnp.concatenate([s.QB[i] for i in range(pairs)], axis=1)
    heads_back = jnp.zeros((T, LANES), f32)
    shared_back = []
    for r in range(QR):
        turned = s.QROT[r]
        product = (query_back * jnp.concatenate([turned] * pairs, axis=1)).astype(bf16)
        heads_back = heads_back + dot_nt(product, s.EQ[r, :LANES, :])
        product = dot_nn(s.QH[...], s.EQ[r]) * query_back
        total = product[:, :LANES]
        for i in range(1, pairs):
            total = total + product[:, i * LANES : (i + 1) * LANES]
        shared_back.append(fold_halves(total))
    low = lane_iota(T) < DH
    shared_tiles = [
        rotated(jnp.where(low, shared_back[2 * t], shared_back[2 * t + 1]), back=True) * (1.0 / QR)
        for t in range(QR // 2)
    ]
    heads_back = heads_back * (1.0 / QR)

    for far in (True, False):
        block = (1 - xo) if far else xo
        at = pl.ds(pl.multiple_of(block * 2 * T, 2 * T), 2 * T)
        s.OP[at, :] = dot_nt(s.HID[at, :], s.DT[...]).astype(bf16)
        n_op.start(far)
    n_op.pass_on()

    for step in list(range(1, A)) + [0]:
        w_kv.pass_on(step)
    w_kv.finish()

    key_shared = rotated(s.DKVO[:, 0:128], back=True)
    value_shared = s.DKVO[:, 128:256]
    head_tile = s.DKVO[:, 256:384]
    for p in range(N):
        s.QGS[p, :, :LANES] = place_lanes(
            canonical_pieces(shared_tiles, LANES, p * y.SQ, y.SQ, 0, 0)
        ).astype(bf16)
        s.QGS[p, :, LANES:] = place_lanes(
            [
                (key_shared, p * y.SK, y.oK, y.SK),
                (value_shared, p * y.SK, y.oV, y.SK),
                (heads_back, p * y.HQ, y.oq, y.HQ),
                (head_tile, p * y.HK, y.ok, y.HK),
                (head_tile, (N + p) * y.HK, y.ov, y.HK),
            ]
        ).astype(bf16)
    for k, peer in enumerate(narrow_peers):
        send(s.QGS.at[peer[1]], s.QGR.at[n], k_a2a + k, peer)
    s.QGR[n] = s.QGS[n]

    first_back = jnp.zeros((T, D), f32)
    for p in range(N):
        first_back = first_back + dot_nt(s.QGS[p], s.WQ[p])
    x_own = tok[own_rows, :].astype(f32)
    r1_own = row_scale(x_own)
    s.GS[0:1, :] = jnp.sum(first_back * x_own * r1_own, axis=0, keepdims=True)
    for k, peer in enumerate(narrow_peers):
        send(s.GS, s.GR.at[k], k_gain + k, peer)
    scaled = first_back * s.GAIN[0:1, :]
    tokens_gradient = (
        s.MG[...]
        + r1_own * scaled
        - x_own * (r1_own * r1_own * r1_own) * jnp.mean(scaled * x_own, axis=-1, keepdims=True)
    )
    o_tok[own_rows, :] = tokens_gradient.astype(bf16)
    for chunk in range(h_tg.chunks):
        h_tg.start(chunk)

    o_out[own_rows, :] = (s.MID[own_rows, :] + n_op.result()).astype(bf16)
    h_og.start(0)

    h_bg.finish()
    grad_blocks(s.PPT, s.BG, s.MIX.at[:, pl.ds(pl.multiple_of(n * 256, 256), 256)], w_pt)

    for k, peer in enumerate(narrow_peers):
        arrive(s.QGR.at[peer[1]], k_a2a + k)
    for k in range(3):
        arrive(s.GR.at[k], k_gain + k)
    gain_rows = s.GS[...]
    for k in range(3):
        gain_rows = gain_rows + s.GR[k]
    lane_row = row_iota(LANES, D)
    spread = jnp.where(
        lane_row == y.og,
        gain_rows[0:1],
        jnp.where(lane_row == y.og + 1, gain_rows[1:2], 0.0),
    )
    gain_columns = spread.T
    per = A // 4
    for j in range(4):
        block = (zi // per + 1 + j) % 4
        lanes = pl.ds(pl.multiple_of(block * 256, 256), 256)
        value = jnp.zeros((256, 256), f32)
        for p in range(N):
            value = value + dot_tn(s.NORM[p * T : (p + 1) * T, lanes], s.QGR[p])
        s.PQ[pl.ds(pl.multiple_of(block * 256, 256), 256), :] = value.astype(bf16)
    s.PQ[:, LANES:] = (s.PQ[:, LANES:].astype(f32) + gain_columns).astype(bf16)
    w_q.start_all()

    for exchange in (w_gu, w_dt, w_pt, w_q):
        for step in list(range(1, A)) + [0]:
            exchange.pass_on(step)

    h_tg.finish()
    h_og.finish()
    for exchange in (w_gu, w_dt, w_pt, w_q):
        exchange.finish()
    for g in [g_wq, g_pt] + g_dt:
        g.sent()
    for copy in pending:
        copy.wait_send()


def solution(mesh):
    W, N = mesh.shape["wide"], mesh.shape["narrow"]

    def on_device(
        tokens,
        documents,
        prenorm,
        qheads,
        qshared,
        kheads,
        kshared,
        vheads,
        vshared,
        project,
        midnorm,
        gating,
        upward,
        downward,
        cotangent,
    ):
        R, T, D = tokens.shape
        L = documents.shape[1]
        RW, F = gating.shape
        y = make_layout(W, N, T, D, F, L, N * kheads.shape[1] // KR)
        assert R == N
        FM = y.FM
        zeros = lambda count: jnp.zeros((RW, count), bf16)
        wq = jnp.concatenate(
            [
                qshared,
                zeros(LANES - y.SQ),
                kshared,
                vshared,
                qheads,
                kheads,
                vheads,
                prenorm[:, None],
                midnorm[:, None],
                zeros(LANES - y.og - 2),
            ],
            axis=1,
        )
        gu = jnp.concatenate([gating[:, :FM], upward[:, :FM], gating[:, FM:], upward[:, FM:]], axis=1)
        dt = jnp.pad(downward.T, ((0, 0), (0, y.FP - F)))
        pt = project.T
        scratch = scratch_list(y)
        copies = 256 + 48 * y.A
        vmem = pl.BlockSpec(memory_space=pltpu.VMEM)

        def kernel(*refs):
            block_kernel(y, tuple(scratch), *refs)

        shape = jax.ShapeDtypeStruct
        out, tok, gu_back, dt_back, pt_back, q_back = pl.pallas_call(
            kernel,
            out_shape=(
                shape((y.M, D), bf16),
                shape((y.M, D), bf16),
                shape((RW, 2 * FM + LANES), f32),
                shape((RW, y.FP), f32),
                shape((RW, 256), f32),
                shape((RW, 256), f32),
            ),
            in_specs=[vmem] * 7,
            out_specs=[vmem] * 6,
            scratch_shapes=[*scratch.values()] + [pltpu.SemaphoreType.DMA((copies,))] * 2,
            compiler_params=pltpu.CompilerParams(
                collective_id=0, has_side_effects=True, vmem_limit_bytes=63 * 2**20
            ),
            name="block",
        )(
            tokens.reshape(y.M, D),
            documents,
            wq,
            gu,
            dt,
            pt,
            cotangent.reshape(y.M, D),
        )
        second = lambda first, count: q_back[:, LANES + first : LANES + first + count]
        half = F - FM
        return (
            out.reshape(R, T, D),
            tok.astype(f32).reshape(R, T, D),
            second(y.og, 1).reshape(RW),
            second(y.oq, y.HQ),
            q_back[:, : y.SQ],
            second(y.ok, y.HK),
            second(y.oK, y.SK),
            second(y.ov, y.HK),
            second(y.oV, y.SK),
            pt_back.T,
            second(y.og + 1, 1).reshape(RW),
            jnp.concatenate([gu_back[:, :FM], gu_back[:, 2 * FM : 2 * FM + half]], axis=1),
            jnp.concatenate([gu_back[:, FM : 2 * FM], gu_back[:, 2 * FM + half :]], axis=1),
            dt_back[:, :F].T,
        )

    split = P("wide", "narrow")
    flipped = P("narrow", "wide")
    whole = P(None, "wide", None)
    gain = P("wide")
    return jax.shard_map(
        on_device,
        mesh=mesh,
        in_specs=(
            whole,
            P(),
            gain,
            split,
            split,
            split,
            split,
            split,
            split,
            flipped,
            gain,
            split,
            split,
            flipped,
            whole,
        ),
        out_specs=(
            whole,
            whole,
            gain,
            split,
            split,
            split,
            split,
            split,
            split,
            flipped,
            gain,
            split,
            split,
            flipped,
        ),
        check_vma=False,
    )
```

```python
import math
from types import SimpleNamespace

import jax
import jax.numpy as jnp
from jax import lax
from jax.experimental import pallas as pl
from jax.experimental.pallas import tpu as pltpu
from jax.sharding import PartitionSpec as P

DH = 64
QR = 6
KR = 2
VR = 2
LANES = 128

epsilon = 1e-06
masked_score = -1e30
MESH = pl.DeviceIdType.MESH
f32 = jnp.float32
bf16 = jnp.bfloat16


def dot_nn(a, b):
    return lax.dot_general(a, b, (((1,), (0,)), ((), ())), preferred_element_type=f32)


def dot_nt(a, b):
    return lax.dot_general(a, b, (((1,), (1,)), ((), ())), preferred_element_type=f32)


def dot_tn(a, b):
    return lax.dot_general(a, b, (((0,), (0,)), ((), ())), preferred_element_type=f32)


def lane_iota(rows, cols=LANES):
    return lax.broadcasted_iota(jnp.int32, (rows, cols), 1)


def row_iota(rows, cols=LANES):
    return lax.broadcasted_iota(jnp.int32, (rows, cols), 0)


def place_lanes(pieces):
    rows = pieces[0][0].shape[0]
    lane = lane_iota(rows)
    result = jnp.zeros((rows, LANES), f32)
    for tile, start, to, count in pieces:
        shift = (to - start) % LANES
        moved = pltpu.roll(tile, shift, 1) if shift else tile
        result = jnp.where((lane >= to) & (lane < to + count), moved, result)
    return result


def canonical_pieces(tiles, width, first, count, start, to):
    pieces = []
    while count:
        part, inside = divmod(first, width)
        take = min(count, width - inside)
        pieces.append((tiles[part], start + inside, to, take))
        first, to, count = first + take, to + take, count - take
    return pieces


def both_halves(tile):
    low = lane_iota(tile.shape[0]) < DH
    turned = pltpu.roll(tile, DH, 1)
    return jnp.where(low, tile, turned), jnp.where(low, turned, tile)


def swap_quarters(tile):
    low = lane_iota(tile.shape[0]) % DH < DH // 2
    return jnp.where(low, pltpu.roll(tile, LANES - DH // 2, 1), pltpu.roll(tile, DH // 2, 1))


def stack_pair(tile):
    low = lane_iota(tile.shape[0]) < DH
    zero = jnp.zeros_like(tile)
    return jnp.concatenate([jnp.where(low, tile, zero), jnp.where(low, zero, tile)], axis=0)


def unstack_pair(rows):
    half = rows.shape[0] // 2
    low = lane_iota(half) < DH
    return jnp.where(low, rows[:half], rows[half:])


def fold_halves(tile):
    return tile + pltpu.roll(tile, DH, 1)


def row_scale(values):
    return lax.rsqrt(jnp.mean(values * values, axis=-1, keepdims=True) + epsilon)


def make_layout(W, N, T, D, F, L, heads):
    lay = SimpleNamespace()
    lay.W, lay.N, lay.T, lay.D, lay.F, lay.L, lay.heads = W, N, T, D, F, L, heads
    lay.A = W // 2
    lay.RW = D // W
    lay.M = N * T
    lay.FM = F // LANES * LANES
    lay.FP = lay.FM + LANES
    lay.pairs = heads // 2
    lay.KB = L if L <= 1024 else 512
    lay.NB = L // lay.KB
    lay.SQ = QR * DH // N
    lay.SK = KR * DH // N
    lay.HQ = heads * QR // N
    lay.HK = heads * KR // N
    lay.oK, lay.oV = 0, lay.SK
    lay.oq = 2 * lay.SK
    lay.ok = lay.oq + lay.HQ
    lay.ov = lay.ok + lay.HK
    lay.og = lay.ov + lay.HK
    assert N == 4 and W % 8 == 0 and T == LANES and D == heads * DH == 1024
    assert F % LANES == DH and lay.SQ <= LANES and lay.og + 2 <= LANES
    return lay


def scratch_list(y):
    W, N, T, D, L, A, RW, M = y.W, y.N, y.T, y.D, y.L, y.A, y.RW, y.M
    vm = lambda *shape, kind=bf16: pltpu.VMEM(shape, kind)
    GUc = 2 * y.FM + LANES
    return dict(
        WQ=vm(N, D, 256),
        PT=vm(N, D, 256),
        GU=vm(D, GUc),
        DT=vm(D, y.FP),
        KVF=vm(L, 384),
        KP=vm(y.pairs, y.KB, LANES),
        VP=vm(y.pairs, y.KB, LANES),
        EQ=vm(QR, LANES, D),
        EK=vm(4, LANES, D),
        BIAS=vm(T, y.KB, kind=f32),
        DOC=vm(T, LANES, kind=f32),
        ROPE=vm(2, T, LANES, kind=f32),
        GAIN=vm(8, D, kind=f32),
        QROT=vm(QR, T, LANES, kind=f32),
        QH=vm(T, 256),
        QP=vm(y.pairs, T, LANES),
        ATT=vm(y.pairs, T, LANES, kind=f32),
        LSE=vm(y.pairs, 2 * T, LANES, kind=f32),
        RUN=vm(y.pairs if y.NB > 1 else 1, 2 * T, LANES, kind=f32),
        MIX=vm(M, D),
        NORM=vm(M, D),
        MID=vm(M, D, kind=f32),
        NM=vm(M, D),
        R2=vm(M, LANES, kind=f32),
        HID=vm(M, y.FP),
        GG=vm(M, GUc),
        MB=vm(M, D),
        MBC=vm(2, T, D),
        MBX=vm(T, D),
        MBS=vm(T, D),
        OP=vm(M, D),
        OPC=vm(2, T, D),
        OPX=vm(T, D),
        OPS=vm(T, D),
        BG=vm(M, D),
        MG=vm(T, D, kind=f32),
        DO=vm(y.pairs, T, LANES),
        QB=vm(y.pairs, T, LANES, kind=f32),
        DKS=vm(4, y.KB, LANES, kind=f32),
        DHD=vm(y.KB, LANES, kind=f32),
        DKVY=vm(A * T, 384),
        DKVR=vm((A + 1) * T, 384),
        DKVO=vm(T, 384, kind=f32),
        QGS=vm(N, T, 256),
        QGR=vm(N, T, 256),
        OUT=vm(M, D),
        TOK=vm(M, D),
        TGU=vm(RW, GUc, kind=f32),
        TDT=vm(RW, y.FP, kind=f32),
        TPT=vm(RW, 256, kind=f32),
        TQ=vm(RW, 256, kind=f32),
        GS=vm(8, D, kind=f32),
        GR=vm(3, 8, D, kind=f32),
        YGU=vm(A * RW, GUc),
        RGU=vm((A + 1) * RW, 1024),
        RZF=vm((A + 1) * 2 * RW, GUc - 1024),
        PDT=vm(D, y.FP),
        YDT=vm(A * RW, y.FP),
        RDT=vm((A + 1) * RW, y.FP),
        PPT=vm(D, 256),
        YPT=vm(A * RW, 256),
        RPT=vm((A + 1) * RW, 256),
        PQ=vm(D, 256),
        YQ=vm(A * RW, 256),
        RQ=vm((A + 1) * RW, 256),
    )


def block_kernel(y, names, *refs):
    tok, docs, prenorm, qheads, qshared, kheads, kshared, vheads, vshared = refs[:9]
    project, midnorm, gating, upward, downward, cot = refs[9:15]
    r_out, r_tok, r_gu, r_dt, r_pt, r_q = refs[15:21]
    s = SimpleNamespace(**dict(zip(names, refs[21:])))
    ssem, rsem, wsem = refs[21 + len(names) :]
    o_out, o_tok, o_gu, o_dt, o_pt, o_q = s.OUT, s.TOK, s.TGU, s.TDT, s.TPT, s.TQ
    written = []

    def write(src, dst):
        copy = pltpu.make_async_copy(src, dst, wsem.at[len(written)])
        copy.start()
        written.append(copy)

    W, N, T, D, F, L, A, RW, M = y.W, y.N, y.T, y.D, y.F, y.L, y.A, y.RW, y.M
    FM, FP, KB, pairs = y.FM, y.FP, y.KB, y.pairs
    w = lax.axis_index("wide")
    n = lax.axis_index("narrow")
    zi, yi = w // 2, w % 2
    xo, co = n // 2, n % 2
    y_peer = (zi * 2 + 1 - yi, n)
    c_peer = (w, xo * 2 + 1 - co)
    x_peer = (w, (1 - xo) * 2 + co)
    d_peer = (w, (1 - xo) * 2 + 1 - co)
    narrow_peers = (c_peer, x_peer, d_peer)
    taken = [0, rsem.shape[0]]

    def take(count=1):
        taken[0] += count
        return taken[0] - count

    def take_send(count):
        taken[1] += count
        return taken[1] - count

    def remote(src, dst, k, peer, send_k=None):
        return pltpu.make_async_remote_copy(
            src_ref=src,
            dst_ref=dst,
            send_sem=ssem.at[k if send_k is None else send_k],
            recv_sem=rsem.at[k],
            device_id=peer,
            device_id_type=MESH,
        )

    pending = []

    def send(src, dst, k, peer, started=pending):
        copy = remote(src, dst, k, peer)
        copy.start()
        started.append(copy)

    def arrive(dst, k):
        remote(dst, dst, k, y_peer).wait_recv()

    def rows(ref, first, count, lanes=None):
        at = pl.ds(pl.multiple_of(first, 16), count)
        return ref.at[at] if lanes is None else ref.at[at, pl.ds(*lanes)]

    def each_at(distance, act):
        if distance == 0:
            act(zi, None)
            return
        pl.when(zi >= distance)(lambda: act(zi - distance, True))
        pl.when(zi + distance < A)(lambda: act(zi + distance, False))

    right_peer = ((zi + 1) * 2 + yi, n)
    left_peer = ((zi - 1) * 2 + yi, n)

    barrier = pltpu.get_barrier_semaphore()
    for peer in (y_peer, *narrow_peers):
        pl.semaphore_signal(barrier, inc=1, device_id=peer, device_id_type=MESH)

    @pl.when(zi > 0)
    def _():
        pl.semaphore_signal(barrier, inc=1, device_id=left_peer, device_id_type=MESH)

    @pl.when(zi < A - 1)
    def _():
        pl.semaphore_signal(barrier, inc=1, device_id=right_peer, device_id_type=MESH)

    pl.semaphore_wait(barrier, jnp.where((zi > 0) & (zi < A - 1), 6, 5))

    class Gather:
        def __init__(self, ref, count, lanes=None, y_first=False):
            self.ref, self.count, self.lanes, self.y_first = ref, count, lanes, y_first
            self.kz, self.ky, self.kl = take(A), take(A), take_send(A)
            self.next = 1

        def part(self, wide):
            return rows(self.ref, wide * self.count, self.count, self.lanes)

        def block(self, z):
            if self.y_first:
                return rows(self.ref, z * 2 * self.count, 2 * self.count, self.lanes)
            return self.part(z * 2 + yi)

        def along(self, z, to_right):
            block = self.block(z)
            if to_right:
                return remote(block, block, self.kz + z, right_peer)
            return remote(block, block, self.kz + z, left_peer, self.kl + z)

        def across(self, z):
            part = self.part(z * 2 + yi)
            return remote(part, part, self.ky + z, y_peer)

        def landed(self, z):
            arrive(self.part(z * 2 + 1 - yi), self.ky + z)

        def launch_y(self):
            self.across(zi).start()

        def launch(self):
            if self.y_first:
                self.landed(zi)
            pl.when(zi < A - 1)(lambda: self.along(zi, True).start())
            pl.when(zi > 0)(lambda: self.along(zi, False).start())

        def hop(self, distance):
            def act(z, to_right):
                arrive(self.block(z), self.kz + z)
                more = zi < A - 1 if to_right else zi > 0
                pl.when(more)(lambda: self.along(z, to_right).start())
                if not self.y_first:
                    self.across(z).start()

            each_at(distance, act)

        def pump(self, count=A):
            for _ in range(min(count, A - self.next)):
                self.hop(self.next)
                self.next += 1

        def landed_all(self):
            if not self.y_first:
                for z in range(A):
                    self.landed(z)

        def sent(self):
            self.across(zi).wait_send()
            pl.when(zi < A - 1)(lambda: self.along(zi, True).wait_send())
            pl.when(zi > 0)(lambda: self.along(zi, False).wait_send())
            for distance in range(1, A):

                def act(z, to_right):
                    more = zi < A - 1 if to_right else zi > 0
                    pl.when(more)(lambda: self.along(z, to_right).wait_send())
                    if not self.y_first:
                        self.across(z).wait_send()

                each_at(distance, act)

    class Spread:
        def __init__(self, gather, ref):
            self.gather, self.ref = gather, ref
            self.next = self.passed = 0
            self.kx, self.kc, self.kd = take(A), take(A), take(A)

        def part(self, owner, z):
            return rows(self.ref.at[owner], z * 2 * RW, 2 * RW)

        def copies(self, z):
            part = self.part(n, z)
            return remote(part, part, self.kx + z, x_peer), remote(part, part, self.kc + z, c_peer)

        def onward(self, z):
            part = self.part(x_peer[1], z)
            return remote(part, part, self.kd + z, c_peer)

        def start(self, distance):
            def act(z, _):
                self.gather.landed(z)
                for copy in self.copies(z):
                    copy.start()

            each_at(distance, act)

        def pump(self, count=A):
            for _ in range(min(count, A - self.next)):
                self.start(self.next)
                self.next += 1

        def pump_forward(self, count=A):
            for _ in range(min(count, A - self.passed)):
                self.forward(self.passed)
                self.passed += 1

        def forward(self, distance):
            def act(z, _):
                arrive(self.part(x_peer[1], z), self.kx + z)
                self.onward(z).start()

            each_at(distance, act)

        def landed(self):
            for z in range(A):
                arrive(self.part(c_peer[1], z), self.kc + z)
                arrive(self.part(d_peer[1], z), self.kd + z)

        def sent(self):
            for z in range(A):
                for copy in self.copies(z):
                    copy.wait_send()
                self.onward(z).wait_send()

    class Share:
        def __init__(self, ref, chunks):
            self.ref, self.chunks = ref, chunks
            self.kx, self.kc, self.kd = take(chunks), take(chunks), take(chunks)
            self.width = D // chunks

        def part(self, owner, chunk):
            lanes = pl.ds(pl.multiple_of(chunk * self.width, LANES), self.width)
            return self.ref.at[pl.ds(pl.multiple_of(owner * T, T), T), lanes]

        def start(self, chunk):
            send(self.part(n, chunk), self.part(n, chunk), self.kx + chunk, x_peer)
            send(self.part(n, chunk), self.part(n, chunk), self.kc + chunk, c_peer)

        def forward(self, chunk):
            part = self.part(x_peer[1], chunk)
            arrive(part, self.kx + chunk)
            send(part, part, self.kd + chunk, c_peer)

        def landed(self, chunk):
            arrive(self.part(c_peer[1], chunk), self.kc + chunk)
            arrive(self.part(d_peer[1], chunk), self.kd + chunk)

        def forward_all(self):
            for chunk in range(self.chunks):
                self.forward(chunk)

        def landed_all(self):
            for chunk in range(self.chunks):
                self.landed(chunk)

        def finish(self):
            self.forward_all()
            self.landed_all()

    class NarrowSum:
        def __init__(self, part_ref, core_ref, x_ref, send_ref):
            self.ref, self.core, self.x, self.out = part_ref, core_ref, x_ref, send_ref
            self.kc, self.kx = take(2), take(1)

        def part(self, owner):
            return rows(self.ref, owner * T, T)

        def start(self, far):
            owner = ((1 - xo) if far else xo) * 2 + 1 - co
            send(self.part(owner), self.core.at[int(far)], self.kc + int(far), c_peer)

        def pass_on(self):
            arrive(self.core.at[1], self.kc + 1)
            total = self.part((1 - xo) * 2 + co)[...].astype(f32) + self.core[1].astype(f32)
            self.out[...] = total.astype(bf16)
            send(self.out, self.x, self.kx, x_peer)

        def result(self):
            arrive(self.core.at[0], self.kc)
            arrive(self.x, self.kx)
            return (
                self.part(n)[...].astype(f32) + self.core[0].astype(f32) + self.x[...].astype(f32)
            )

    class WideSum:
        def __init__(self, part_ref, y_ref, z_ref, out_ref, count, lanes=None, z_first=False):
            self.ref, self.y, self.z, self.total = part_ref, y_ref, z_ref, out_ref
            self.count, self.lanes, self.z_first = count, lanes, z_first
            self.size = 2 * count if z_first else count
            self.next = 0
            self.z_lanes = (0, lanes[1]) if z_first else lanes
            self.ky, self.kz, self.kl = take(1 if z_first else A), take(A + 1), take_send(A)

        def part(self, wide):
            return rows(self.ref, wide * self.count, self.count, self.lanes)

        def block(self, z):
            if self.z_first:
                return rows(self.ref, z * 2 * self.count, 2 * self.count, self.lanes)
            return self.part(z * 2 + yi)

        def got_y(self, z):
            return rows(self.y, z * self.count, self.count, self.lanes)

        def got_z(self, slot):
            return rows(self.z, slot * self.size, self.size, self.z_lanes)

        def across(self, z):
            return remote(self.part(z * 2 + 1 - yi), self.got_y(z), self.ky + z, y_peer)

        def along(self, z, to_right):
            block = self.block(z)
            if to_right:
                return remote(block, self.got_z(z), self.kz + z, right_peer)
            slot = jnp.where(z == zi - 1, A, z)
            return remote(block, self.got_z(slot), self.kz + slot, left_peer, self.kl + z)

        def start(self, z):
            if not self.z_first:
                self.across(z).start()

        def gather_y(self, z):
            block = self.block(z)[...].astype(f32)
            if self.z_first:
                return block
            arrive(self.got_y(z), self.ky + z)
            return block + self.got_y(z)[...].astype(f32)

        def stage(self, step):
            def move(z, to_right, joined):
                value = self.gather_y(z)
                if joined:
                    arrive(self.got_z(z), self.kz + z)
                    value = value + self.got_z(z)[...].astype(f32)
                self.block(z)[...] = value.astype(bf16)
                self.along(z, to_right).start()

            right, left = A - 1 - step + zi, step - (A - 1 - zi)
            to_right = (right < A) & (right > zi)
            to_left = (left >= 0) & (left < zi)
            pl.when(to_right & (zi > 0))(lambda: move(right, True, True))
            pl.when(to_left & (zi < A - 1))(lambda: move(left, False, True))
            if not self.z_first:
                pl.when(to_right & (zi == 0))(lambda: move(right, True, False))
                pl.when(to_left & (zi == A - 1))(lambda: move(left, False, False))

        def pump(self, count=A):
            for _ in range(min(count, A - 1 - self.next)):
                self.stage(self.next)
                self.next += 1

        def start_ends(self):
            @pl.when(zi == 0)
            def _():
                for z in range(A - 1, 0, -1):
                    self.along(z, True).start()

            @pl.when(zi == A - 1)
            def _():
                for z in range(A - 1):
                    self.along(z, False).start()

        def add(self, slot):
            arrive(self.got_z(slot), self.kz + slot)
            got = self.got_z(slot)[...].astype(f32)
            if not self.z_first:
                self.total[...] += got
                return
            block = self.block(zi)
            block[...] = (block[...].astype(f32) + got).astype(bf16)

        def finish(self):
            if not self.z_first:
                self.total[...] = self.gather_y(zi)
            pl.when(zi > 0)(lambda: self.add(zi))
            pl.when(zi < A - 1)(lambda: self.add(A))
            if self.z_first:
                self.last_across().start()

        def last_across(self):
            return remote(self.part(zi * 2 + 1 - yi), self.got_y(0), self.ky, y_peer)

        def finish_y(self):
            if self.z_first:
                arrive(self.got_y(0), self.ky)
                mine = self.part(zi * 2 + yi)[...].astype(f32)
                self.total[...] = mine + self.got_y(0)[...].astype(f32)

        def sent(self):
            if self.z_first:
                self.last_across().wait_send()
            for z in range(A):
                if not self.z_first:
                    self.across(z).wait_send()
                pl.when(zi < z)(lambda: self.along(z, True).wait_send())
                pl.when(zi > z)(lambda: self.along(z, False).wait_send())

    if A == 4:
        z_order = []
        for row in zip((3, 2, 1, 0), (3, 2, 0, 1), (0, 1, 3, 2), (0, 1, 2, 3)):
            z_order.append(sum(jnp.where(zi == at, z, 0) for at, z in enumerate(row)))
    else:
        z_order = range(A)

    GUc = 2 * FM + LANES
    cuts = ((0, 512), (512, 512), (1024, GUc - 1024))
    g_wq = Gather(s.WQ.at[n], RW)
    g_pt = Gather(s.PT.at[n], RW)
    g_kv = Gather(s.KVF, T)
    g_dt = Gather(s.DT, RW)
    g_gu = [Gather(s.GU, RW, lanes, y_first=i == 2) for i, lanes in enumerate(cuts)]
    f_wq, f_pt = Spread(g_wq, s.WQ), Spread(g_pt, s.PT)
    h_mix, h_bg, h_og, h_tg = Share(s.MIX, 4), Share(s.BG, 1), Share(o_out, 1), Share(o_tok, 2)
    n_mb = NarrowSum(s.MB, s.MBC, s.MBX, s.MBS)
    n_op = NarrowSum(s.OP, s.OPC, s.OPX, s.OPS)
    w_kv = WideSum(s.KVF, s.DKVY, s.DKVR, s.DKVO, T)
    w_gu = []
    for i, lanes in enumerate(cuts):
        refs_z = s.RZF if i == 2 else s.RGU
        out = o_gu.at[:, pl.ds(*lanes)]
        w_gu.append(WideSum(s.GU, s.YGU, refs_z, out, RW, lanes, z_first=i == 2))
    w_dt = WideSum(s.PDT, s.YDT, s.RDT, o_dt, RW)
    w_pt = WideSum(s.PPT, s.YPT, s.RPT, o_pt, RW)
    w_q = WideSum(s.PQ, s.YQ, s.RQ, o_q, RW)
    k_a2a, k_gain = take(3), take(3)
    assert taken[0] <= rsem.shape[0] and taken[1] <= ssem.shape[0]

    own = pl.ds(pl.multiple_of(w * RW, RW), RW)
    blank = lambda count, kind=bf16: jnp.zeros((count, RW), kind)
    shared_part = jnp.concatenate([qshared[...].astype(f32), blank(LANES - y.SQ, f32)], axis=0)
    gain_row = row_iota(8, RW)
    gain_part = jnp.where(
        gain_row == 0,
        prenorm[...].astype(f32),
        jnp.where(gain_row == 1, midnorm[...].astype(f32), 0.0),
    )
    second_part = jnp.concatenate(
        [part[...].astype(f32) for part in (kshared, vshared, qheads, kheads, vheads)]
        + [gain_part, blank(LANES - y.og - 8, f32)],
        axis=0,
    )
    s.WQ[n, own, :LANES] = shared_part.T.astype(bf16)
    s.WQ[n, own, LANES:] = second_part.T.astype(bf16)
    g_wq.launch()
    g_wq.launch_y()
    for first in range(0, 256, LANES):
        s.PT[n, own, first : first + LANES] = project[first : first + LANES, :].T
    g_pt.launch()
    for first in range(0, FM, LANES):
        s.DT[own, first : first + LANES] = downward[first : first + LANES, :].T
    s.DT[own, FM:] = jnp.concatenate([downward[FM:, :], blank(FP - F)], axis=0).T
    for first in range(0, FM, LANES):
        s.GU[own, first : first + LANES] = gating[first : first + LANES, :].T
        s.GU[own, FM + first : FM + first + LANES] = upward[first : first + LANES, :].T
    s.GU[own, 2 * FM :] = jnp.concatenate([gating[FM:, :], upward[FM:, :]], axis=0).T
    g_gu[2].launch_y()

    column, head = row_iota(LANES, D), lane_iota(LANES, D) >> 6
    for r in range(QR):
        s.EQ[r] = jnp.where(column == head * QR + r, 1.0, 0.0).astype(bf16)
    for r in range(KR):
        s.EK[r] = jnp.where(column == head * KR + r, 1.0, 0.0).astype(bf16)
        s.EK[KR + r] = jnp.where(column == y.heads * KR + head * VR + r, 1.0, 0.0).astype(bf16)
    place = (w * T + row_iota(T)).astype(f32)
    lane = lane_iota(T)
    angle = place * jnp.exp((lane % (DH // 2)).astype(f32) * (-math.log(10000.0) / (DH // 2)))
    s.ROPE[0] = jnp.cos(angle)
    s.ROPE[1] = jnp.where(lane % DH < DH // 2, -jnp.sin(angle), jnp.sin(angle))

    def own_row(values):
        mine = row_iota(N, values.shape[1]) == n
        return jnp.sum(jnp.where(mine, values.astype(f32), 0.0), axis=0, keepdims=True)

    own_docs = own_row(docs[:, pl.ds(pl.multiple_of(w * T, T), T)])
    own_docs = jnp.transpose(jnp.broadcast_to(own_docs, (T, T)))
    s.DOC[...] = own_docs

    def mask_block(block):
        first = block * KB
        key_docs = own_row(docs[:, pl.ds(pl.multiple_of(first, KB), KB)])
        allowed = (lane_iota(T, KB) + first <= row_iota(T, KB) + w * T) & (
            key_docs == s.DOC[:, :1]
        )
        s.BIAS[...] = jnp.where(allowed, 0.0, masked_score)

    mask_block(0)

    g_wq.pump(1)
    g_pt.launch_y()
    f_wq.pump(1)
    g_wq.pump(1)
    f_wq.pump(1)
    g_dt.launch()
    g_dt.launch_y()
    g_wq.pump()
    g_pt.pump(1)
    f_wq.pump(1)
    g_pt.pump(1)
    f_wq.pump()
    g_pt.pump()
    g_dt.pump(1)
    f_wq.pump_forward()
    f_wq.landed()

    gains = s.WQ[0, :, LANES:].astype(f32).T
    s.GAIN[0:1, :] = gains[y.og : y.og + 1]
    s.GAIN[1:2, :] = gains[y.og + 1 : y.og + 2]

    def rotated(tile, back=False):
        turned = swap_quarters(tile) * s.ROPE[1]
        return tile * s.ROPE[0] - turned if back else tile * s.ROPE[0] + turned

    own_rows = pl.ds(pl.multiple_of(n * T, T), T)
    x_own = tok[own_rows, :].astype(f32)
    r1_own = row_scale(x_own)
    normed_own = (x_own * r1_own * s.GAIN[0:1, :]).astype(bf16)
    factors = [dot_nn(normed_own, s.WQ[p]) for p in range(N)]
    first_tiles = [part[:, :LANES] for part in factors]
    second_tiles = [part[:, LANES:] for part in factors]

    def collect(start, width):
        pieces = []
        for p in range(N):
            pieces += [(second_tiles[p], start, p * width, width)]
        return place_lanes(pieces)

    kv_own = pl.ds(pl.multiple_of(w * T, T), T)
    s.KVF[kv_own, 0:128] = rotated(collect(y.oK, y.SK)).astype(bf16)
    s.KVF[kv_own, 128:256] = collect(y.oV, y.SK).astype(bf16)
    s.KVF[kv_own, 256:384] = place_lanes(
        [(second_tiles[p], y.ok, p * y.HK, y.HK) for p in range(N)]
        + [(second_tiles[p], y.ov, (N + p) * y.HK, y.HK) for p in range(N)]
    ).astype(bf16)
    g_kv.launch()
    g_kv.launch_y()
    g_gu[0].launch()
    g_gu[0].launch_y()

    query_heads = collect(y.oq, y.HQ)
    heads_high = query_heads.astype(bf16)
    s.QH[:, :LANES] = heads_high
    s.QH[:, LANES:] = (query_heads - heads_high.astype(f32)).astype(bf16)

    def spread_heads(r):
        return dot_nn(s.QH[:, :LANES], s.EQ[r]) + dot_nn(s.QH[:, LANES:], s.EQ[r])

    queries = jnp.zeros((T, D), f32)
    for r in range(QR):
        pieces = canonical_pieces(first_tiles, y.SQ, r * DH, DH, 0, 0)
        pieces += canonical_pieces(first_tiles, y.SQ, r * DH, DH, 0, DH)
        turned = rotated(place_lanes(pieces))
        s.QROT[r] = turned
        queries = queries + spread_heads(r) * jnp.concatenate([turned] * pairs, axis=1)
    for i in range(pairs):
        tile = (queries[:, i * LANES : (i + 1) * LANES] * (1.0 / QR)).astype(bf16)
        s.QP[i] = tile * jnp.asarray(DH**-0.5, bf16)

    def norm_rows(block, _):
        at = pl.ds(pl.multiple_of(block * T, T), T)
        values = tok[at, :].astype(f32)
        s.NORM[at, :] = (values * row_scale(values) * s.GAIN[0:1, :]).astype(bf16)
        return 0

    lax.fori_loop(0, N, norm_rows, 0)

    g_dt.pump(1)
    f_pt.pump()
    g_dt.pump()
    g_kv.pump(1)
    g_gu[1].launch()
    g_gu[1].launch_y()
    g_kv.pump(1)
    g_kv.pump()
    f_pt.pump_forward(2)
    g_gu[0].pump(1)
    g_kv.landed_all()

    def expand_block(block):
        chunk_rows = 256

        def expand(chunk, _):
            at = pl.ds(pl.multiple_of(block * KB + chunk * chunk_rows, chunk_rows), chunk_rows)
            to = pl.ds(pl.multiple_of(chunk * chunk_rows, chunk_rows), chunk_rows)
            heads = s.KVF[at, 256:384]
            for ref, lanes, e in ((s.KP, 0, 0), (s.VP, 128, KR)):
                one, two = both_halves(s.KVF[at, lanes : lanes + 128].astype(f32))
                left = dot_nn(heads, s.EK[e])
                right = dot_nn(heads, s.EK[e + 1])
                for i in range(pairs):
                    cut = slice(i * LANES, (i + 1) * LANES)
                    ref[i, to, :] = ((left[:, cut] * one + right[:, cut] * two) * 0.5).astype(bf16)
            return 0

        lax.fori_loop(0, KB // chunk_rows, expand, 0)

    def pair_bias():
        bias = s.BIAS[...]
        return jnp.concatenate([bias, bias], axis=0)

    def forward_pair(i):
        scores = dot_nt(stack_pair(s.QP[i]), s.KP[i]) + pair_bias()
        top = jnp.max(scores, axis=1, keepdims=True)
        if y.NB > 1:
            old_top = s.LSE[i][:, :1]
            top = jnp.maximum(top, old_top)
        weights = jnp.exp(scores - top)
        total = jnp.sum(weights, axis=1, keepdims=True)
        rows_out = dot_nn(weights.astype(bf16), s.VP[i])
        if y.NB > 1:
            factor = jnp.exp(old_top - top)
            total = total + s.RUN[i][:, :1] * factor
            s.LSE[i] = jnp.broadcast_to(top, (2 * T, LANES))
            s.RUN[i] = jnp.broadcast_to(total, (2 * T, LANES))
            keep = stack_pair(s.ATT[i]) * factor
            s.ATT[i] = unstack_pair(rows_out + keep)
        return top, total, rows_out

    def store_mixture(i, attended, top, total):
        s.ATT[i] = attended
        s.LSE[i] = jnp.broadcast_to(top + jnp.log(total), (2 * T, LANES))
        s.MIX[own_rows, pl.ds(pl.multiple_of(i * LANES, LANES), LANES)] = attended.astype(bf16)

    if y.NB == 1:
        expand_block(0)

        def forward_step(i, _):
            top, total, rows_out = forward_pair(i)
            store_mixture(i, unstack_pair(rows_out / total), top, total)
            return 0

        per = pairs // h_mix.chunks
        for chunk in range(h_mix.chunks):
            lax.fori_loop(chunk * per, (chunk + 1) * per, forward_step, 0)
            h_mix.start(chunk)
            if chunk == 0:
                g_gu[0].pump(1)
            elif chunk == 1:
                g_gu[0].pump()
                g_gu[2].launch()
            else:
                g_gu[1].pump(1)
    else:
        s.LSE[...] = jnp.full(s.LSE.shape, masked_score, f32)
        s.RUN[...] = jnp.zeros(s.RUN.shape, f32)
        s.ATT[...] = jnp.zeros(s.ATT.shape, f32)

        def forward_block(block, _):
            mask_block(block)
            expand_block(block)

            def step(i, _):
                forward_pair(i)
                return 0

            lax.fori_loop(0, pairs, step, 0)
            return 0

        lax.fori_loop(0, y.NB, forward_block, 0)

        def finish_step(i, _):
            total = s.RUN[i][:, :1]
            store_mixture(i, unstack_pair(stack_pair(s.ATT[i]) / total), s.LSE[i][:, :1], total)
            return 0

        lax.fori_loop(0, pairs, finish_step, 0)
        for chunk in range(h_mix.chunks):
            h_mix.start(chunk)

    g_gu[0].pump()
    if y.NB > 1:
        g_gu[2].launch()
    f_pt.pump_forward()
    h_mix.forward_all()
    g_gu[1].pump()
    g_gu[2].pump(1)
    h_mix.landed_all()
    f_pt.landed()
    def middle_rows(block, _):
        at = pl.ds(pl.multiple_of(block * 2 * T, 2 * T), 2 * T)
        values = tok[at, :].astype(f32)
        for p in range(N):
            values = values + dot_nt(s.MIX[at, p * 256 : (p + 1) * 256], s.PT[p])
        scale = row_scale(values)
        s.MID[at, :] = values
        s.R2[at, :] = jnp.broadcast_to(scale, (2 * T, LANES))
        s.NM[at, :] = (values * scale * s.GAIN[1:2, :]).astype(bf16)
        return 0

    lax.fori_loop(0, 2, middle_rows, 0)
    g_gu[2].pump()
    for g in [g_dt] + g_gu:
        g.landed_all()

    tail_low = lane_iota(2 * T) < DH

    def dense_rows(far):
        block = (1 - xo) if far else xo
        at = pl.ds(pl.multiple_of(block * 2 * T, 2 * T), 2 * T)
        both = dot_nn(s.NM[at, :], s.GU[...])
        back = dot_nn(cot[at, :], s.DT[...])
        tail = both[:, 2 * FM :]
        up_tail = pltpu.roll(tail, DH, 1)

        def gates(gate, up, pushed):
            chance = 1.0 / (1.0 + jnp.exp(-gate))
            silu = gate * chance
            return (
                silu * up,
                pushed * up * chance * (1.0 + gate * (1.0 - chance)),
                pushed * silu,
            )

        hidden, gate_gradient, up_gradient = gates(both[:, :FM], both[:, FM : 2 * FM], back[:, :FM])
        s.HID[at, :FM] = hidden.astype(bf16)
        s.GG[at, :FM] = gate_gradient.astype(bf16)
        s.GG[at, FM : 2 * FM] = up_gradient.astype(bf16)
        hidden, gate_gradient, up_gradient = gates(tail, up_tail, back[:, FM:])
        s.HID[at, FM:] = jnp.where(tail_low, hidden, 0.0).astype(bf16)
        s.GG[at, 2 * FM :] = jnp.where(
            tail_low, gate_gradient, pltpu.roll(up_gradient, DH, 1)
        ).astype(bf16)
        s.MB[at, :] = dot_nt(s.GG[at, :], s.GU[...]).astype(bf16)

    dense_rows(True)
    n_mb.start(True)
    dense_rows(False)
    n_mb.start(False)
    n_mb.pass_on()

    def grad_blocks(target, left, right, exchanges, lanes=slice(None)):
        per = A // 4
        for j in range(4):
            block = z_order[j] if A == 4 else j
            at = pl.ds(pl.multiple_of(block * 256, 256), 256)
            target[at, lanes] = dot_tn(left[:, at], right[:, lanes]).astype(bf16)
            for exchange in exchanges:
                for q in range(per):
                    exchange.start(block * per + q)

    grad_blocks(s.PDT, cot, s.HID, [w_dt])
    for g in g_gu:
        g.sent()
    grad_blocks(s.GU, s.NM, s.GG, [], slice(cuts[2][0], GUc))
    w_gu[2].start_ends()

    mid_back = n_mb.result()
    mid_own = s.MID[own_rows, :]
    r2_own = s.R2[own_rows, :][:, :1]
    scaled = mid_back * s.GAIN[1:2, :]
    s.GS[1:2, :] = jnp.sum(mid_back * mid_own * r2_own, axis=0, keepdims=True)
    middle_gradient = (
        cot[own_rows, :].astype(f32)
        + r2_own * scaled
        - mid_own * (r2_own * r2_own * r2_own) * jnp.mean(scaled * mid_own, axis=-1, keepdims=True)
    )
    s.MG[...] = middle_gradient
    branch = middle_gradient.astype(bf16)
    s.BG[own_rows, :] = branch
    h_bg.start(0)
    for p in range(N):
        part = dot_nn(branch, s.PT[p]).astype(bf16)
        s.DO[2 * p] = part[:, :LANES]
        s.DO[2 * p + 1] = part[:, LANES:]

    def backward_block(block, between=lambda part: None):
        s.DKS[...] = jnp.zeros(s.DKS.shape, f32)
        s.DHD[...] = jnp.zeros(s.DHD.shape, f32)

        def step(i, _):
            query, pushed = s.QP[i], s.DO[i]
            query2, pushed2 = stack_pair(query), stack_pair(pushed)
            product = pushed.astype(f32) * s.ATT[i]
            delta = jnp.sum(stack_pair(product), axis=1, keepdims=True)
            scores = dot_nt(query2, s.KP[i]) + pair_bias()
            chance = jnp.exp(scores - s.LSE[i][:, :1])
            gradient = (chance * (dot_nt(pushed2, s.VP[i]) - delta)).astype(bf16)
            s.QB[i] = s.QB[i] + unstack_pair(dot_nn(gradient, s.KP[i])) * DH**-0.5
            key_back = dot_tn(gradient, query2)
            value_back = dot_tn(chance.astype(bf16), pushed2)
            at = pl.ds(pl.multiple_of(block * KB, KB), KB)
            lanes = pl.ds(pl.multiple_of(i * LANES, LANES), LANES)
            heads = s.KVF[at, 256:384]
            found = s.DHD[...]
            for back, first, e in ((key_back, 0, 0), (value_back, 128, KR)):
                one, two = both_halves(s.KVF[at, first : first + 128].astype(f32))
                spread = jnp.concatenate([s.EK[e, :, lanes], s.EK[e + 1, :, lanes]], axis=1)
                joined = jnp.concatenate([back * one, back * two], axis=1).astype(bf16)
                found = found + dot_nt(joined, spread)
                wide = dot_nn(heads, spread)
                s.DKS[e] = s.DKS[e] + wide[:, :LANES] * back
                s.DKS[e + 1] = s.DKS[e + 1] + wide[:, LANES:] * back
            s.DHD[...] = found
            return 0

        quarter = pairs // 4
        for part in range(4):
            lax.fori_loop(part * quarter, (part + 1) * quarter, step, 0)
            between(part)
        at = pl.ds(pl.multiple_of(block * KB, KB), KB)
        low = lane_iota(KB) < DH
        for e in (0, KR):
            both = jnp.where(low, fold_halves(s.DKS[e]), fold_halves(s.DKS[e + 1])) * 0.5
            s.KVF[at, e * DH : e * DH + 128] = both.astype(bf16)
        s.KVF[at, 256:384] = (s.DHD[...] * 0.5).astype(bf16)

    s.QB[...] = jnp.zeros(s.QB.shape, f32)
    g_kv.sent()
    if y.NB == 1:

        def between(part):
            if part < 3:
                w_dt.pump(1)
                w_gu[2].pump(2 if part == 0 else 1)

        backward_block(0, between)
    else:

        def backward_step(block, _):
            mask_block(block)
            expand_block(block)
            backward_block(block)
            return 0

        lax.fori_loop(0, y.NB, backward_step, 0)
    for z in z_order:
        w_kv.start(z)
    for i in range(2):
        grad_blocks(s.GU, s.NM, s.GG, [w_gu[i]], slice(cuts[i][0], sum(cuts[i])))
    w_gu[2].pump()
    w_gu[2].finish()
    w_kv.pump(1)
    query_back = jnp.concatenate([s.QB[i] for i in range(pairs)], axis=1)
    heads_back = jnp.zeros((T, LANES), f32)
    shared_back = []
    for r in range(QR):
        turned = s.QROT[r]
        product = (query_back * jnp.concatenate([turned] * pairs, axis=1)).astype(bf16)
        heads_back = heads_back + dot_nt(product, s.EQ[r])
        product = spread_heads(r) * query_back
        total = product[:, :LANES]
        for i in range(1, pairs):
            total = total + product[:, i * LANES : (i + 1) * LANES]
        shared_back.append(fold_halves(total))
    low = lane_iota(T) < DH
    shared_tiles = [
        rotated(jnp.where(low, shared_back[2 * t], shared_back[2 * t + 1]), back=True) * (1.0 / QR)
        for t in range(QR // 2)
    ]
    heads_back = heads_back * (1.0 / QR)

    w_kv.pump(1)
    for far in (True, False):
        block = (1 - xo) if far else xo
        at = pl.ds(pl.multiple_of(block * 2 * T, 2 * T), 2 * T)
        s.OP[at, :] = dot_nt(s.HID[at, :], s.DT[...]).astype(bf16)
        n_op.start(far)
    w_kv.pump()
    n_op.pass_on()
    w_dt.pump()
    w_dt.finish()
    w_kv.finish()

    key_shared = rotated(s.DKVO[:, 0:128], back=True)
    value_shared = s.DKVO[:, 128:256]
    head_tile = s.DKVO[:, 256:384]
    for p in range(N):
        s.QGS[p, :, :LANES] = place_lanes(
            canonical_pieces(shared_tiles, LANES, p * y.SQ, y.SQ, 0, 0)
        ).astype(bf16)
        s.QGS[p, :, LANES:] = place_lanes(
            [
                (key_shared, p * y.SK, y.oK, y.SK),
                (value_shared, p * y.SK, y.oV, y.SK),
                (heads_back, p * y.HQ, y.oq, y.HQ),
                (head_tile, p * y.HK, y.ok, y.HK),
                (head_tile, (N + p) * y.HK, y.ov, y.HK),
            ]
        ).astype(bf16)
    for k, peer in enumerate(narrow_peers):
        send(s.QGS.at[peer[1]], s.QGR.at[n], k_a2a + k, peer)
    s.QGR[n] = s.QGS[n]

    first_back = jnp.zeros((T, D), f32)
    for p in range(N):
        first_back = first_back + dot_nt(s.QGS[p], s.WQ[p])
    x_own = tok[own_rows, :].astype(f32)
    r1_own = row_scale(x_own)
    s.GS[0:1, :] = jnp.sum(first_back * x_own * r1_own, axis=0, keepdims=True)
    for k, peer in enumerate(narrow_peers):
        send(s.GS, s.GR.at[k], k_gain + k, peer)
    scaled = first_back * s.GAIN[0:1, :]
    tokens_gradient = (
        s.MG[...]
        + r1_own * scaled
        - x_own * (r1_own * r1_own * r1_own) * jnp.mean(scaled * x_own, axis=-1, keepdims=True)
    )
    o_tok[own_rows, :] = tokens_gradient.astype(bf16)
    for chunk in range(h_tg.chunks):
        h_tg.start(chunk)

    o_out[own_rows, :] = (s.MID[own_rows, :] + n_op.result()).astype(bf16)
    h_og.start(0)

    w_gu[0].pump(1)
    h_bg.finish()
    grad_blocks(s.PPT, s.BG, s.MIX.at[:, pl.ds(pl.multiple_of(n * 256, 256), 256)], [w_pt])
    w_gu[0].pump(1)
    for k, peer in enumerate(narrow_peers):
        arrive(s.QGR.at[peer[1]], k_a2a + k)
    for k in range(3):
        arrive(s.GR.at[k], k_gain + k)
    gain_rows = s.GS[...]
    for k in range(3):
        gain_rows = gain_rows + s.GR[k]
    lane_row = row_iota(LANES, D)
    spread = jnp.where(
        lane_row == y.og,
        gain_rows[0:1],
        jnp.where(lane_row == y.og + 1, gain_rows[1:2], 0.0),
    )
    gain_columns = spread.T
    for j in range(4):
        block = z_order[j] if A == 4 else j
        lanes = pl.ds(pl.multiple_of(block * 256, 256), 256)
        value = jnp.zeros((256, 256), f32)
        for p in range(N):
            value = value + dot_tn(s.NORM[p * T : (p + 1) * T, lanes], s.QGR[p])
        s.PQ[pl.ds(pl.multiple_of(block * 256, 256), 256), :] = value.astype(bf16)
    s.PQ[:, LANES:] = (s.PQ[:, LANES:].astype(f32) + gain_columns).astype(bf16)
    for z in z_order:
        w_q.start(z)

    w_gu[0].pump()
    w_gu[1].pump(1)
    w_gu[0].finish()
    w_gu[1].pump(1)
    w_pt.pump(1)
    w_gu[1].pump()
    w_pt.pump(1)
    w_q.pump(1)
    h_tg.finish()
    write(o_tok, r_tok)
    h_og.finish()
    write(o_out, r_out)
    w_gu[1].finish()
    w_gu[2].finish_y()
    write(o_gu, r_gu)
    write(o_dt, r_dt)
    w_pt.pump()
    w_q.pump(1)
    w_pt.finish()
    write(o_pt, r_pt)
    w_q.pump()
    w_q.finish()
    write(o_q, r_q)
    for exchange in (g_wq, g_pt, g_dt, f_wq, f_pt, w_kv, w_dt, *w_gu, w_pt, w_q):
        exchange.sent()
    for copy in pending:
        copy.wait_send()
    for copy in written:
        copy.wait()


def results_kernel(y, out, tok, gu, dt, pt, q, *outs):
    o_out, o_tok, o_pre, o_qh, o_qs, o_kh, o_ks, o_vh, o_vs, o_pt, o_mid, o_gate, o_up, o_down = outs
    FM, F, half = y.FM, y.F, y.F - y.FM
    o_out[...] = out[...]
    o_tok[...] = tok[...].astype(f32)
    o_qs[...] = q[:, :LANES].T[: y.SQ]
    second = q[:, LANES:].T
    o_ks[...] = second[y.oK : y.oK + y.SK]
    o_vs[...] = second[y.oV : y.oV + y.SK]
    o_qh[...] = second[y.oq : y.oq + y.HQ]
    o_kh[...] = second[y.ok : y.ok + y.HK]
    o_vh[...] = second[y.ov : y.ov + y.HK]
    o_pre[...] = second[y.og : y.og + 1]
    o_mid[...] = second[y.og + 1 : y.og + 2]
    for first in range(0, 256, LANES):
        o_pt[first : first + LANES, :] = pt[:, first : first + LANES].T
    for first in range(0, FM, LANES):
        o_down[first : first + LANES, :] = dt[:, first : first + LANES].T
        o_gate[first : first + LANES, :] = gu[:, first : first + LANES].T
        o_up[first : first + LANES, :] = gu[:, FM + first : FM + first + LANES].T
    tail = gu[:, 2 * FM :].T
    o_gate[FM:, :] = tail[:half]
    o_up[FM:, :] = tail[half:]
    o_down[FM:, :] = dt[:, FM:].T[:half]


def solution(mesh):
    W, N = mesh.shape["wide"], mesh.shape["narrow"]

    def on_device(
        tokens,
        documents,
        prenorm,
        qheads,
        qshared,
        kheads,
        kshared,
        vheads,
        vshared,
        project,
        midnorm,
        gating,
        upward,
        downward,
        cotangent,
    ):
        R, T, D = tokens.shape
        L = documents.shape[1]
        RW, F = gating.shape
        y = make_layout(W, N, T, D, F, L, N * kheads.shape[1] // KR)
        assert R == N
        scratch = scratch_list(y)
        arrivals = 33 * y.A + 44
        sends = arrivals + 14 * y.A
        vmem = pl.BlockSpec(memory_space=pltpu.VMEM)

        def kernel(*refs):
            block_kernel(y, tuple(scratch), *refs)

        shape = jax.ShapeDtypeStruct
        width = 2 * y.FM + LANES
        raw = pl.pallas_call(
            kernel,
            out_shape=(
                shape((y.M, D), bf16),
                shape((y.M, D), bf16),
                shape((RW, width), f32),
                shape((RW, y.FP), f32),
                shape((RW, 256), f32),
                shape((RW, 256), f32),
            ),
            in_specs=[vmem] * 15,
            out_specs=[pl.BlockSpec(memory_space=pl.ANY)] * 6,
            scratch_shapes=[*scratch.values()]
            + [pltpu.SemaphoreType.DMA((count,)) for count in (sends, arrivals, 6)],
            compiler_params=pltpu.CompilerParams(
                collective_id=0, has_side_effects=True, vmem_limit_bytes=63 * 2**20
            ),
            name="block",
        )(
            tokens.reshape(y.M, D),
            documents,
            prenorm.reshape(1, RW),
            qheads.T,
            qshared.T,
            kheads.T,
            kshared.T,
            vheads.T,
            vshared.T,
            project,
            midnorm.reshape(1, RW),
            gating.T,
            upward.T,
            downward,
            cotangent.reshape(y.M, D),
        )

        def results(*refs):
            results_kernel(y, *refs)

        outputs = pl.pallas_call(
            results,
            out_shape=(
                shape((y.M, D), bf16),
                shape((y.M, D), f32),
                shape((1, RW), f32),
                shape((y.HQ, RW), f32),
                shape((y.SQ, RW), f32),
                shape((y.HK, RW), f32),
                shape((y.SK, RW), f32),
                shape((y.HK, RW), f32),
                shape((y.SK, RW), f32),
                shape((256, RW), f32),
                shape((1, RW), f32),
                shape((F, RW), f32),
                shape((F, RW), f32),
                shape((F, RW), f32),
            ),
            in_specs=[vmem] * 6,
            out_specs=[vmem] * 14,
            compiler_params=pltpu.CompilerParams(vmem_limit_bytes=63 * 2**20),
            name="results",
        )(*raw)
        turned = (3, 4, 5, 6, 7, 8, 11, 12)
        outputs = [v.T if i in turned else v for i, v in enumerate(outputs)]
        outputs[0] = outputs[0].reshape(R, T, D)
        outputs[1] = outputs[1].reshape(R, T, D)
        outputs[2] = outputs[2].reshape(RW)
        outputs[10] = outputs[10].reshape(RW)
        return tuple(outputs)

    split = P("wide", "narrow")
    flipped = P("narrow", "wide")
    whole = P(None, "wide", None)
    gain = P("wide")
    return jax.shard_map(
        on_device,
        mesh=mesh,
        in_specs=(
            whole,
            P(),
            gain,
            split,
            split,
            split,
            split,
            split,
            split,
            flipped,
            gain,
            split,
            split,
            flipped,
            whole,
        ),
        out_specs=(
            whole,
            whole,
            gain,
            split,
            split,
            split,
            split,
            split,
            split,
            flipped,
            gain,
            split,
            split,
            flipped,
        ),
        check_vma=False,
    )
```

```python
import math
from types import SimpleNamespace

import jax
import jax.numpy as jnp
from jax import lax
from jax.experimental import pallas as pl
from jax.experimental.pallas import tpu as pltpu
from jax.sharding import PartitionSpec as P

DH = 64
QR = 6
KR = 2
VR = 2
LANES = 128

epsilon = 1e-06
masked_score = -1e30
MESH = pl.DeviceIdType.MESH
y_first_chunks = (2,)
z_first_chunks = (2,)
f32 = jnp.float32
bf16 = jnp.bfloat16


def dot_nn(a, b):
    return lax.dot_general(a, b, (((1,), (0,)), ((), ())), preferred_element_type=f32)


def dot_nt(a, b):
    return lax.dot_general(a, b, (((1,), (1,)), ((), ())), preferred_element_type=f32)


def dot_tn(a, b):
    return lax.dot_general(a, b, (((0,), (0,)), ((), ())), preferred_element_type=f32)


def lane_iota(rows, cols=LANES):
    return lax.broadcasted_iota(jnp.int32, (rows, cols), 1)


def row_iota(rows, cols=LANES):
    return lax.broadcasted_iota(jnp.int32, (rows, cols), 0)


def place_lanes(pieces):
    rows = pieces[0][0].shape[0]
    lane = lane_iota(rows)
    result = jnp.zeros((rows, LANES), f32)
    for tile, start, to, count in pieces:
        shift = (to - start) % LANES
        moved = pltpu.roll(tile, shift, 1) if shift else tile
        result = jnp.where((lane >= to) & (lane < to + count), moved, result)
    return result


def canonical_pieces(tiles, width, first, count, start, to):
    pieces = []
    while count:
        part, inside = divmod(first, width)
        take = min(count, width - inside)
        pieces.append((tiles[part], start + inside, to, take))
        first, to, count = first + take, to + take, count - take
    return pieces


def both_halves(tile):
    low = lane_iota(tile.shape[0]) < DH
    turned = pltpu.roll(tile, DH, 1)
    return jnp.where(low, tile, turned), jnp.where(low, turned, tile)


def swap_quarters(tile):
    low = lane_iota(tile.shape[0]) % DH < DH // 2
    return jnp.where(low, pltpu.roll(tile, LANES - DH // 2, 1), pltpu.roll(tile, DH // 2, 1))


def stack_pair(tile):
    low = lane_iota(tile.shape[0]) < DH
    zero = jnp.zeros_like(tile)
    return jnp.concatenate([jnp.where(low, tile, zero), jnp.where(low, zero, tile)], axis=0)


def unstack_pair(rows):
    half = rows.shape[0] // 2
    low = lane_iota(half) < DH
    return jnp.where(low, rows[:half], rows[half:])


def fold_halves(tile):
    return tile + pltpu.roll(tile, DH, 1)


def row_scale(values):
    return lax.rsqrt(jnp.mean(values * values, axis=-1, keepdims=True) + epsilon)


def make_layout(W, N, T, D, F, L, heads):
    lay = SimpleNamespace()
    lay.W, lay.N, lay.T, lay.D, lay.F, lay.L, lay.heads = W, N, T, D, F, L, heads
    lay.A = W // 2
    lay.RW = D // W
    lay.M = N * T
    lay.FM = F // LANES * LANES
    lay.FP = lay.FM + LANES
    full = lay.FM // 256
    lay.chunks = [(768 * i, 512, 256 * i, 256) for i in range(full)]
    lay.chunks.append((768 * full, 3 * LANES, 256 * full, 256))
    lay.FW = 768 * full + 5 * LANES
    assert lay.FM % 256 == LANES
    lay.pairs = heads // 2
    assert len(lay.chunks) == 3
    lay.KB = L if L <= 1024 else 512
    lay.NB = L // lay.KB
    lay.SQ = QR * DH // N
    lay.SK = KR * DH // N
    lay.HQ = heads * QR // N
    lay.HK = heads * KR // N
    lay.oK, lay.oV = 0, lay.SK
    lay.oq = 2 * lay.SK
    lay.ok = lay.oq + lay.HQ
    lay.ov = lay.ok + lay.HK
    lay.og = lay.ov + lay.HK
    assert N == 4 and W % 8 == 0 and T == LANES and D == heads * DH == 1024
    assert F % LANES == DH and lay.SQ <= LANES and lay.og + 2 <= LANES
    return lay


def scratch_list(y):
    W, N, T, D, L, A, RW, M = y.W, y.N, y.T, y.D, y.L, y.A, y.RW, y.M
    vm = lambda *shape, kind=bf16: pltpu.VMEM(shape, kind)
    GUc = 2 * y.FM + LANES
    return dict(
        WQ=vm(N, D, 256),
        PT=vm(N, D, 256),
        FW=vm(D, y.FW),
        KVF=vm(L, 384),
        KP=vm(y.pairs, LANES, y.KB),
        VP=vm(y.pairs, LANES, y.KB),
        EQ=vm(QR, LANES, D),
        SHARED=vm(2, LANES, y.KB, kind=f32),
        HT=vm(y.pairs, 8, y.KB, kind=f32),
        DHT=vm(y.pairs, 8, y.KB, kind=f32),
        BIAS=vm(T, y.KB, kind=f32),
        DOC=vm(T, LANES, kind=f32),
        ROPE=vm(2, T, LANES, kind=f32),
        GAIN=vm(8, D, kind=f32),
        QROT=vm(QR, T, LANES, kind=f32),
        QH=vm(T, 256),
        QP=vm(y.pairs, T, LANES),
        ATT=vm(y.pairs, T, LANES, kind=f32),
        LSE=vm(y.pairs, 2 * T, LANES, kind=f32),
        RUN=vm(y.pairs if y.NB > 1 else 1, 2 * T, LANES, kind=f32),
        MIX=vm(M, D),
        NORM=vm(M, D),
        MID=vm(M, D, kind=f32),
        NM=vm(M, D),
        R2=vm(M, LANES, kind=f32),
        HID=vm(M, y.FP),
        GG=vm(M, GUc),
        MB=vm(M, D),
        MBC=vm(2, T, D),
        MBX=vm(T, D),
        MBS=vm(T, D),
        OP=vm(M, D),
        OPC=vm(2, T, D),
        OPX=vm(T, D),
        OPS=vm(T, D),
        BG=vm(M, D),
        MG=vm(T, D, kind=f32),
        DO=vm(y.pairs, T, LANES),
        QB=vm(y.pairs, T, LANES, kind=f32),
        DST=vm(2, LANES, y.KB, kind=f32),
        DKVY=vm(A * T, 384),
        DKVR=vm((A + 1) * T, 384),
        DKVO=vm(T, 384, kind=f32),
        QGS=vm(N, T, 256),
        QGR=vm(N, T, 256),
        OUT=vm(M, D),
        TOK=vm(M, D),
        TFW=vm(RW, y.FW, kind=f32),
        TPT=vm(RW, 256, kind=f32),
        TQ=vm(RW, 256, kind=f32),
        GS=vm(8, D, kind=f32),
        GR=vm(3, 8, D, kind=f32),
        YFW=vm(A * RW, y.FW),
        **{
            f"RF{i}": vm((A + 1) * RW * (2 if i in z_first_chunks else 1), wide + units)
            for i, (_, wide, _, units) in enumerate(y.chunks)
        },
        PPT=vm(D, 256),
        YPT=vm(A * RW, 256),
        RPT=vm((A + 1) * RW, 256),
        PQ=vm(D, 256),
        YQ=vm(A * RW, 256),
        RQ=vm((A + 1) * RW, 256),
    )


schedule = (
    "prep_wq", "wq.L", "wq.Ly", "prep_pt", "pt.Ly", "pt.L", "wq.h1", "fwq.s0", "prep_fw", "c.Ly",
    "b.L", "consts", "wq.h2", "fwq.s1", "pt.h1", "b.h1", "fwq.s2", "a.L", "b.Ly", "wq.h3", "b.h2",
    "pt.h2", "fwq.s3", "fwq.f0", "fwq.f1", "fwq.f2", "b.y1", "fpt.s0", "c.L", "b.y2", "a.Ly",
    "fwq.f3", "project", "kv.L", "pt.h3", "kv.h1", "kv.h2", "fpt.s1", "fpt.f0", "kv.Ly", "a.h1",
    "kv.h3", "a.h2", "b.h3", "a.y1", "a.y2", "fpt.s2", "fpt.s3", "c.h1", "queries", "at_x", "at0",
    "at1", "a.h3", "a.y3", "fpt.f1", "fpt.f2", "at2", "at3", "mix.f0", "mix.f1", "c.h2", "fpt.f3",
    "mix.f2", "b.y3", "mix.f3", "middle", "ff_a", "ff_b", "c.h3", "ffCf", "ffCn", "mb.pass",
    "g_c", "wc.ends", "g_b", "mid", "bq0", "op.start", "wc.s1", "bq1", "bq2", "bq3", "wc.s2",
    "op.pass", "kvst", "bg.f", "wb.s0", "pt.g", "wkv.d0", "wb.s1", "op.res", "qb", "wpt.d0",
    "wkv.d1", "wkv.d2", "g_a", "wb.s2", "wa.s0", "wpt.d1", "wkv.fin", "qg", "wc.fin", "wa.s1",
    "fb", "q.g", "og.f", "wa.s2", "wc.finy", "wpt.d2", "tg.f", "wq2.d0", "wq2.d1", "tg.l",
    "wq2.d2", "wa.fin", "wpt.fin", "og.l", "wb.fin", "wq2.fin",
)


def block_kernel(y, names, *refs):
    tok, docs, prenorm, qheads, qshared, kheads, kshared, vheads, vshared = refs[:9]
    project, midnorm, gating, upward, downward, cot = refs[9:15]
    r_out, r_tok, r_fw, r_pt, r_q = refs[15:20]
    s = SimpleNamespace(**dict(zip(names, refs[20:])))
    ssem, rsem, wsem = refs[20 + len(names) :]
    o_out, o_tok, o_fw, o_pt, o_q = s.OUT, s.TOK, s.TFW, s.TPT, s.TQ
    written = []

    def write(src, dst):
        copy = pltpu.make_async_copy(src, dst, wsem.at[len(written)])
        copy.start()
        written.append(copy)

    W, N, T, D, F, L, A, RW, M = y.W, y.N, y.T, y.D, y.F, y.L, y.A, y.RW, y.M
    FM, FP, KB, pairs = y.FM, y.FP, y.KB, y.pairs
    w = lax.axis_index("wide")
    n = lax.axis_index("narrow")
    zi, yi = w // 2, w % 2
    xo, co = n // 2, n % 2
    y_peer = (zi * 2 + 1 - yi, n)
    c_peer = (w, xo * 2 + 1 - co)
    x_peer = (w, (1 - xo) * 2 + co)
    d_peer = (w, (1 - xo) * 2 + 1 - co)
    narrow_peers = (c_peer, x_peer, d_peer)
    taken = [0, rsem.shape[0]]

    def take(count=1):
        taken[0] += count
        return taken[0] - count

    def take_send(count):
        taken[1] += count
        return taken[1] - count

    def remote(src, dst, k, peer, send_k=None):
        return pltpu.make_async_remote_copy(
            src_ref=src,
            dst_ref=dst,
            send_sem=ssem.at[k if send_k is None else send_k],
            recv_sem=rsem.at[k],
            device_id=peer,
            device_id_type=MESH,
        )

    pending = []

    def send(src, dst, k, peer, started=pending):
        copy = remote(src, dst, k, peer)
        copy.start()
        started.append(copy)

    def arrive(dst, k):
        remote(dst, dst, k, y_peer).wait_recv()

    def rows(ref, first, count, lanes=None):
        at = pl.ds(pl.multiple_of(first, 16), count)
        return ref.at[at] if lanes is None else ref.at[at, pl.ds(*lanes)]

    def each_at(distance, act):
        if distance == 0:
            act(zi, None)
            return
        pl.when(zi >= distance)(lambda: act(zi - distance, True))
        pl.when(zi + distance < A)(lambda: act(zi + distance, False))

    right_peer = ((zi + 1) * 2 + yi, n)
    left_peer = ((zi - 1) * 2 + yi, n)

    barrier = pltpu.get_barrier_semaphore()
    z_peers = [(((zi + step) % A) * 2 + yi, n) for step in range(1, A)]
    peers = [y_peer, *narrow_peers, *z_peers]
    for peer in peers:
        pl.semaphore_signal(barrier, inc=1, device_id=peer, device_id_type=MESH)
    pl.semaphore_wait(barrier, len(peers))

    class Gather:
        def __init__(self, ref, count, lanes=None, y_first=False):
            self.ref, self.count, self.lanes, self.y_first = ref, count, lanes, y_first
            self.kz, self.ky, self.kl = take(A), take(A), take_send(A)
            self.next = self.next_y = 1

        def part(self, wide):
            return rows(self.ref, wide * self.count, self.count, self.lanes)

        def block(self, z):
            if self.y_first:
                return rows(self.ref, z * 2 * self.count, 2 * self.count, self.lanes)
            return self.part(z * 2 + yi)

        def along(self, z, to_right):
            block = self.block(z)
            if to_right:
                return remote(block, block, self.kz + z, right_peer)
            return remote(block, block, self.kz + z, left_peer, self.kl + z)

        def across(self, z):
            part = self.part(z * 2 + yi)
            return remote(part, part, self.ky + z, y_peer)

        def landed(self, z):
            arrive(self.part(z * 2 + 1 - yi), self.ky + z)

        def launch_y(self):
            self.across(zi).start()

        def launch(self):
            if self.y_first:
                self.landed(zi)
            pl.when(zi < A - 1)(lambda: self.along(zi, True).start())
            pl.when(zi > 0)(lambda: self.along(zi, False).start())

        def hop(self, distance, across):
            def act(z, to_right):
                arrive(self.block(z), self.kz + z)
                more = zi < A - 1 if to_right else zi > 0
                pl.when(more)(lambda: self.along(z, to_right).start())
                if across and not self.y_first:
                    self.across(z).start()

            each_at(distance, act)

        def pump(self, count=A, across=True):
            for _ in range(min(count, A - self.next)):
                self.hop(self.next, across)
                self.next += 1

        def pump_y(self, count=A):
            for _ in range(min(count, self.next - self.next_y)):
                each_at(self.next_y, lambda z, _: self.across(z).start())
                self.next_y += 1

        def landed_all(self):
            if not self.y_first:
                for z in range(A):
                    self.landed(z)

        def sent(self):
            self.across(zi).wait_send()
            pl.when(zi < A - 1)(lambda: self.along(zi, True).wait_send())
            pl.when(zi > 0)(lambda: self.along(zi, False).wait_send())
            for distance in range(1, A):

                def act(z, to_right):
                    more = zi < A - 1 if to_right else zi > 0
                    pl.when(more)(lambda: self.along(z, to_right).wait_send())
                    if not self.y_first:
                        self.across(z).wait_send()

                each_at(distance, act)

    class Spread:
        def __init__(self, gather, ref):
            self.gather, self.ref = gather, ref
            self.next = self.passed = 0
            self.kx, self.kc, self.kd = take(A), take(A), take(A)

        def part(self, owner, z):
            return rows(self.ref.at[owner], z * 2 * RW, 2 * RW)

        def copies(self, z):
            part = self.part(n, z)
            return remote(part, part, self.kx + z, x_peer), remote(part, part, self.kc + z, c_peer)

        def onward(self, z):
            part = self.part(x_peer[1], z)
            return remote(part, part, self.kd + z, c_peer)

        def start(self, distance):
            def act(z, _):
                self.gather.landed(z)
                for copy in self.copies(z):
                    copy.start()

            each_at(distance, act)

        def pump(self, count=A):
            for _ in range(min(count, A - self.next)):
                self.start(self.next)
                self.next += 1

        def pump_forward(self, count=A):
            for _ in range(min(count, A - self.passed)):
                self.forward(self.passed)
                self.passed += 1

        def forward(self, distance):
            def act(z, _):
                arrive(self.part(x_peer[1], z), self.kx + z)
                self.onward(z).start()

            each_at(distance, act)

        def landed(self):
            for z in range(A):
                arrive(self.part(c_peer[1], z), self.kc + z)
                arrive(self.part(d_peer[1], z), self.kd + z)

        def sent(self):
            for z in range(A):
                for copy in self.copies(z):
                    copy.wait_send()
                self.onward(z).wait_send()

    class Share:
        def __init__(self, ref, chunks):
            self.ref, self.chunks = ref, chunks
            self.kx, self.kc, self.kd = take(chunks), take(chunks), take(chunks)
            self.width = D // chunks

        def part(self, owner, chunk):
            lanes = pl.ds(pl.multiple_of(chunk * self.width, LANES), self.width)
            return self.ref.at[pl.ds(pl.multiple_of(owner * T, T), T), lanes]

        def start(self, chunk):
            send(self.part(n, chunk), self.part(n, chunk), self.kx + chunk, x_peer)
            send(self.part(n, chunk), self.part(n, chunk), self.kc + chunk, c_peer)

        def forward(self, chunk):
            part = self.part(x_peer[1], chunk)
            arrive(part, self.kx + chunk)
            send(part, part, self.kd + chunk, c_peer)

        def landed(self, chunk):
            arrive(self.part(c_peer[1], chunk), self.kc + chunk)
            arrive(self.part(d_peer[1], chunk), self.kd + chunk)

        def forward_all(self):
            for chunk in range(self.chunks):
                self.forward(chunk)

        def landed_all(self):
            for chunk in range(self.chunks):
                self.landed(chunk)

        def finish(self):
            self.forward_all()
            self.landed_all()

    class NarrowSum:
        def __init__(self, part_ref, core_ref, x_ref, send_ref):
            self.ref, self.core, self.x, self.out = part_ref, core_ref, x_ref, send_ref
            self.kc, self.kx = take(2), take(1)

        def part(self, owner):
            return rows(self.ref, owner * T, T)

        def start(self, far):
            owner = ((1 - xo) if far else xo) * 2 + 1 - co
            send(self.part(owner), self.core.at[int(far)], self.kc + int(far), c_peer)

        def pass_on(self):
            arrive(self.core.at[1], self.kc + 1)
            total = self.part((1 - xo) * 2 + co)[...].astype(f32) + self.core[1].astype(f32)
            self.out[...] = total.astype(bf16)
            send(self.out, self.x, self.kx, x_peer)

        def result(self):
            arrive(self.core.at[0], self.kc)
            arrive(self.x, self.kx)
            return (
                self.part(n)[...].astype(f32) + self.core[0].astype(f32) + self.x[...].astype(f32)
            )

    class WideSum:
        def __init__(self, part_ref, y_ref, z_ref, out_ref, count, lanes=None, z_first=False):
            self.ref, self.y, self.z, self.total = part_ref, y_ref, z_ref, out_ref
            self.count, self.lanes, self.z_first = count, lanes, z_first
            self.size = 2 * count if z_first else count
            self.next = 0
            self.z_lanes = lanes and (0, lanes[1])
            self.ky, self.kz, self.kl = take(1 if z_first else A), take(A + 1), take_send(A)

        def part(self, wide):
            return rows(self.ref, wide * self.count, self.count, self.lanes)

        def block(self, z):
            if self.z_first:
                return rows(self.ref, z * 2 * self.count, 2 * self.count, self.lanes)
            return self.part(z * 2 + yi)

        def got_y(self, z):
            return rows(self.y, z * self.count, self.count, self.lanes)

        def got_z(self, slot):
            return rows(self.z, slot * self.size, self.size, self.z_lanes)

        def across(self, z):
            return remote(self.part(z * 2 + 1 - yi), self.got_y(z), self.ky + z, y_peer)

        def along(self, z, to_right):
            block = self.block(z)
            if to_right:
                return remote(block, self.got_z(z), self.kz + z, right_peer)
            slot = jnp.where(z == zi - 1, A, z)
            return remote(block, self.got_z(slot), self.kz + slot, left_peer, self.kl + z)

        def start(self, z):
            if not self.z_first:
                self.across(z).start()

        def gather_y(self, z):
            block = self.block(z)[...].astype(f32)
            if self.z_first:
                return block
            arrive(self.got_y(z), self.ky + z)
            return block + self.got_y(z)[...].astype(f32)

        def stage(self, step):
            def move(z, to_right, joined):
                value = self.gather_y(z)
                if joined:
                    arrive(self.got_z(z), self.kz + z)
                    value = value + self.got_z(z)[...].astype(f32)
                self.block(z)[...] = value.astype(bf16)
                self.along(z, to_right).start()

            right, left = A - 1 - step + zi, step - (A - 1 - zi)
            to_right = (right < A) & (right > zi)
            to_left = (left >= 0) & (left < zi)
            pl.when(to_right & (zi > 0))(lambda: move(right, True, True))
            pl.when(to_left & (zi < A - 1))(lambda: move(left, False, True))
            if not self.z_first:
                pl.when(to_right & (zi == 0))(lambda: move(right, True, False))
                pl.when(to_left & (zi == A - 1))(lambda: move(left, False, False))

        def pump(self, count=A):
            for _ in range(min(count, A - 1 - self.next)):
                self.stage(self.next)
                self.next += 1

        def send_direct(self, count=A):
            for k in range(self.next, min(self.next + count, A - 1)):
                self.next += 1
                z = z_order[k] if A == 4 else (zi + 1 + k) % A
                block = self.block(z)
                block[...] = self.gather_y(z).astype(bf16)
                self.direct(z).start()

        def direct(self, z):
            return remote(
                self.block(z), self.got_z(zi), self.kz + zi, (z * 2 + yi, n), self.kl + z
            )

        def finish_direct(self):
            self.total[...] = self.gather_y(zi)
            for step in range(1, A):
                self.add((zi + step) % A)

        def sent_direct(self):
            for z in range(A):
                self.across(z).wait_send()
                pl.when(zi != z)(lambda: self.direct(z).wait_send())

        def start_ends(self):
            @pl.when(zi == 0)
            def _():
                for z in range(A - 1, 0, -1):
                    self.along(z, True).start()

            @pl.when(zi == A - 1)
            def _():
                for z in range(A - 1):
                    self.along(z, False).start()

        def add(self, slot):
            arrive(self.got_z(slot), self.kz + slot)
            got = self.got_z(slot)[...].astype(f32)
            if not self.z_first:
                self.total[...] += got
                return
            block = self.block(zi)
            block[...] = (block[...].astype(f32) + got).astype(bf16)

        def finish(self):
            if not self.z_first:
                self.total[...] = self.gather_y(zi)
            pl.when(zi > 0)(lambda: self.add(zi))
            pl.when(zi < A - 1)(lambda: self.add(A))
            if self.z_first:
                self.last_across().start()

        def last_across(self):
            return remote(self.part(zi * 2 + 1 - yi), self.got_y(0), self.ky, y_peer)

        def finish_y(self):
            if self.z_first:
                arrive(self.got_y(0), self.ky)
                mine = self.part(zi * 2 + yi)[...].astype(f32)
                self.total[...] = mine + self.got_y(0)[...].astype(f32)

        def sent(self):
            if self.z_first:
                self.last_across().wait_send()
            for z in range(A):
                if not self.z_first:
                    self.across(z).wait_send()
                pl.when(zi < z)(lambda: self.along(z, True).wait_send())
                pl.when(zi > z)(lambda: self.along(z, False).wait_send())

    if A == 4:
        z_order = []
        for row in zip((3, 2, 1, 0), (3, 2, 0, 1), (0, 1, 3, 2), (0, 1, 2, 3)):
            z_order.append(sum(jnp.where(zi == at, z, 0) for at, z in enumerate(row)))
    else:
        z_order = range(A)

    chunks = y.chunks
    last = len(chunks) - 1
    cuts = [(base, wide + units) for base, wide, _, units in chunks]
    g_wq = Gather(s.WQ.at[n], RW)
    g_pt = Gather(s.PT.at[n], RW)
    g_kv = Gather(s.KVF, T)
    g_fw = [Gather(s.FW, RW, lanes, i in y_first_chunks) for i, lanes in enumerate(cuts)]
    f_wq, f_pt = Spread(g_wq, s.WQ), Spread(g_pt, s.PT)
    h_mix, h_bg, h_og, h_tg = Share(s.MIX, 4), Share(s.BG, 1), Share(o_out, 1), Share(o_tok, 2)
    n_mb = NarrowSum(s.MB, s.MBC, s.MBX, s.MBS)
    n_op = NarrowSum(s.OP, s.OPC, s.OPX, s.OPS)
    w_kv = WideSum(s.KVF, s.DKVY, s.DKVR, s.DKVO, T)
    w_fw = []
    for i, lanes in enumerate(cuts):
        out = o_fw.at[:, pl.ds(*lanes)]
        got = (s.RF0, s.RF1, s.RF2)[i]
        w_fw.append(WideSum(s.FW, s.YFW, got, out, RW, lanes, i in z_first_chunks))
    w_pt = WideSum(s.PPT, s.YPT, s.RPT, o_pt, RW)
    w_q = WideSum(s.PQ, s.YQ, s.RQ, o_q, RW)
    k_a2a, k_gain = take(3), take(3)
    assert taken[0] <= rsem.shape[0] and taken[1] <= ssem.shape[0]

    ops = {}

    def op(name):
        def keep(act):
            ops[name] = act
            return act

        return keep

    def gather_ops(name, gather, split):
        ops[f"{name}.L"], ops[f"{name}.Ly"] = gather.launch, gather.launch_y
        for i in range(1, 4):
            count = A if i == 3 else 1
            ops[f"{name}.h{i}"] = lambda count=count: gather.pump(count, not split)
            if split and not gather.y_first:
                ops[f"{name}.y{i}"] = lambda count=count: gather.pump_y(count)

    def spread_ops(name, spread):
        for i in range(4):
            count = A if i == 3 else 1
            ops[f"{name}.s{i}"] = lambda count=count: spread.pump(count)
            ops[f"{name}.f{i}"] = lambda count=count: spread.pump_forward(count)

    def sum_ops(name, exchange, finish, direct=False):
        for i in range(3):
            count = A if i == 2 else 1
            if direct:
                ops[f"{name}.d{i}"] = lambda count=count: exchange.send_direct(count)
            else:
                extra = 1 if exchange.z_first and i == 1 else 0
                ops[f"{name}.s{i}"] = lambda count=count + extra: exchange.pump(count)
        if exchange.z_first:
            ops[f"{name}.ends"] = exchange.start_ends
            ops[f"{name}.finy"] = finish
            ops[f"{name}.fin"] = exchange.finish
        else:
            ops[f"{name}.fin"] = finish

    gather_ops("wq", g_wq, False)
    gather_ops("pt", g_pt, False)
    gather_ops("kv", g_kv, False)
    spread_ops("fwq", f_wq)
    spread_ops("fpt", f_pt)

    def chunk_finish(i):
        exchange, lanes = w_fw[i], pl.ds(*cuts[i])
        (exchange.finish_y if exchange.z_first else exchange.finish)()
        write(exchange.total, r_fw.at[:, lanes])

    for i, name in enumerate("abc"):
        gather_ops(name, g_fw[i], True)
        sum_ops("w" + name, w_fw[i], lambda i=i: chunk_finish(i))

    def direct_finish(exchange, target=None):
        exchange.finish_direct()
        if target is not None:
            write(exchange.total, target)

    sum_ops("wkv", w_kv, lambda: direct_finish(w_kv), True)
    sum_ops("wpt", w_pt, lambda: direct_finish(w_pt, r_pt), True)
    sum_ops("wq2", w_q, lambda: direct_finish(w_q, r_q), True)

    own = pl.ds(pl.multiple_of(w * RW, RW), RW)
    own_rows = pl.ds(pl.multiple_of(n * T, T), T)
    blank = lambda count, kind=bf16: jnp.zeros((count, RW), kind)
    held = SimpleNamespace()

    @op("prep_wq")
    def _():
        shared_part = jnp.concatenate([qshared[...].astype(f32), blank(LANES - y.SQ, f32)], axis=0)
        gain_row = row_iota(8, RW)
        gain_part = jnp.where(
            gain_row == 0,
            prenorm[...].astype(f32),
            jnp.where(gain_row == 1, midnorm[...].astype(f32), 0.0),
        )
        second_part = jnp.concatenate(
            [part[...].astype(f32) for part in (kshared, vshared, qheads, kheads, vheads)]
            + [gain_part, blank(LANES - y.og - 8, f32)],
            axis=0,
        )
        s.WQ[n, own, :LANES] = shared_part.T.astype(bf16)
        s.WQ[n, own, LANES:] = second_part.T.astype(bf16)

    @op("prep_pt")
    def _():
        for first in range(0, 256, LANES):
            s.PT[n, own, first : first + LANES] = project[first : first + LANES, :].T

    @op("prep_fw")
    def _():
        for base, wide, unit, _ in chunks[:last]:
            for part, weight in enumerate((gating, upward, downward)):
                for first in range(0, 256, LANES):
                    to = base + part * 256 + first
                    s.FW[own, to : to + LANES] = weight[unit + first : unit + first + LANES, :].T
        base, wide, unit, _ = chunks[last]
        s.FW[own, base : base + LANES] = gating[unit:FM, :].T
        s.FW[own, base + LANES : base + 2 * LANES] = upward[unit:FM, :].T
        s.FW[own, base + 2 * LANES : base + wide] = jnp.concatenate(
            [gating[FM:, :], upward[FM:, :]], axis=0
        ).T
        s.FW[own, base + wide : base + wide + LANES] = downward[unit:FM, :].T
        s.FW[own, base + wide + LANES :] = jnp.concatenate(
            [downward[FM:, :], blank(FP - F)], axis=0
        ).T

    def own_row(values):
        mine = row_iota(N, values.shape[1]) == n
        return jnp.sum(jnp.where(mine, values.astype(f32), 0.0), axis=0, keepdims=True)

    def mask_block(block):
        first = block * KB
        key_docs = own_row(docs[:, pl.ds(pl.multiple_of(first, KB), KB)])
        allowed = (lane_iota(T, KB) + first <= row_iota(T, KB) + w * T) & (
            key_docs == s.DOC[:, :1]
        )
        s.BIAS[...] = jnp.where(allowed, 0.0, masked_score)

    @op("consts")
    def _():
        column, head = row_iota(LANES, D), lane_iota(LANES, D) >> 6
        for r in range(QR):
            s.EQ[r] = jnp.where(column == head * QR + r, 1.0, 0.0).astype(bf16)
        place = (w * T + row_iota(T)).astype(f32)
        lane = lane_iota(T)
        angle = place * jnp.exp((lane % (DH // 2)).astype(f32) * (-math.log(10000.0) / (DH // 2)))
        s.ROPE[0] = jnp.cos(angle)
        s.ROPE[1] = jnp.where(lane % DH < DH // 2, -jnp.sin(angle), jnp.sin(angle))

        own_docs = own_row(docs[:, pl.ds(pl.multiple_of(w * T, T), T)])
        own_docs = jnp.transpose(jnp.broadcast_to(own_docs, (T, T)))
        s.DOC[...] = own_docs

        mask_block(0)

    def rotated(tile, back=False):
        turned = swap_quarters(tile) * s.ROPE[1]
        return tile * s.ROPE[0] - turned if back else tile * s.ROPE[0] + turned

    def collect(start, width):
        pieces = []
        for p in range(N):
            pieces += [(held.second_tiles[p], start, p * width, width)]
        return place_lanes(pieces)

    @op("project")
    def _():
        f_wq.landed()
        gains = s.WQ[0, :, LANES:].astype(f32).T
        s.GAIN[0:1, :] = gains[y.og : y.og + 1]
        s.GAIN[1:2, :] = gains[y.og + 1 : y.og + 2]

        x_own = tok[own_rows, :].astype(f32)
        r1_own = row_scale(x_own)
        normed_own = (x_own * r1_own * s.GAIN[0:1, :]).astype(bf16)
        factors = [dot_nn(normed_own, s.WQ[p]) for p in range(N)]
        held.first_tiles = [part[:, :LANES] for part in factors]
        held.second_tiles = [part[:, LANES:] for part in factors]

        kv_own = pl.ds(pl.multiple_of(w * T, T), T)
        s.KVF[kv_own, 0:128] = rotated(collect(y.oK, y.SK)).astype(bf16)
        s.KVF[kv_own, 128:256] = collect(y.oV, y.SK).astype(bf16)
        s.KVF[kv_own, 256:384] = place_lanes(
            [(held.second_tiles[p], y.ok, p * y.HK, y.HK) for p in range(N)]
            + [(held.second_tiles[p], y.ov, (N + p) * y.HK, y.HK) for p in range(N)]
        ).astype(bf16)

    def spread_heads(r):
        return dot_nn(s.QH[:, :LANES], s.EQ[r]) + dot_nn(s.QH[:, LANES:], s.EQ[r])

    @op("queries")
    def _():
        query_heads = collect(y.oq, y.HQ)
        heads_high = query_heads.astype(bf16)
        s.QH[:, :LANES] = heads_high
        s.QH[:, LANES:] = (query_heads - heads_high.astype(f32)).astype(bf16)

        queries = jnp.zeros((T, D), f32)
        for r in range(QR):
            pieces = canonical_pieces(held.first_tiles, y.SQ, r * DH, DH, 0, 0)
            pieces += canonical_pieces(held.first_tiles, y.SQ, r * DH, DH, 0, DH)
            turned = rotated(place_lanes(pieces))
            s.QROT[r] = turned
            queries = queries + spread_heads(r) * jnp.concatenate([turned] * pairs, axis=1)
        for i in range(pairs):
            tile = (queries[:, i * LANES : (i + 1) * LANES] * (1.0 / QR)).astype(bf16)
            s.QP[i] = tile * jnp.asarray(DH**-0.5, bf16)

        def norm_rows(block, _):
            at = pl.ds(pl.multiple_of(block * T, T), T)
            values = tok[at, :].astype(f32)
            s.NORM[at, :] = (values * row_scale(values) * s.GAIN[0:1, :]).astype(bf16)
            return 0

        lax.fori_loop(0, N, norm_rows, 0)

    def expand_block(block):
        at = pl.ds(pl.multiple_of(block * KB, KB), KB)
        s.SHARED[0] = s.KVF[at, 0:128].astype(f32).T
        s.SHARED[1] = s.KVF[at, 128:256].astype(f32).T
        heads = s.KVF[at, 256:384].astype(f32).T
        for i in range(pairs):
            for kind in range(2):
                first = kind * y.heads * KR + 4 * i
                s.HT[i, 4 * kind : 4 * kind + 4, :] = heads[first : first + 4]

        def expand(i, _):
            for kind, ref in enumerate((s.KP, s.VP)):
                one, two = s.SHARED[kind, :DH, :], s.SHARED[kind, DH:, :]
                for half in range(2):
                    row = 4 * kind + 2 * half
                    joined = s.HT[i, row : row + 1, :] * one + s.HT[i, row + 1 : row + 2, :] * two
                    ref[i, half * DH : (half + 1) * DH, :] = (joined * 0.5).astype(bf16)
            return 0

        lax.fori_loop(0, pairs, expand, 0)

    def pair_bias():
        bias = s.BIAS[...]
        return jnp.concatenate([bias, bias], axis=0)

    def forward_pair(i):
        scores = dot_nn(stack_pair(s.QP[i]), s.KP[i]) + pair_bias()
        top = jnp.max(scores, axis=1, keepdims=True)
        if y.NB > 1:
            old_top = s.LSE[i][:, :1]
            top = jnp.maximum(top, old_top)
        weights = jnp.exp(scores - top)
        total = jnp.sum(weights, axis=1, keepdims=True)
        rows_out = dot_nt(weights.astype(bf16), s.VP[i])
        if y.NB > 1:
            factor = jnp.exp(old_top - top)
            total = total + s.RUN[i][:, :1] * factor
            s.LSE[i] = jnp.broadcast_to(top, (2 * T, LANES))
            s.RUN[i] = jnp.broadcast_to(total, (2 * T, LANES))
            keep = stack_pair(s.ATT[i]) * factor
            s.ATT[i] = unstack_pair(rows_out + keep)
        return top, total, rows_out

    def store_mixture(i, attended, top, total):
        s.ATT[i] = attended
        s.LSE[i] = jnp.broadcast_to(top + jnp.log(total), (2 * T, LANES))
        s.MIX[own_rows, pl.ds(pl.multiple_of(i * LANES, LANES), LANES)] = attended.astype(bf16)

    def forward_step(i, _):
        top, total, rows_out = forward_pair(i)
        store_mixture(i, unstack_pair(rows_out / total), top, total)
        return 0

    @op("at_x")
    def _():
        g_kv.landed_all()
        if y.NB == 1:
            expand_block(0)
            return
        s.LSE[...] = jnp.full(s.LSE.shape, masked_score, f32)
        s.RUN[...] = jnp.zeros(s.RUN.shape, f32)
        s.ATT[...] = jnp.zeros(s.ATT.shape, f32)

        def forward_block(block, _):
            mask_block(block)
            expand_block(block)

            def step(i, _):
                forward_pair(i)
                return 0

            lax.fori_loop(0, pairs, step, 0)
            return 0

        lax.fori_loop(0, y.NB, forward_block, 0)

        def finish_step(i, _):
            total = s.RUN[i][:, :1]
            store_mixture(i, unstack_pair(stack_pair(s.ATT[i]) / total), s.LSE[i][:, :1], total)
            return 0

        lax.fori_loop(0, pairs, finish_step, 0)

    def forward_chunk(chunk):
        per = pairs // h_mix.chunks
        if y.NB == 1:
            lax.fori_loop(chunk * per, (chunk + 1) * per, forward_step, 0)
        h_mix.start(chunk)

    for i in range(h_mix.chunks):
        ops[f"at{i}"] = lambda i=i: forward_chunk(i)
        ops[f"mix.f{i}"] = lambda i=i: h_mix.forward(i)

    @op("middle")
    def _():
        h_mix.landed_all()
        f_pt.landed()
        def middle_rows(block, _):
            at = pl.ds(pl.multiple_of(block * 2 * T, 2 * T), 2 * T)
            values = tok[at, :].astype(f32)
            for p in range(N):
                values = values + dot_nt(s.MIX[at, p * 256 : (p + 1) * 256], s.PT[p])
            scale = row_scale(values)
            s.MID[at, :] = values
            s.R2[at, :] = jnp.broadcast_to(scale, (2 * T, LANES))
            s.NM[at, :] = (values * scale * s.GAIN[1:2, :]).astype(bf16)
            return 0

        lax.fori_loop(0, 2, middle_rows, 0)

    def gates(gate, up, pushed):
        chance = 1.0 / (1.0 + jnp.exp(-gate))
        silu = gate * chance
        back = pushed * up * chance * (1.0 + gate * (1.0 - chance))
        return silu * up, back, pushed * silu

    tail_low = lane_iota(2 * T) < DH

    def dense_rows(chunk, far):
        base, wide, unit, units = chunks[chunk]
        first = sum(part[1] for part in chunks[:chunk])
        block = (1 - xo) if far else xo
        at = pl.ds(pl.multiple_of(block * 2 * T, 2 * T), 2 * T)
        both = dot_nn(s.NM[at, :], s.FW[:, base : base + wide])
        back = dot_nn(cot[at, :], s.FW[:, base + wide : base + wide + units])
        width = 256 if chunk < last else LANES
        hidden, gate_back, up_back = gates(
            both[:, :width], both[:, width : 2 * width], back[:, :width]
        )
        s.HID[at, unit : unit + width] = hidden.astype(bf16)
        s.GG[at, first : first + width] = gate_back.astype(bf16)
        s.GG[at, first + width : first + 2 * width] = up_back.astype(bf16)
        if chunk == last:
            tail = both[:, 2 * width :]
            hidden, gate_back, up_back = gates(tail, pltpu.roll(tail, DH, 1), back[:, width:])
            s.HID[at, unit + width :] = jnp.where(tail_low, hidden, 0.0).astype(bf16)
            up_back = pltpu.roll(up_back, DH, 1)
            s.GG[at, first + 2 * width :] = jnp.where(tail_low, gate_back, up_back).astype(bf16)
        mid = dot_nt(s.GG[at, first : first + wide], s.FW[:, base : base + wide])
        out = dot_nt(s.HID[at, unit : unit + units], s.FW[:, base + wide : base + wide + units])
        if chunk:
            mid = mid + s.MB[at, :].astype(f32)
            out = out + s.OP[at, :].astype(f32)
        s.MB[at, :] = mid.astype(bf16)
        s.OP[at, :] = out.astype(bf16)

    def grad_blocks(parts, exchange):
        per = A // 4
        for j in range(4):
            block = z_order[j] if A == 4 else j
            at = pl.ds(pl.multiple_of(block * 256, 256), 256)
            for target, to, left, right, lanes in parts:
                value = dot_tn(left[:, at], right[:, lanes]).astype(bf16)
                target[at, to : to + value.shape[1]] = value
            if not exchange.z_first:
                for q in range(per):
                    exchange.start(block * per + q)

    def dense_grads(chunk):
        base, wide, unit, units = chunks[chunk]
        first = sum(part[1] for part in chunks[:chunk])
        g_fw[chunk].sent()
        grad_blocks(
            [
                (s.FW, base, s.NM, s.GG, slice(first, first + wide)),
                (s.FW, base + wide, cot, s.HID, slice(unit, unit + units)),
            ],
            w_fw[chunk],
        )


    def dense_chunk(chunk):
        g_fw[chunk].landed_all()
        dense_rows(chunk, True)
        dense_rows(chunk, False)

    for i, name in enumerate("abc"):
        ops["ff_" + name] = lambda i=i: dense_chunk(i)
        ops["g_" + name] = lambda i=i: dense_grads(i)

    def last_dense(far):
        if far:
            g_fw[last].landed_all()
        dense_rows(last, far)
        n_mb.start(far)

    ops["ffCf"] = lambda: last_dense(True)
    ops["ffCn"] = lambda: last_dense(False)
    ops["mb.pass"] = n_mb.pass_on

    @op("op.start")
    def _():
        n_op.start(True)
        n_op.start(False)

    ops["op.pass"] = n_op.pass_on

    @op("mid")
    def _():
        mid_back = n_mb.result()
        mid_own = s.MID[own_rows, :]
        r2_own = s.R2[own_rows, :][:, :1]
        scaled = mid_back * s.GAIN[1:2, :]
        s.GS[1:2, :] = jnp.sum(mid_back * mid_own * r2_own, axis=0, keepdims=True)
        middle_gradient = (
            cot[own_rows, :].astype(f32)
            + r2_own * scaled
            - mid_own * (r2_own * r2_own * r2_own) * jnp.mean(scaled * mid_own, axis=-1, keepdims=True)
        )
        s.MG[...] = middle_gradient
        branch = middle_gradient.astype(bf16)
        s.BG[own_rows, :] = branch
        h_bg.start(0)
        for p in range(N):
            part = dot_nn(branch, s.PT[p]).astype(bf16)
            s.DO[2 * p] = part[:, :LANES]
            s.DO[2 * p + 1] = part[:, LANES:]

    def backward_part(block, part):
        if part == 0:
            s.DST[...] = jnp.zeros(s.DST.shape, f32)

        def step(i, _):
            query, pushed = s.QP[i], s.DO[i]
            query2, pushed2 = stack_pair(query), stack_pair(pushed)
            product = pushed.astype(f32) * s.ATT[i]
            delta = jnp.sum(stack_pair(product), axis=1, keepdims=True)
            scores = dot_nn(query2, s.KP[i]) + pair_bias()
            chance = jnp.exp(scores - jnp.concatenate([s.LSE[i]] * (KB // LANES), axis=1))
            gradient = (chance * (dot_nn(pushed2, s.VP[i]) - delta)).astype(bf16)
            s.QB[i] = s.QB[i] + unstack_pair(dot_nt(gradient, s.KP[i])) * DH**-0.5
            key_back = dot_tn(query2, gradient)
            value_back = dot_tn(pushed2, chance.astype(bf16))
            for kind, back in enumerate((key_back, value_back)):
                for r in range(KR):
                    shared = slice(r * DH, (r + 1) * DH)
                    found = s.DST[kind, shared, :]
                    for half in range(2):
                        mine = back[half * DH : (half + 1) * DH]
                        row = 4 * kind + 2 * half + r
                        found = found + s.HT[i, row : row + 1, :] * mine
                        s.DHT[i, row : row + 1, :] = jnp.sum(
                            mine * s.SHARED[kind, shared, :], axis=0, keepdims=True
                        )
                    s.DST[kind, shared, :] = found
            return 0

        quarter = pairs // 4
        lax.fori_loop(part * quarter, (part + 1) * quarter, step, 0)
        if part < 3:
            return
        at = pl.ds(pl.multiple_of(block * KB, KB), KB)
        for kind in range(2):
            s.KVF[at, kind * 128 : kind * 128 + 128] = (s.DST[kind] * 0.5).T.astype(bf16)
        heads = [s.DHT[i, 4 * kind : 4 * kind + 4, :] for kind in range(2) for i in range(pairs)]
        heads.append(jnp.zeros((LANES - 8 * pairs, KB), f32))
        s.KVF[at, 256:384] = (jnp.concatenate(heads, axis=0) * 0.5).T.astype(bf16)

    def backward_quarter(part):
        if part == 0:
            s.QB[...] = jnp.zeros(s.QB.shape, f32)
            g_kv.sent()
        if y.NB == 1:
            backward_part(0, part)
        elif part == 0:

            def backward_step(block, _):
                mask_block(block)
                expand_block(block)
                for each in range(4):
                    backward_part(block, each)
                return 0

            lax.fori_loop(0, y.NB, backward_step, 0)

    for i in range(4):
        ops[f"bq{i}"] = lambda i=i: backward_quarter(i)

    @op("kvst")
    def _():
        for z in z_order:
            w_kv.start(z)

    ops["bg.f"] = h_bg.forward_all

    @op("pt.g")
    def _():
        h_bg.landed_all()
        mine = pl.ds(pl.multiple_of(n * 256, 256), 256)
        grad_blocks([(s.PPT, 0, s.BG, s.MIX, mine)], w_pt)

    @op("qb")
    def _():
        query_back = jnp.concatenate([s.QB[i] for i in range(pairs)], axis=1)
        heads_back = jnp.zeros((T, LANES), f32)
        shared_back = []
        for r in range(QR):
            turned = s.QROT[r]
            product = (query_back * jnp.concatenate([turned] * pairs, axis=1)).astype(bf16)
            heads_back = heads_back + dot_nt(product, s.EQ[r])
            product = spread_heads(r) * query_back
            total = product[:, :LANES]
            for i in range(1, pairs):
                total = total + product[:, i * LANES : (i + 1) * LANES]
            shared_back.append(fold_halves(total))
        low = lane_iota(T) < DH
        held.shared_tiles = [
            rotated(jnp.where(low, shared_back[2 * t], shared_back[2 * t + 1]), back=True) * (1.0 / QR)
            for t in range(QR // 2)
        ]
        held.heads_back = heads_back * (1.0 / QR)

    @op("op.res")
    def _():
        o_out[own_rows, :] = (s.MID[own_rows, :] + n_op.result()).astype(bf16)
        h_og.start(0)

    ops["og.f"] = h_og.forward_all

    @op("og.l")
    def _():
        h_og.landed_all()
        write(o_out, r_out)

    ops["tg.f"] = h_tg.forward_all

    @op("tg.l")
    def _():
        h_tg.landed_all()
        write(o_tok, r_tok)

    @op("qg")
    def _():
        key_shared = rotated(s.DKVO[:, 0:128], back=True)
        value_shared = s.DKVO[:, 128:256]
        head_tile = s.DKVO[:, 256:384]
        for p in range(N):
            s.QGS[p, :, :LANES] = place_lanes(
                canonical_pieces(held.shared_tiles, LANES, p * y.SQ, y.SQ, 0, 0)
            ).astype(bf16)
            s.QGS[p, :, LANES:] = place_lanes(
                [
                    (key_shared, p * y.SK, y.oK, y.SK),
                    (value_shared, p * y.SK, y.oV, y.SK),
                    (held.heads_back, p * y.HQ, y.oq, y.HQ),
                    (head_tile, p * y.HK, y.ok, y.HK),
                    (head_tile, (N + p) * y.HK, y.ov, y.HK),
                ]
            ).astype(bf16)
        for k, peer in enumerate(narrow_peers):
            send(s.QGS.at[peer[1]], s.QGR.at[n], k_a2a + k, peer)
        s.QGR[n] = s.QGS[n]

    @op("fb")
    def _():
        first_back = jnp.zeros((T, D), f32)
        for p in range(N):
            first_back = first_back + dot_nt(s.QGS[p], s.WQ[p])
        x_own = tok[own_rows, :].astype(f32)
        r1_own = row_scale(x_own)
        s.GS[0:1, :] = jnp.sum(first_back * x_own * r1_own, axis=0, keepdims=True)
        for k, peer in enumerate(narrow_peers):
            send(s.GS, s.GR.at[k], k_gain + k, peer)
        scaled = first_back * s.GAIN[0:1, :]
        tokens_gradient = (
            s.MG[...]
            + r1_own * scaled
            - x_own * (r1_own * r1_own * r1_own) * jnp.mean(scaled * x_own, axis=-1, keepdims=True)
        )
        o_tok[own_rows, :] = tokens_gradient.astype(bf16)
        for chunk in range(h_tg.chunks):
            h_tg.start(chunk)

    @op("q.g")
    def _():
        for k, peer in enumerate(narrow_peers):
            arrive(s.QGR.at[peer[1]], k_a2a + k)
        for k in range(3):
            arrive(s.GR.at[k], k_gain + k)
        gain_rows = s.GS[...]
        for k in range(3):
            gain_rows = gain_rows + s.GR[k]
        lane_row = row_iota(LANES, D)
        spread = jnp.where(
            lane_row == y.og,
            gain_rows[0:1],
            jnp.where(lane_row == y.og + 1, gain_rows[1:2], 0.0),
        )
        gain_columns = spread.T
        for j in range(4):
            block = z_order[j] if A == 4 else j
            lanes = pl.ds(pl.multiple_of(block * 256, 256), 256)
            value = jnp.zeros((256, 256), f32)
            for p in range(N):
                value = value + dot_tn(s.NORM[p * T : (p + 1) * T, lanes], s.QGR[p])
            s.PQ[pl.ds(pl.multiple_of(block * 256, 256), 256), :] = value.astype(bf16)
        s.PQ[:, LANES:] = (s.PQ[:, LANES:].astype(f32) + gain_columns).astype(bf16)
        for z in z_order:
            w_q.start(z)

    for name in schedule:
        ops[name]()

    for exchange in (g_wq, g_pt, f_wq, f_pt, *w_fw):
        exchange.sent()
    for exchange in (w_kv, w_pt, w_q):
        exchange.sent_direct()
    for copy in pending:
        copy.wait_send()
    for copy in written:
        copy.wait()


def results_kernel(y, out, tok, fw, pt, q, *outs):
    o_out, o_tok, o_pre, o_qh, o_qs, o_kh, o_ks, o_vh, o_vs, o_pt, o_mid, o_gate, o_up, o_down = outs
    FM, F, half = y.FM, y.F, y.F - y.FM
    o_out[...] = out[...]
    o_tok[...] = tok[...].astype(f32)
    o_qs[...] = q[:, :LANES].T[: y.SQ]
    second = q[:, LANES:].T
    o_ks[...] = second[y.oK : y.oK + y.SK]
    o_vs[...] = second[y.oV : y.oV + y.SK]
    o_qh[...] = second[y.oq : y.oq + y.HQ]
    o_kh[...] = second[y.ok : y.ok + y.HK]
    o_vh[...] = second[y.ov : y.ov + y.HK]
    o_pre[...] = second[y.og : y.og + 1]
    o_mid[...] = second[y.og + 1 : y.og + 2]
    for first in range(0, 256, LANES):
        o_pt[first : first + LANES, :] = pt[:, first : first + LANES].T
    *whole_chunks, (base, wide, unit, _) = y.chunks
    for at, _, start, _ in whole_chunks:
        for part, target in enumerate((o_gate, o_up, o_down)):
            for first in range(0, 256, LANES):
                place = at + part * 256 + first
                target[start + first : start + first + LANES, :] = fw[:, place : place + LANES].T
    o_gate[unit:FM, :] = fw[:, base : base + LANES].T
    o_up[unit:FM, :] = fw[:, base + LANES : base + 2 * LANES].T
    tail = fw[:, base + 2 * LANES : base + wide].T
    o_gate[FM:, :] = tail[:half]
    o_up[FM:, :] = tail[half:]
    o_down[unit:FM, :] = fw[:, base + wide : base + wide + LANES].T
    o_down[FM:, :] = fw[:, base + wide + LANES :].T[:half]


def solution(mesh):
    W, N = mesh.shape["wide"], mesh.shape["narrow"]

    def on_device(
        tokens,
        documents,
        prenorm,
        qheads,
        qshared,
        kheads,
        kshared,
        vheads,
        vshared,
        project,
        midnorm,
        gating,
        upward,
        downward,
        cotangent,
    ):
        R, T, D = tokens.shape
        L = documents.shape[1]
        RW, F = gating.shape
        y = make_layout(W, N, T, D, F, L, N * kheads.shape[1] // KR)
        assert R == N
        scratch = scratch_list(y)
        line, direct = y.A + 2, 2 * y.A + 1
        arrivals = 18 * y.A + 36 + 3 * direct
        arrivals += sum(line if i in z_first_chunks else direct for i in range(3))
        sends = arrivals + 12 * y.A
        vmem = pl.BlockSpec(memory_space=pltpu.VMEM)

        def kernel(*refs):
            block_kernel(y, tuple(scratch), *refs)

        shape = jax.ShapeDtypeStruct
        raw = pl.pallas_call(
            kernel,
            out_shape=(
                shape((y.M, D), bf16),
                shape((y.M, D), bf16),
                shape((RW, y.FW), f32),
                shape((RW, 256), f32),
                shape((RW, 256), f32),
            ),
            in_specs=[vmem] * 15,
            out_specs=[pl.BlockSpec(memory_space=pl.ANY)] * 5,
            scratch_shapes=[*scratch.values()]
            + [pltpu.SemaphoreType.DMA((count,)) for count in (sends, arrivals, 7)],
            compiler_params=pltpu.CompilerParams(
                collective_id=0, has_side_effects=True, vmem_limit_bytes=63 * 2**20
            ),
            name="block",
        )(
            tokens.reshape(y.M, D),
            documents,
            prenorm.reshape(1, RW),
            qheads.T,
            qshared.T,
            kheads.T,
            kshared.T,
            vheads.T,
            vshared.T,
            project,
            midnorm.reshape(1, RW),
            gating.T,
            upward.T,
            downward,
            cotangent.reshape(y.M, D),
        )

        def results(*refs):
            results_kernel(y, *refs)

        outputs = pl.pallas_call(
            results,
            out_shape=(
                shape((y.M, D), bf16),
                shape((y.M, D), f32),
                shape((1, RW), f32),
                shape((y.HQ, RW), f32),
                shape((y.SQ, RW), f32),
                shape((y.HK, RW), f32),
                shape((y.SK, RW), f32),
                shape((y.HK, RW), f32),
                shape((y.SK, RW), f32),
                shape((256, RW), f32),
                shape((1, RW), f32),
                shape((F, RW), f32),
                shape((F, RW), f32),
                shape((F, RW), f32),
            ),
            in_specs=[vmem] * 5,
            out_specs=[vmem] * 14,
            compiler_params=pltpu.CompilerParams(vmem_limit_bytes=63 * 2**20),
            name="results",
        )(*raw)
        turned = (3, 4, 5, 6, 7, 8, 11, 12)
        outputs = [v.T if i in turned else v for i, v in enumerate(outputs)]
        outputs[0] = outputs[0].reshape(R, T, D)
        outputs[1] = outputs[1].reshape(R, T, D)
        outputs[2] = outputs[2].reshape(RW)
        outputs[10] = outputs[10].reshape(RW)
        return tuple(outputs)

    split = P("wide", "narrow")
    flipped = P("narrow", "wide")
    whole = P(None, "wide", None)
    gain = P("wide")
    return jax.shard_map(
        on_device,
        mesh=mesh,
        in_specs=(
            whole,
            P(),
            gain,
            split,
            split,
            split,
            split,
            split,
            split,
            flipped,
            gain,
            split,
            split,
            flipped,
            whole,
        ),
        out_specs=(
            whole,
            whole,
            gain,
            split,
            split,
            split,
            split,
            split,
            split,
            flipped,
            gain,
            split,
            split,
            flipped,
        ),
        check_vma=False,
    )
```

```python
import math
from types import SimpleNamespace

import jax
import jax.numpy as jnp
from jax import lax
from jax.experimental import pallas as pl
from jax.experimental.pallas import tpu as pltpu
from jax.sharding import PartitionSpec as P

DH = 64
QR = 6
KR = 2
VR = 2
LANES = 128

epsilon = 1e-06
masked_score = -1e30
MESH = pl.DeviceIdType.MESH
y_first_chunks = (1,)
z_first_chunks = (0,)
chunk_order = (0, 2, 1)
y_first_gathers = ()
z_first_sums = ()
direct_sums = ("wkv", "wqa", "wqb")
f32 = jnp.float32
bf16 = jnp.bfloat16


def dot_nn(a, b):
    return lax.dot_general(a, b, (((1,), (0,)), ((), ())), preferred_element_type=f32)


def dot_nt(a, b):
    return lax.dot_general(a, b, (((1,), (1,)), ((), ())), preferred_element_type=f32)


def dot_tn(a, b):
    return lax.dot_general(a, b, (((0,), (0,)), ((), ())), preferred_element_type=f32)


def lane_iota(rows, cols=LANES):
    return lax.broadcasted_iota(jnp.int32, (rows, cols), 1)


def row_iota(rows, cols=LANES):
    return lax.broadcasted_iota(jnp.int32, (rows, cols), 0)


def place_lanes(pieces):
    rows = pieces[0][0].shape[0]
    lane = lane_iota(rows)
    result = jnp.zeros((rows, LANES), f32)
    for tile, start, to, count in pieces:
        shift = (to - start) % LANES
        moved = pltpu.roll(tile, shift, 1) if shift else tile
        result = jnp.where((lane >= to) & (lane < to + count), moved, result)
    return result


def canonical_pieces(tiles, width, first, count, start, to):
    pieces = []
    while count:
        part, inside = divmod(first, width)
        take = min(count, width - inside)
        pieces.append((tiles[part], start + inside, to, take))
        first, to, count = first + take, to + take, count - take
    return pieces


def swap_quarters(tile):
    low = lane_iota(tile.shape[0]) % DH < DH // 2
    return jnp.where(low, pltpu.roll(tile, LANES - DH // 2, 1), pltpu.roll(tile, DH // 2, 1))


def stack_pair(tile):
    low = lane_iota(tile.shape[0]) < DH
    zero = jnp.zeros_like(tile)
    return jnp.concatenate([jnp.where(low, tile, zero), jnp.where(low, zero, tile)], axis=0)


def unstack_pair(rows):
    half = rows.shape[0] // 2
    low = lane_iota(half) < DH
    return jnp.where(low, rows[:half], rows[half:])


def pack_heads(tile):
    quarter = tile.shape[0] // 4
    low = lane_iota(quarter) < DH
    parts = [tile[i * quarter : (i + 1) * quarter] for i in range(4)]
    pairs = [
        jnp.where(low, parts[i], pltpu.roll(parts[i + 1], DH, 1)) for i in (0, 2)
    ]
    return jnp.concatenate(pairs, axis=1)


def unpack_heads(rows):
    tiles = (rows[:, :LANES], rows[:, LANES:])
    parts = [part for tile in tiles for part in (tile, pltpu.roll(tile, DH, 1))]
    return jnp.concatenate(parts, axis=0)


def fold_halves(tile):
    return tile + pltpu.roll(tile, DH, 1)


def row_scale(values):
    return lax.rsqrt(jnp.mean(values * values, axis=-1, keepdims=True) + epsilon)


def make_layout(W, N, T, D, F, L, heads):
    lay = SimpleNamespace()
    lay.W, lay.N, lay.T, lay.D, lay.F, lay.L, lay.heads = W, N, T, D, F, L, heads
    lay.A = W // 2
    lay.RW = D // W
    lay.M = N * T
    lay.KT = T + T // 4
    lay.FM = F // LANES * LANES
    lay.FP = lay.FM + LANES
    full = lay.FM // 256
    lay.chunks = [(768 * i, 512, 256 * i, 256) for i in range(full)]
    lay.chunks.append((768 * full, 3 * LANES, 256 * full, 256))
    lay.FW = 768 * full + 5 * LANES
    assert lay.FM % 256 == LANES
    lay.pairs = heads // 2
    assert len(lay.chunks) == 3
    lay.KB = L if L <= 1024 else 512
    lay.NB = L // lay.KB
    lay.SQ = QR * DH // N
    lay.SK = KR * DH // N
    lay.HQ = heads * QR // N
    lay.HK = heads * KR // N
    lay.oK, lay.oV = 0, lay.SK
    lay.oq = 2 * lay.SK
    lay.ok = lay.oq + lay.HQ
    lay.ov = lay.ok + lay.HK
    lay.og = lay.ov + lay.HK
    assert N == 4 and W % 8 == 0 and T == LANES and D == heads * DH == 1024
    assert F % LANES == DH and lay.SQ <= LANES and lay.og + 2 <= LANES
    return lay


def scratch_list(y):
    W, N, T, D, L, A, RW, M = y.W, y.N, y.T, y.D, y.L, y.A, y.RW, y.M
    vm = lambda *shape, kind=bf16: pltpu.VMEM(shape, kind)
    GUc = 2 * y.FM + LANES
    return dict(
        PIN=vm(256, RW),
        GIN=vm(y.F, RW),
        UIN=vm(y.F, RW),
        DIN=vm(y.F, RW),
        XIN=vm(M, D),
        CIN=vm(M, D),
        WQ=vm(N, D, 256),
        PT=vm(N, D, 256),
        FW=vm(D, y.FW),
        KVF=vm(L // T * y.KT, 256),
        KP=vm(y.pairs, LANES, y.KB),
        VP=vm(y.pairs, LANES, y.KB),
        EQ=vm(QR, LANES, D),
        SHARED=vm(2, LANES, y.KB, kind=f32),
        HT=vm(y.pairs, 8, y.KB, kind=f32),
        DHT=vm(y.pairs, 8, y.KB, kind=f32),
        BIAS=vm(T, y.KB, kind=f32),
        DOC=vm(T, LANES, kind=f32),
        ROPE=vm(2, T, LANES, kind=f32),
        GAIN=vm(8, D, kind=f32),
        QROT=vm(QR, T, LANES, kind=f32),
        QH=vm(T, 256),
        QP=vm(y.pairs, T, LANES),
        ATT=vm(y.pairs, T, LANES, kind=f32),
        LSE=vm(y.pairs, 2 * T, LANES, kind=f32),
        RUN=vm(y.pairs if y.NB > 1 else 1, 2 * T, LANES, kind=f32),
        MIX=vm(M, D),
        NORM=vm(M, D),
        MID=vm(M, D, kind=f32),
        NM=vm(M, D),
        R2=vm(M, LANES, kind=f32),
        HID=vm(M, y.FP),
        GG=vm(M, GUc),
        MB=vm(M, D),
        MBC=vm(2, T, D),
        MBX=vm(T, D),
        MBS=vm(T, D),
        OP=vm(M, D),
        OPC=vm(2, T, D),
        OPX=vm(T, D),
        OPS=vm(T, D),
        BG=vm(M, D),
        MG=vm(T, D, kind=f32),
        DO=vm(y.pairs, T, LANES),
        QB=vm(y.pairs, T, LANES, kind=f32),
        DST=vm(2, LANES, y.KB, kind=f32),
        DKVY=vm(A * y.KT, 256),
        DKVR=vm((A + 1) * y.KT * (1 + ("wkv" in z_first_sums)), 256),
        DKVO=vm(y.KT, 256, kind=f32),
        QGS=vm(N, T, 256),
        QGR=vm(N, T, 256),
        OUT=vm(M, D),
        TOK=vm(M, D),
        TFW=vm(RW, y.FW, kind=f32),
        TPT=vm(RW, 256, kind=f32),
        TQ=vm(RW, 256, kind=f32),
        GS=vm(8, D, kind=f32),
        GR=vm(3, 8, D, kind=f32),
        YFW=vm(A * RW, y.FW),
        **{
            f"RF{i}": vm((A + 1) * RW * (2 if i in z_first_chunks else 1), wide + units)
            for i, (_, wide, _, units) in enumerate(y.chunks)
        },
        PPT=vm(D, 256),
        YPT=vm(A * RW, 256),
        RPT=vm((A + 1) * RW * (1 + ("wpt" in z_first_sums)), 256),
        PQ=vm(D, 256),
        YQ=vm(A * RW, 256),
        RQ0=vm((A + 1) * RW, LANES),
        RQ1=vm((A + 1) * RW, LANES),
    )


schedule = (
    "prep_wq", "wq.L", "prep_pt", "pt.L", "wq.Ly", "wq.h1", "fwq.s0", "prep_fw", "pt.h1", "wq.h2",
    "a.L", "fwq.s1", "b.L", "pt.Ly", "wq.h3", "fwq.f0", "c.Ly", "fwq.s2", "fwq.s3", "fwq.f1",
    "a.h1", "consts", "b.Ly", "a.Ly", "fwq.f2", "fwq.f3", "pt.h2", "project", "kv.L", "b.h1",
    "fpt.s0", "fpt.s1", "kv.h1", "pt.h3", "kv.Ly", "kv.h2", "kv.h3", "a.h2", "fpt.s2", "b.h2",
    "c.L", "a.y1", "a.y2", "fpt.f0", "queries", "fpt.s3", "at_x", "a.h3", "at0", "at1", "a.y3",
    "at2", "mix.f0", "at3", "b.y1", "fpt.f1", "b.y2", "mix.f1", "mix.f2", "b.h3", "fpt.f2",
    "fpt.f3", "mix.f3", "c.h1", "b.y3", "middle", "ff_a", "g_a", "wa.ends", "c.h2", "ff_b", "g_b",
    "c.h3", "ffCf", "ffCn", "mb.pass", "wa.s1", "g_c", "wa.s2", "wb.s0", "mid", "bq0", "bq1",
    "wc.s0", "bq2", "op.start", "bq3", "op.pass", "bg.f", "wb.s1", "wc.s1", "kvst", "qb", "qg1",
    "fb1", "op.res", "wkv.d0", "q.g1", "wkv.d1", "pt.g", "wkv.d2", "wb.s2", "wqa.d0", "wkv.fin",
    "qg", "fb", "wpt.s0", "wa.fin", "wqa.d1", "wpt.s1", "wb.fin", "wqa.d2", "wc.s2", "wpt.s2",
    "q.g", "og.f", "wqb.d0", "wqa.fin", "wc.fin", "wqb.d1", "og.l", "wqb.d2", "wpt.fin", "tg.f",
    "tg.l", "wa.finy", "wqb.fin",
)


def block_kernel(y, names, *refs):
    docs, prenorm, qheads, qshared, kheads, kshared, vheads, vshared, midnorm = refs[:9]
    sources = refs[9:15]
    r_out, r_tok, r_fw, r_pt, r_q = refs[15:20]
    s = SimpleNamespace(**dict(zip(names, refs[20:])))
    ssem, rsem, wsem, lsem = refs[20 + len(names) :]
    o_out, o_tok, o_fw, o_pt, o_q = s.OUT, s.TOK, s.TFW, s.TPT, s.TQ
    written = []

    def write(src, dst):
        copy = pltpu.make_async_copy(src, dst, wsem.at[len(written)])
        copy.start()
        written.append(copy)

    project, gating, upward, downward, tok, cot = s.PIN, s.GIN, s.UIN, s.DIN, s.XIN, s.CIN
    loads = []
    for source, target in zip(sources, (project, gating, upward, downward, tok, cot)):
        loads.append(pltpu.make_async_copy(source, target, lsem.at[len(loads)]))
        loads[-1].start()

    W, N, T, D, F, L, A, RW, M = y.W, y.N, y.T, y.D, y.F, y.L, y.A, y.RW, y.M
    FM, FP, KB, pairs = y.FM, y.FP, y.KB, y.pairs
    w = lax.axis_index("wide")
    n = lax.axis_index("narrow")
    zi, yi = w // 2, w % 2
    xo, co = n // 2, n % 2
    y_peer = (zi * 2 + 1 - yi, n)
    c_peer = (w, xo * 2 + 1 - co)
    x_peer = (w, (1 - xo) * 2 + co)
    d_peer = (w, (1 - xo) * 2 + 1 - co)
    narrow_peers = (c_peer, x_peer, d_peer)
    taken = [0, 0]

    def take(count=1):
        taken[0] += count
        return taken[0] - count

    def take_send(count=1):
        taken[1] += count
        return taken[1] - count

    def remote(src, dst, k, peer, send_k):
        return pltpu.make_async_remote_copy(
            src_ref=src,
            dst_ref=dst,
            send_sem=ssem.at[send_k],
            recv_sem=rsem.at[k],
            device_id=peer,
            device_id_type=MESH,
        )

    def all_sent(ref, send_k):
        remote(ref, ref, 0, y_peer, send_k).wait_send()

    pending = []

    def send(src, dst, k, peer):
        copy = remote(src, dst, k, peer, take_send())
        copy.start()
        pending.append(copy)

    def arrive(dst, k):
        remote(dst, dst, k, y_peer, 0).wait_recv()

    def rows(ref, first, count, lanes=None):
        at = pl.ds(pl.multiple_of(first, 16), count)
        return ref.at[at] if lanes is None else ref.at[at, pl.ds(*lanes)]

    def each_at(distance, act):
        if distance == 0:
            act(zi, None)
            return
        pl.when(zi >= distance)(lambda: act(zi - distance, True))
        pl.when(zi + distance < A)(lambda: act(zi + distance, False))

    right_peer = ((zi + 1) * 2 + yi, n)
    left_peer = ((zi - 1) * 2 + yi, n)

    barrier = pltpu.get_barrier_semaphore()
    z_peers = [(((zi + step) % A) * 2 + yi, n) for step in range(1, A)]
    peers = [y_peer, *narrow_peers, *z_peers]
    for peer in peers:
        pl.semaphore_signal(barrier, inc=1, device_id=peer, device_id_type=MESH)
    pl.semaphore_wait(barrier, len(peers))

    class Gather:
        def __init__(self, ref, count, lanes=None, y_first=False):
            self.ref, self.count, self.lanes, self.y_first = ref, count, lanes, y_first
            self.kz, self.ky = take(A), take(A)
            self.sy, self.sr = take_send(), take_send()
            self.sl = take_send() if y_first else self.sr
            self.next = self.next_y = 1

        def part(self, wide):
            return rows(self.ref, wide * self.count, self.count, self.lanes)

        def block(self, z):
            if self.y_first:
                return rows(self.ref, z * 2 * self.count, 2 * self.count, self.lanes)
            return self.part(z * 2 + yi)

        def along(self, z, to_right):
            block = self.block(z)
            if to_right:
                return remote(block, block, self.kz + z, right_peer, self.sr)
            return remote(block, block, self.kz + z, left_peer, self.sl)

        def across(self, z):
            part = self.part(z * 2 + yi)
            return remote(part, part, self.ky + z, y_peer, self.sy)

        def landed(self, z):
            arrive(self.part(z * 2 + 1 - yi), self.ky + z)

        def launch_y(self):
            self.across(zi).start()

        def launch(self):
            if self.y_first:
                self.landed(zi)
            pl.when(zi < A - 1)(lambda: self.along(zi, True).start())
            pl.when(zi > 0)(lambda: self.along(zi, False).start())

        def hop(self, distance, across):
            def act(z, to_right):
                arrive(self.block(z), self.kz + z)
                more = zi < A - 1 if to_right else zi > 0
                pl.when(more)(lambda: self.along(z, to_right).start())
                if across and not self.y_first:
                    self.across(z).start()

            each_at(distance, act)

        def pump(self, count=A, across=True):
            for _ in range(min(count, A - self.next)):
                self.hop(self.next, across)
                self.next += 1

        def pump_y(self, count=A):
            for _ in range(min(count, self.next - self.next_y)):
                each_at(self.next_y, lambda z, _: self.across(z).start())
                self.next_y += 1

        def landed_all(self):
            if not self.y_first:
                for z in range(A):
                    self.landed(z)

        def sent(self):
            def blocks(count):
                return rows(self.ref, 0, count * self.count, self.lanes)

            all_sent(blocks(1 if self.y_first else A), self.sy)
            if self.y_first:
                for z in range(A - 1):
                    pl.when(zi == z)(lambda: all_sent(blocks(2 * z + 2), self.sr))
                    pl.when(zi == z + 1)(lambda: all_sent(blocks(2 * (A - z - 1)), self.sl))
                return
            inner = (zi > 0) & (zi < A - 1)
            pl.when(inner)(lambda: all_sent(blocks(A + 1), self.sr))
            pl.when(jnp.logical_not(inner))(lambda: all_sent(blocks(1), self.sr))

    class Spread:
        def __init__(self, gather, ref):
            self.gather, self.ref = gather, ref
            self.next = self.passed = 0
            self.kx, self.kc, self.kd = take(A), take(A), take(A)
            self.sx, self.sc, self.sd = take_send(), take_send(), take_send()

        def part(self, owner, z):
            return rows(self.ref.at[owner], z * 2 * RW, 2 * RW)

        def copies(self, z):
            part = self.part(n, z)
            to_x = remote(part, part, self.kx + z, x_peer, self.sx)
            return to_x, remote(part, part, self.kc + z, c_peer, self.sc)

        def onward(self, z):
            part = self.part(x_peer[1], z)
            return remote(part, part, self.kd + z, c_peer, self.sd)

        def start(self, distance):
            def act(z, _):
                if not self.gather.y_first:
                    self.gather.landed(z)
                for copy in self.copies(z):
                    copy.start()

            each_at(distance, act)

        def pump(self, count=A):
            for _ in range(min(count, A - self.next)):
                self.start(self.next)
                self.next += 1

        def pump_forward(self, count=A):
            for _ in range(min(count, A - self.passed)):
                self.forward(self.passed)
                self.passed += 1

        def forward(self, distance):
            def act(z, _):
                arrive(self.part(x_peer[1], z), self.kx + z)
                self.onward(z).start()

            each_at(distance, act)

        def landed(self):
            for z in range(A):
                arrive(self.part(c_peer[1], z), self.kc + z)
                arrive(self.part(d_peer[1], z), self.kd + z)

        def sent(self):
            for k in (self.sx, self.sc, self.sd):
                all_sent(self.ref.at[n], k)

    class Share:
        def __init__(self, ref, chunks):
            self.ref, self.chunks = ref, chunks
            self.kx, self.kc, self.kd = take(chunks), take(chunks), take(chunks)
            self.width = D // chunks

        def part(self, owner, chunk):
            lanes = pl.ds(pl.multiple_of(chunk * self.width, LANES), self.width)
            return self.ref.at[pl.ds(pl.multiple_of(owner * T, T), T), lanes]

        def start(self, chunk):
            send(self.part(n, chunk), self.part(n, chunk), self.kx + chunk, x_peer)
            send(self.part(n, chunk), self.part(n, chunk), self.kc + chunk, c_peer)

        def forward(self, chunk):
            part = self.part(x_peer[1], chunk)
            arrive(part, self.kx + chunk)
            send(part, part, self.kd + chunk, c_peer)

        def landed(self, chunk):
            arrive(self.part(c_peer[1], chunk), self.kc + chunk)
            arrive(self.part(d_peer[1], chunk), self.kd + chunk)

        def forward_all(self):
            for chunk in range(self.chunks):
                self.forward(chunk)

        def landed_all(self):
            for chunk in range(self.chunks):
                self.landed(chunk)

        def finish(self):
            self.forward_all()
            self.landed_all()

    class NarrowSum:
        def __init__(self, part_ref, core_ref, x_ref, send_ref):
            self.ref, self.core, self.x, self.out = part_ref, core_ref, x_ref, send_ref
            self.kc, self.kx = take(2), take(1)

        def part(self, owner):
            return rows(self.ref, owner * T, T)

        def start(self, far):
            owner = ((1 - xo) if far else xo) * 2 + 1 - co
            send(self.part(owner), self.core.at[int(far)], self.kc + int(far), c_peer)

        def pass_on(self):
            arrive(self.core.at[1], self.kc + 1)
            total = self.part((1 - xo) * 2 + co)[...].astype(f32) + self.core[1].astype(f32)
            self.out[...] = total.astype(bf16)
            send(self.out, self.x, self.kx, x_peer)

        def result(self):
            arrive(self.core.at[0], self.kc)
            arrive(self.x, self.kx)
            return (
                self.part(n)[...].astype(f32) + self.core[0].astype(f32) + self.x[...].astype(f32)
            )

    class WideSum:
        def __init__(self, part_ref, y_ref, z_ref, out_ref, count, lanes=None, z_first=False):
            self.ref, self.y, self.z, self.total = part_ref, y_ref, z_ref, out_ref
            self.count, self.lanes, self.z_first = count, lanes, z_first
            self.size = 2 * count if z_first else count
            self.next = 0
            self.z_lanes = lanes and (0, lanes[1])
            self.ky, self.kz = take(1 if z_first else A), take(A + 1)
            self.sy, self.sz = take_send(), take_send()

        def part(self, wide):
            return rows(self.ref, wide * self.count, self.count, self.lanes)

        def block(self, z):
            if self.z_first:
                return rows(self.ref, z * 2 * self.count, 2 * self.count, self.lanes)
            return self.part(z * 2 + yi)

        def got_y(self, z):
            return rows(self.y, z * self.count, self.count, self.lanes)

        def got_z(self, slot):
            return rows(self.z, slot * self.size, self.size, self.z_lanes)

        def across(self, z):
            return remote(self.part(z * 2 + 1 - yi), self.got_y(z), self.ky + z, y_peer, self.sy)

        def along(self, z, to_right):
            block = self.block(z)
            if to_right:
                return remote(block, self.got_z(z), self.kz + z, right_peer, self.sz)
            slot = jnp.where(z == zi - 1, A, z)
            return remote(block, self.got_z(slot), self.kz + slot, left_peer, self.sz)

        def start(self, z):
            if not self.z_first:
                self.across(z).start()

        def gather_y(self, z):
            block = self.block(z)[...].astype(f32)
            if self.z_first:
                return block
            arrive(self.got_y(z), self.ky + z)
            return block + self.got_y(z)[...].astype(f32)

        def stage(self, step):
            def move(z, to_right, joined):
                value = self.gather_y(z)
                if joined:
                    arrive(self.got_z(z), self.kz + z)
                    value = value + self.got_z(z)[...].astype(f32)
                self.block(z)[...] = value.astype(bf16)
                self.along(z, to_right).start()

            right, left = A - 1 - step + zi, step - (A - 1 - zi)
            to_right = (right < A) & (right > zi)
            to_left = (left >= 0) & (left < zi)
            pl.when(to_right & (zi > 0))(lambda: move(right, True, True))
            pl.when(to_left & (zi < A - 1))(lambda: move(left, False, True))
            if not self.z_first:
                pl.when(to_right & (zi == 0))(lambda: move(right, True, False))
                pl.when(to_left & (zi == A - 1))(lambda: move(left, False, False))

        def pump(self, count=A):
            for _ in range(min(count, A - 1 - self.next)):
                self.stage(self.next)
                self.next += 1

        def send_direct(self, count=A):
            for k in range(self.next, min(self.next + count, A - 1)):
                self.next += 1
                z = z_order[k] if A == 4 else (zi + 1 + k) % A
                block = self.block(z)
                block[...] = self.gather_y(z).astype(bf16)
                self.direct(z).start()

        def direct(self, z):
            return remote(
                self.block(z), self.got_z(zi), self.kz + zi, (z * 2 + yi, n), self.sz
            )

        def finish_direct(self):
            self.total[...] = self.gather_y(zi)
            for step in range(1, A):
                self.add((zi + step) % A)

        def start_ends(self):
            @pl.when(zi == 0)
            def _():
                for z in range(A - 1, 0, -1):
                    self.along(z, True).start()

            @pl.when(zi == A - 1)
            def _():
                for z in range(A - 1):
                    self.along(z, False).start()

        def add(self, slot):
            arrive(self.got_z(slot), self.kz + slot)
            got = self.got_z(slot)[...].astype(f32)
            if not self.z_first:
                self.total[...] += got
                return
            block = self.block(zi)
            block[...] = (block[...].astype(f32) + got).astype(bf16)

        def finish(self):
            if not self.z_first:
                self.total[...] = self.gather_y(zi)
            pl.when(zi > 0)(lambda: self.add(zi))
            pl.when(zi < A - 1)(lambda: self.add(A))
            if self.z_first:
                self.last_across().start()

        def last_across(self):
            return remote(self.part(zi * 2 + 1 - yi), self.got_y(0), self.ky, y_peer, self.sy)

        def finish_y(self):
            if self.z_first:
                arrive(self.got_y(0), self.ky)
                mine = self.part(zi * 2 + yi)[...].astype(f32)
                self.total[...] = mine + self.got_y(0)[...].astype(f32)

        def sent(self):
            def parts(count):
                return rows(self.ref, 0, count * self.count, self.lanes)

            all_sent(parts(1 if self.z_first else A), self.sy)
            all_sent(parts((A - 1) * (2 if self.z_first else 1)), self.sz)

    if A == 4:
        z_order = []
        for row in zip((3, 2, 1, 0), (3, 2, 0, 1), (0, 1, 3, 2), (0, 1, 2, 3)):
            z_order.append(sum(jnp.where(zi == at, z, 0) for at, z in enumerate(row)))
    else:
        z_order = range(A)

    chunks = y.chunks
    last = len(chunks) - 1
    cuts = [(base, wide + units) for base, wide, _, units in chunks]
    g_wq = Gather(s.WQ.at[n], RW, y_first="wq" in y_first_gathers)
    g_pt = Gather(s.PT.at[n], RW, y_first="pt" in y_first_gathers)
    g_kv = Gather(s.KVF, y.KT, y_first="kv" in y_first_gathers)
    g_fw = [Gather(s.FW, RW, lanes, i in y_first_chunks) for i, lanes in enumerate(cuts)]
    f_wq, f_pt = Spread(g_wq, s.WQ), Spread(g_pt, s.PT)
    h_mix, h_bg, h_og, h_tg = Share(s.MIX, 4), Share(s.BG, 1), Share(o_out, 1), Share(o_tok, 2)
    n_mb = NarrowSum(s.MB, s.MBC, s.MBX, s.MBS)
    n_op = NarrowSum(s.OP, s.OPC, s.OPX, s.OPS)
    w_kv = WideSum(s.KVF, s.DKVY, s.DKVR, s.DKVO, y.KT, z_first="wkv" in z_first_sums)
    w_fw = []
    for i, lanes in enumerate(cuts):
        out = o_fw.at[:, pl.ds(*lanes)]
        got = (s.RF0, s.RF1, s.RF2)[i]
        w_fw.append(WideSum(s.FW, s.YFW, got, out, RW, lanes, i in z_first_chunks))
    w_pt = WideSum(s.PPT, s.YPT, s.RPT, o_pt, RW, z_first="wpt" in z_first_sums)
    w_q, tiles = [], [(0, LANES), (LANES, LANES)]
    for lanes, got in zip(tiles, (s.RQ0, s.RQ1)):
        w_q.append(WideSum(s.PQ, s.YQ, got, o_q.at[:, pl.ds(*lanes)], RW, lanes))
    k_a2a, k_gain = (take(3), take(3)), take(3)

    ops = {}

    def op(name):
        def keep(act):
            ops[name] = act
            return act

        return keep

    def gather_ops(name, gather, split):
        ops[f"{name}.L"], ops[f"{name}.Ly"] = gather.launch, gather.launch_y
        for i in range(1, 4):
            count = A if i == 3 else 1
            ops[f"{name}.h{i}"] = lambda count=count: gather.pump(count, not split)
            if split and not gather.y_first:
                ops[f"{name}.y{i}"] = lambda count=count: gather.pump_y(count)

    def spread_ops(name, spread):
        for i in range(4):
            count = A if i == 3 else 1
            ops[f"{name}.s{i}"] = lambda count=count: spread.pump(count)
            ops[f"{name}.f{i}"] = lambda count=count: spread.pump_forward(count)

    def sum_ops(name, exchange, finish):
        for i in range(3):
            count = A if i == 2 else 1
            if name in direct_sums:
                ops[f"{name}.d{i}"] = lambda count=count: exchange.send_direct(count)
            else:
                extra = 1 if exchange.z_first and i == 1 else 0
                ops[f"{name}.s{i}"] = lambda count=count + extra: exchange.pump(count)
        if exchange.z_first:
            ops[f"{name}.ends"] = exchange.start_ends
            ops[f"{name}.finy"] = finish
            ops[f"{name}.fin"] = exchange.finish
        else:
            ops[f"{name}.fin"] = finish

    gather_ops("wq", g_wq, False)
    gather_ops("pt", g_pt, False)
    gather_ops("kv", g_kv, False)
    spread_ops("fwq", f_wq)
    spread_ops("fpt", f_pt)

    def chunk_finish(i, name):
        exchange, lanes = w_fw[i], pl.ds(*cuts[i])
        if name in direct_sums:
            exchange.finish_direct()
        else:
            (exchange.finish_y if exchange.z_first else exchange.finish)()
        write(exchange.total, r_fw.at[:, lanes])

    for i, name in zip(chunk_order, "abc"):
        gather_ops(name, g_fw[i], True)
        sum_ops("w" + name, w_fw[i], lambda i=i, name="w" + name: chunk_finish(i, name))

    def factor_finish(name, exchange, target=None):
        if name in direct_sums:
            exchange.finish_direct()
        else:
            (exchange.finish_y if exchange.z_first else exchange.finish)()
        if target is not None:
            write(exchange.total, target)

    sum_ops("wkv", w_kv, lambda: factor_finish("wkv", w_kv))
    sum_ops("wpt", w_pt, lambda: factor_finish("wpt", w_pt, r_pt))
    for i, name in enumerate(("wqa", "wqb")):
        target = r_q.at[:, pl.ds(*tiles[i])]
        sum_ops(
            name,
            w_q[i],
            lambda i=i, name=name, target=target: factor_finish(name, w_q[i], target),
        )

    own = pl.ds(pl.multiple_of(w * RW, RW), RW)
    own_rows = pl.ds(pl.multiple_of(n * T, T), T)
    blank = lambda count, kind=bf16: jnp.zeros((count, RW), kind)
    held = SimpleNamespace()

    @op("prep_wq")
    def _():
        shared_part = jnp.concatenate([qshared[...].astype(f32), blank(LANES - y.SQ, f32)], axis=0)
        gain_row = row_iota(8, RW)
        gain_part = jnp.where(
            gain_row == 0,
            prenorm[...].astype(f32),
            jnp.where(gain_row == 1, midnorm[...].astype(f32), 0.0),
        )
        second_part = jnp.concatenate(
            [part[...].astype(f32) for part in (kshared, vshared, qheads, kheads, vheads)]
            + [gain_part, blank(LANES - y.og - 8, f32)],
            axis=0,
        )
        s.WQ[n, own, :LANES] = shared_part.T.astype(bf16)
        s.WQ[n, own, LANES:] = second_part.T.astype(bf16)

    @op("prep_pt")
    def _():
        loads[0].wait()
        for first in range(0, 256, LANES):
            s.PT[n, own, first : first + LANES] = project[first : first + LANES, :].T

    @op("prep_fw")
    def _():
        for load in loads[1:4]:
            load.wait()
        for base, wide, unit, _ in chunks[:last]:
            for part, weight in enumerate((gating, upward, downward)):
                for first in range(0, 256, LANES):
                    to = base + part * 256 + first
                    s.FW[own, to : to + LANES] = weight[unit + first : unit + first + LANES, :].T
        base, wide, unit, _ = chunks[last]
        s.FW[own, base : base + LANES] = gating[unit:FM, :].T
        s.FW[own, base + LANES : base + 2 * LANES] = upward[unit:FM, :].T
        s.FW[own, base + 2 * LANES : base + wide] = jnp.concatenate(
            [gating[FM:, :], upward[FM:, :]], axis=0
        ).T
        s.FW[own, base + wide : base + wide + LANES] = downward[unit:FM, :].T
        s.FW[own, base + wide + LANES :] = jnp.concatenate(
            [downward[FM:, :], blank(FP - F)], axis=0
        ).T

    def own_row(values):
        mine = row_iota(N, values.shape[1]) == n
        return jnp.sum(jnp.where(mine, values.astype(f32), 0.0), axis=0, keepdims=True)

    def mask_block(block):
        first = block * KB
        key_docs = own_row(docs[:, pl.ds(pl.multiple_of(first, KB), KB)])
        allowed = (lane_iota(T, KB) + first <= row_iota(T, KB) + w * T) & (
            key_docs == s.DOC[:, :1]
        )
        s.BIAS[...] = jnp.where(allowed, 0.0, masked_score)

    @op("consts")
    def _():
        column, head = row_iota(LANES, D), lane_iota(LANES, D) >> 6
        for r in range(QR):
            s.EQ[r] = jnp.where(column == head * QR + r, 1.0, 0.0).astype(bf16)
        place = (w * T + row_iota(T)).astype(f32)
        lane = lane_iota(T)
        angle = place * jnp.exp((lane % (DH // 2)).astype(f32) * (-math.log(10000.0) / (DH // 2)))
        s.ROPE[0] = jnp.cos(angle)
        s.ROPE[1] = jnp.where(lane % DH < DH // 2, -jnp.sin(angle), jnp.sin(angle))

        own_docs = own_row(docs[:, pl.ds(pl.multiple_of(w * T, T), T)])
        own_docs = jnp.transpose(jnp.broadcast_to(own_docs, (T, T)))
        s.DOC[...] = own_docs

        mask_block(0)

    def rotated(tile, back=False):
        turned = swap_quarters(tile) * s.ROPE[1]
        return tile * s.ROPE[0] - turned if back else tile * s.ROPE[0] + turned

    def collect(start, width):
        pieces = []
        for p in range(N):
            pieces += [(held.second_tiles[p], start, p * width, width)]
        return place_lanes(pieces)

    @op("project")
    def _():
        loads[4].wait()
        f_wq.landed()
        gains = s.WQ[0, :, LANES:].astype(f32).T
        s.GAIN[0:1, :] = gains[y.og : y.og + 1]
        s.GAIN[1:2, :] = gains[y.og + 1 : y.og + 2]

        x_own = tok[own_rows, :].astype(f32)
        r1_own = row_scale(x_own)
        normed_own = (x_own * r1_own * s.GAIN[0:1, :]).astype(bf16)
        factors = [dot_nn(normed_own, s.WQ[p]) for p in range(N)]
        held.first_tiles = [part[:, :LANES] for part in factors]
        held.second_tiles = [part[:, LANES:] for part in factors]

        kv_own = pl.ds(pl.multiple_of(w * T, T), T)
        kv_own = pl.multiple_of(w * y.KT, 32)
        s.KVF[pl.ds(kv_own, T), 0:128] = rotated(collect(y.oK, y.SK)).astype(bf16)
        s.KVF[pl.ds(kv_own, T), 128:256] = collect(y.oV, y.SK).astype(bf16)
        heads = place_lanes(
            [(held.second_tiles[p], y.ok, p * y.HK, y.HK) for p in range(N)]
            + [(held.second_tiles[p], y.ov, (N + p) * y.HK, y.HK) for p in range(N)]
        )
        s.KVF[pl.ds(kv_own + T, T // 4), :] = pack_heads(heads).astype(bf16)

    def spread_heads(r):
        return dot_nn(s.QH[:, :LANES], s.EQ[r]) + dot_nn(s.QH[:, LANES:], s.EQ[r])

    @op("queries")
    def _():
        query_heads = collect(y.oq, y.HQ)
        heads_high = query_heads.astype(bf16)
        s.QH[:, :LANES] = heads_high
        s.QH[:, LANES:] = (query_heads - heads_high.astype(f32)).astype(bf16)

        queries = jnp.zeros((T, D), f32)
        for r in range(QR):
            pieces = canonical_pieces(held.first_tiles, y.SQ, r * DH, DH, 0, 0)
            pieces += canonical_pieces(held.first_tiles, y.SQ, r * DH, DH, 0, DH)
            turned = rotated(place_lanes(pieces))
            s.QROT[r] = turned
            queries = queries + spread_heads(r) * jnp.concatenate([turned] * pairs, axis=1)
        for i in range(pairs):
            tile = (queries[:, i * LANES : (i + 1) * LANES] * (1.0 / QR)).astype(bf16)
            s.QP[i] = tile * jnp.asarray(DH**-0.5, bf16)

        def norm_rows(block, _):
            at = pl.ds(pl.multiple_of(block * T, T), T)
            values = tok[at, :].astype(f32)
            s.NORM[at, :] = (values * row_scale(values) * s.GAIN[0:1, :]).astype(bf16)
            return 0

        lax.fori_loop(0, N, norm_rows, 0)

    def expand_block(block):
        tiles = []
        for t in range(KB // T):
            first = pl.multiple_of((block * (KB // T) + t) * y.KT, 32)
            lanes = slice(t * T, (t + 1) * T)
            for kind in range(2):
                shared = s.KVF[pl.ds(first, T), kind * 128 : kind * 128 + 128]
                s.SHARED[kind, :, lanes] = shared.astype(f32).T
            tiles.append(unpack_heads(s.KVF[pl.ds(first + T, T // 4), :].astype(f32)).T)
        heads = jnp.concatenate(tiles, axis=1)
        for i in range(pairs):
            for kind in range(2):
                first = kind * y.heads * KR + 4 * i
                s.HT[i, 4 * kind : 4 * kind + 4, :] = heads[first : first + 4]

        def expand(i, _):
            for kind, ref in enumerate((s.KP, s.VP)):
                one, two = s.SHARED[kind, :DH, :], s.SHARED[kind, DH:, :]
                for half in range(2):
                    row = 4 * kind + 2 * half
                    joined = s.HT[i, row : row + 1, :] * one + s.HT[i, row + 1 : row + 2, :] * two
                    ref[i, half * DH : (half + 1) * DH, :] = (joined * 0.5).astype(bf16)
            return 0

        lax.fori_loop(0, pairs, expand, 0)

    def pair_bias():
        bias = s.BIAS[...]
        return jnp.concatenate([bias, bias], axis=0)

    def forward_pair(i):
        scores = dot_nn(stack_pair(s.QP[i]), s.KP[i]) + pair_bias()
        top = jnp.max(scores, axis=1, keepdims=True)
        if y.NB > 1:
            old_top = s.LSE[i][:, :1]
            top = jnp.maximum(top, old_top)
        weights = jnp.exp(scores - top)
        total = jnp.sum(weights, axis=1, keepdims=True)
        rows_out = dot_nt(weights.astype(bf16), s.VP[i])
        if y.NB > 1:
            factor = jnp.exp(old_top - top)
            total = total + s.RUN[i][:, :1] * factor
            s.LSE[i] = jnp.broadcast_to(top, (2 * T, LANES))
            s.RUN[i] = jnp.broadcast_to(total, (2 * T, LANES))
            keep = stack_pair(s.ATT[i]) * factor
            s.ATT[i] = unstack_pair(rows_out + keep)
        return top, total, rows_out

    def store_mixture(i, attended, top, total):
        s.ATT[i] = attended
        s.LSE[i] = jnp.broadcast_to(top + jnp.log(total), (2 * T, LANES))
        s.MIX[own_rows, pl.ds(pl.multiple_of(i * LANES, LANES), LANES)] = attended.astype(bf16)

    def forward_step(i, _):
        top, total, rows_out = forward_pair(i)
        store_mixture(i, unstack_pair(rows_out / total), top, total)
        return 0

    @op("at_x")
    def _():
        g_kv.landed_all()
        if y.NB == 1:
            expand_block(0)
            return
        s.LSE[...] = jnp.full(s.LSE.shape, masked_score, f32)
        s.RUN[...] = jnp.zeros(s.RUN.shape, f32)
        s.ATT[...] = jnp.zeros(s.ATT.shape, f32)

        def forward_block(block, _):
            mask_block(block)
            expand_block(block)

            def step(i, _):
                forward_pair(i)
                return 0

            lax.fori_loop(0, pairs, step, 0)
            return 0

        lax.fori_loop(0, y.NB, forward_block, 0)

        def finish_step(i, _):
            total = s.RUN[i][:, :1]
            store_mixture(i, unstack_pair(stack_pair(s.ATT[i]) / total), s.LSE[i][:, :1], total)
            return 0

        lax.fori_loop(0, pairs, finish_step, 0)

    def forward_chunk(chunk):
        per = pairs // h_mix.chunks
        if y.NB == 1:
            lax.fori_loop(chunk * per, (chunk + 1) * per, forward_step, 0)
        h_mix.start(chunk)

    for i in range(h_mix.chunks):
        ops[f"at{i}"] = lambda i=i: forward_chunk(i)
        ops[f"mix.f{i}"] = lambda i=i: h_mix.forward(i)

    @op("middle")
    def _():
        loads[5].wait()
        h_mix.landed_all()
        f_pt.landed()
        def middle_rows(block, _):
            at = pl.ds(pl.multiple_of(block * 2 * T, 2 * T), 2 * T)
            values = tok[at, :].astype(f32)
            for p in range(N):
                values = values + dot_nt(s.MIX[at, p * 256 : (p + 1) * 256], s.PT[p])
            scale = row_scale(values)
            s.MID[at, :] = values
            s.R2[at, :] = jnp.broadcast_to(scale, (2 * T, LANES))
            s.NM[at, :] = (values * scale * s.GAIN[1:2, :]).astype(bf16)
            return 0

        lax.fori_loop(0, 2, middle_rows, 0)

    def gates(gate, up, pushed):
        chance = 1.0 / (1.0 + jnp.exp(-gate))
        silu = gate * chance
        back = pushed * up * chance * (1.0 + gate * (1.0 - chance))
        return silu * up, back, pushed * silu

    tail_low = lane_iota(2 * T) < DH

    def dense_rows(chunk, far):
        base, wide, unit, units = chunks[chunk]
        first = sum(part[1] for part in chunks[:chunk])
        block = (1 - xo) if far else xo
        at = pl.ds(pl.multiple_of(block * 2 * T, 2 * T), 2 * T)
        both = dot_nn(s.NM[at, :], s.FW[:, base : base + wide])
        back = dot_nn(cot[at, :], s.FW[:, base + wide : base + wide + units])
        width = 256 if chunk < last else LANES
        hidden, gate_back, up_back = gates(
            both[:, :width], both[:, width : 2 * width], back[:, :width]
        )
        s.HID[at, unit : unit + width] = hidden.astype(bf16)
        s.GG[at, first : first + width] = gate_back.astype(bf16)
        s.GG[at, first + width : first + 2 * width] = up_back.astype(bf16)
        if chunk == last:
            tail = both[:, 2 * width :]
            hidden, gate_back, up_back = gates(tail, pltpu.roll(tail, DH, 1), back[:, width:])
            s.HID[at, unit + width :] = jnp.where(tail_low, hidden, 0.0).astype(bf16)
            up_back = pltpu.roll(up_back, DH, 1)
            s.GG[at, first + 2 * width :] = jnp.where(tail_low, gate_back, up_back).astype(bf16)
        mid = dot_nt(s.GG[at, first : first + wide], s.FW[:, base : base + wide])
        out = dot_nt(s.HID[at, unit : unit + units], s.FW[:, base + wide : base + wide + units])
        if chunk != chunk_order[0]:
            mid = mid + s.MB[at, :].astype(f32)
            out = out + s.OP[at, :].astype(f32)
        s.MB[at, :] = mid.astype(bf16)
        s.OP[at, :] = out.astype(bf16)

    def grad_blocks(parts, exchange):
        per = A // 4
        for j in range(4):
            block = z_order[j] if A == 4 else j
            at = pl.ds(pl.multiple_of(block * 256, 256), 256)
            for target, to, left, right, lanes in parts:
                value = dot_tn(left[:, at], right[:, lanes]).astype(bf16)
                target[at, to : to + value.shape[1]] = value
            if not exchange.z_first:
                for q in range(per):
                    exchange.start(block * per + q)

    def dense_grads(chunk):
        base, wide, unit, units = chunks[chunk]
        first = sum(part[1] for part in chunks[:chunk])
        g_fw[chunk].sent()
        grad_blocks(
            [
                (s.FW, base, s.NM, s.GG, slice(first, first + wide)),
                (s.FW, base + wide, cot, s.HID, slice(unit, unit + units)),
            ],
            w_fw[chunk],
        )


    def dense_chunk(chunk):
        g_fw[chunk].landed_all()
        dense_rows(chunk, True)
        dense_rows(chunk, False)

    for i, name in zip(chunk_order, "abc"):
        ops["ff_" + name] = lambda i=i: dense_chunk(i)
        ops["g_" + name] = lambda i=i: dense_grads(i)

    def last_dense(far):
        if far:
            g_fw[chunk_order[-1]].landed_all()
        dense_rows(chunk_order[-1], far)
        n_mb.start(far)

    ops["ffCf"] = lambda: last_dense(True)
    ops["ffCn"] = lambda: last_dense(False)
    ops["mb.pass"] = n_mb.pass_on

    @op("op.start")
    def _():
        n_op.start(True)
        n_op.start(False)

    ops["op.pass"] = n_op.pass_on

    @op("mid")
    def _():
        mid_back = n_mb.result()
        mid_own = s.MID[own_rows, :]
        r2_own = s.R2[own_rows, :][:, :1]
        scaled = mid_back * s.GAIN[1:2, :]
        s.GS[1:2, :] = jnp.sum(mid_back * mid_own * r2_own, axis=0, keepdims=True)
        middle_gradient = (
            cot[own_rows, :].astype(f32)
            + r2_own * scaled
            - mid_own * (r2_own * r2_own * r2_own) * jnp.mean(scaled * mid_own, axis=-1, keepdims=True)
        )
        s.MG[...] = middle_gradient
        branch = middle_gradient.astype(bf16)
        s.BG[own_rows, :] = branch
        h_bg.start(0)
        for p in range(N):
            part = dot_nn(branch, s.PT[p]).astype(bf16)
            s.DO[2 * p] = part[:, :LANES]
            s.DO[2 * p + 1] = part[:, LANES:]

    def backward_part(block, part):
        if part == 0:
            s.DST[...] = jnp.zeros(s.DST.shape, f32)

        def step(i, _):
            query, pushed = s.QP[i], s.DO[i]
            query2, pushed2 = stack_pair(query), stack_pair(pushed)
            product = pushed.astype(f32) * s.ATT[i]
            delta = jnp.sum(stack_pair(product), axis=1, keepdims=True)
            scores = dot_nn(query2, s.KP[i]) + pair_bias()
            chance = jnp.exp(scores - jnp.concatenate([s.LSE[i]] * (KB // LANES), axis=1))
            gradient = (chance * (dot_nn(pushed2, s.VP[i]) - delta)).astype(bf16)
            s.QB[i] = s.QB[i] + unstack_pair(dot_nt(gradient, s.KP[i])) * DH**-0.5
            key_back = dot_tn(query2, gradient)
            value_back = dot_tn(pushed2, chance.astype(bf16))
            for kind, back in enumerate((key_back, value_back)):
                for r in range(KR):
                    shared = slice(r * DH, (r + 1) * DH)
                    found = s.DST[kind, shared, :]
                    for half in range(2):
                        mine = back[half * DH : (half + 1) * DH]
                        row = 4 * kind + 2 * half + r
                        found = found + s.HT[i, row : row + 1, :] * mine
                        s.DHT[i, row : row + 1, :] = jnp.sum(
                            mine * s.SHARED[kind, shared, :], axis=0, keepdims=True
                        )
                    s.DST[kind, shared, :] = found
            return 0

        quarter = pairs // 4
        lax.fori_loop(part * quarter, (part + 1) * quarter, step, 0)
        if part < 3:
            return
        at = pl.ds(pl.multiple_of(block * KB, KB), KB)
        heads = [s.DHT[i, 4 * kind : 4 * kind + 4, :] for kind in range(2) for i in range(pairs)]
        heads.append(jnp.zeros((LANES - 8 * pairs, KB), f32))
        heads = jnp.concatenate(heads, axis=0) * 0.5
        for t in range(KB // T):
            first = pl.multiple_of((block * (KB // T) + t) * y.KT, 32)
            lanes = slice(t * T, (t + 1) * T)
            for kind in range(2):
                shared = (s.DST[kind, :, lanes] * 0.5).T
                s.KVF[pl.ds(first, T), kind * 128 : kind * 128 + 128] = shared.astype(bf16)
            s.KVF[pl.ds(first + T, T // 4), :] = pack_heads(heads[:, lanes].T).astype(bf16)

    def backward_quarter(part):
        if part == 0:
            s.QB[...] = jnp.zeros(s.QB.shape, f32)
            g_kv.sent()
        if y.NB == 1:
            backward_part(0, part)
        elif part == 0:

            def backward_step(block, _):
                mask_block(block)
                expand_block(block)
                for each in range(4):
                    backward_part(block, each)
                return 0

            lax.fori_loop(0, y.NB, backward_step, 0)

    for i in range(4):
        ops[f"bq{i}"] = lambda i=i: backward_quarter(i)

    @op("kvst")
    def _():
        for z in z_order:
            w_kv.start(z)

    ops["bg.f"] = h_bg.forward_all

    @op("pt.g")
    def _():
        h_bg.landed_all()
        mine = pl.ds(pl.multiple_of(n * 256, 256), 256)
        grad_blocks([(s.PPT, 0, s.BG, s.MIX, mine)], w_pt)

    @op("qb")
    def _():
        query_back = jnp.concatenate([s.QB[i] for i in range(pairs)], axis=1)
        heads_back = jnp.zeros((T, LANES), f32)
        shared_back = []
        for r in range(QR):
            turned = s.QROT[r]
            product = (query_back * jnp.concatenate([turned] * pairs, axis=1)).astype(bf16)
            heads_back = heads_back + dot_nt(product, s.EQ[r])
            product = spread_heads(r) * query_back
            total = product[:, :LANES]
            for i in range(1, pairs):
                total = total + product[:, i * LANES : (i + 1) * LANES]
            shared_back.append(fold_halves(total))
        low = lane_iota(T) < DH
        held.shared_tiles = [
            rotated(jnp.where(low, shared_back[2 * t], shared_back[2 * t + 1]), back=True) * (1.0 / QR)
            for t in range(QR // 2)
        ]
        held.heads_back = heads_back * (1.0 / QR)

    @op("op.res")
    def _():
        o_out[own_rows, :] = (s.MID[own_rows, :] + n_op.result()).astype(bf16)
        h_og.start(0)

    ops["og.f"] = h_og.forward_all

    @op("og.l")
    def _():
        h_og.landed_all()
        write(o_out, r_out)

    ops["tg.f"] = h_tg.forward_all

    @op("tg.l")
    def _():
        h_tg.landed_all()
        write(o_tok, r_tok)

    def exchange_factors(tile):
        lanes = pl.ds(*tiles[tile])
        for k, peer in enumerate(narrow_peers):
            to = s.QGR.at[n, :, lanes]
            send(s.QGS.at[peer[1], :, lanes], to, k_a2a[tile] + k, peer)
        s.QGR[n, :, lanes] = s.QGS[n, :, lanes]

    def factors_through(tile):
        lanes = pl.ds(*tiles[tile])
        total = jnp.zeros((T, D), f32)
        for p in range(N):
            total = total + dot_nt(s.QGS[p, :, lanes], s.WQ[p, :, lanes])
        return total

    def factor_gradients(tile):
        lanes = pl.ds(*tiles[tile])
        for k, peer in enumerate(narrow_peers):
            arrive(s.QGR.at[peer[1], :, lanes], k_a2a[tile] + k)
        for j in range(4):
            block = pl.ds(pl.multiple_of(j * 256, 256), 256)
            value = jnp.zeros((256, LANES), f32)
            for p in range(N):
                value = value + dot_tn(s.NORM[p * T : (p + 1) * T, block], s.QGR[p, :, lanes])
            s.PQ[block, lanes] = value.astype(bf16)

    @op("qg1")
    def _():
        for p in range(N):
            s.QGS[p, :, :LANES] = place_lanes(
                canonical_pieces(held.shared_tiles, LANES, p * y.SQ, y.SQ, 0, 0)
            ).astype(bf16)
        exchange_factors(0)

    @op("fb1")
    def _():
        held.first_back = factors_through(0)

    @op("q.g1")
    def _():
        factor_gradients(0)
        for z in z_order:
            w_q[0].start(z)

    @op("qg")
    def _():
        key_shared = rotated(s.DKVO[:T, 0:128], back=True)
        value_shared = s.DKVO[:T, 128:256]
        head_tile = unpack_heads(s.DKVO[T:, :])
        for p in range(N):
            s.QGS[p, :, LANES:] = place_lanes(
                [
                    (key_shared, p * y.SK, y.oK, y.SK),
                    (value_shared, p * y.SK, y.oV, y.SK),
                    (held.heads_back, p * y.HQ, y.oq, y.HQ),
                    (head_tile, p * y.HK, y.ok, y.HK),
                    (head_tile, (N + p) * y.HK, y.ov, y.HK),
                ]
            ).astype(bf16)
        exchange_factors(1)

    @op("fb")
    def _():
        first_back = held.first_back + factors_through(1)
        x_own = tok[own_rows, :].astype(f32)
        r1_own = row_scale(x_own)
        s.GS[0:1, :] = jnp.sum(first_back * x_own * r1_own, axis=0, keepdims=True)
        for k, peer in enumerate(narrow_peers):
            send(s.GS, s.GR.at[k], k_gain + k, peer)
        scaled = first_back * s.GAIN[0:1, :]
        tokens_gradient = (
            s.MG[...]
            + r1_own * scaled
            - x_own * (r1_own * r1_own * r1_own) * jnp.mean(scaled * x_own, axis=-1, keepdims=True)
        )
        o_tok[own_rows, :] = tokens_gradient.astype(bf16)
        for chunk in range(h_tg.chunks):
            h_tg.start(chunk)

    @op("q.g")
    def _():
        for k in range(3):
            arrive(s.GR.at[k], k_gain + k)
        factor_gradients(1)
        gain_rows = s.GS[...]
        for k in range(3):
            gain_rows = gain_rows + s.GR[k]
        lane_row = row_iota(LANES, D)
        spread = jnp.where(
            lane_row == y.og,
            gain_rows[0:1],
            jnp.where(lane_row == y.og + 1, gain_rows[1:2], 0.0),
        )
        gain_columns = spread.T
        s.PQ[:, LANES:] = (s.PQ[:, LANES:].astype(f32) + gain_columns).astype(bf16)
        for z in z_order:
            w_q[1].start(z)

    for name in schedule:
        ops[name]()

    for exchange in (g_wq, g_pt, f_wq, f_pt, *w_fw, w_kv, w_pt, *w_q):
        exchange.sent()
    assert (taken[0], taken[1]) == (rsem.shape[0], ssem.shape[0])
    for copy in pending:
        copy.wait_send()
    for copy in written:
        copy.wait()


def results_kernel(y, out, tok, fw, pt, q, *refs):
    r_out, r_tok, r_pt, r_gate, r_up, r_down = refs[:6]
    o_pre, o_qh, o_qs, o_kh, o_ks, o_vh, o_vs, o_mid = refs[6:14]
    in_fw, in_pt, in_q, in_tok, in_out, o_tok, o_pt, o_gate, o_up, o_down, sems = refs[14:]
    FM, F, half = y.FM, y.F, y.F - y.FM
    used = []

    def start(src, dst):
        copy = pltpu.make_async_copy(src, dst, sems.at[len(used)])
        copy.start()
        used.append(copy)
        return copy

    got_fw, got_pt, got_q = start(fw, in_fw), start(pt, in_pt), start(q, in_q)
    got_tok, got_out = start(tok, in_tok), start(out, in_out)
    got_fw.wait()
    *whole_chunks, (base, wide, unit, _) = y.chunks
    for part, (target, result) in enumerate(((o_gate, r_gate), (o_up, r_up), (o_down, r_down))):
        for at, _, first_unit, _ in whole_chunks:
            for first in range(0, 256, LANES):
                place = at + part * 256 + first
                to = first_unit + first
                target[to : to + LANES, :] = in_fw[:, place : place + LANES].T
        place = base + (wide if part == 2 else part * LANES)
        target[unit:FM, :] = in_fw[:, place : place + LANES].T
        tail = base + (wide + LANES if part == 2 else 2 * LANES)
        tail = in_fw[:, tail : tail + LANES].T
        target[FM:, :] = tail[half:] if part == 1 else tail[:half]
        start(target, result)
    got_tok.wait()
    o_tok[...] = in_tok[...].astype(f32)
    start(o_tok, r_tok)
    got_out.wait()
    start(in_out, r_out)
    got_pt.wait()
    for first in range(0, 256, LANES):
        o_pt[first : first + LANES, :] = in_pt[:, first : first + LANES].T
    start(o_pt, r_pt)
    got_q.wait()
    o_qs[...] = in_q[:, :LANES].T[: y.SQ]
    second = in_q[:, LANES:].T
    o_ks[...] = second[y.oK : y.oK + y.SK]
    o_vs[...] = second[y.oV : y.oV + y.SK]
    o_qh[...] = second[y.oq : y.oq + y.HQ]
    o_kh[...] = second[y.ok : y.ok + y.HK]
    o_vh[...] = second[y.ov : y.ov + y.HK]
    o_pre[...] = second[y.og : y.og + 1]
    o_mid[...] = second[y.og + 1 : y.og + 2]
    for copy in used[5:]:
        copy.wait()


def solution(mesh):
    W, N = mesh.shape["wide"], mesh.shape["narrow"]

    def on_device(
        tokens,
        documents,
        prenorm,
        qheads,
        qshared,
        kheads,
        kshared,
        vheads,
        vshared,
        project,
        midnorm,
        gating,
        upward,
        downward,
        cotangent,
    ):
        R, T, D = tokens.shape
        L = documents.shape[1]
        RW, F = gating.shape
        y = make_layout(W, N, T, D, F, L, N * kheads.shape[1] // KR)
        assert R == N
        scratch = scratch_list(y)
        z_first = len(z_first_chunks) + len(z_first_sums)
        arrivals = 18 * y.A + 39 + z_first * (y.A + 2) + (7 - z_first) * (2 * y.A + 1)
        sends = 71 + len(y_first_chunks) + len(y_first_gathers)
        vmem = pl.BlockSpec(memory_space=pltpu.VMEM)

        def kernel(*refs):
            block_kernel(y, tuple(scratch), *refs)

        shape = jax.ShapeDtypeStruct
        raw = pl.pallas_call(
            kernel,
            out_shape=(
                shape((y.M, D), bf16),
                shape((y.M, D), bf16),
                shape((RW, y.FW), f32),
                shape((RW, 256), f32),
                shape((RW, 256), f32),
            ),
            in_specs=[vmem] * 9 + [pl.BlockSpec(memory_space=pl.ANY)] * 6,
            out_specs=[pl.BlockSpec(memory_space=pl.ANY)] * 5,
            scratch_shapes=[*scratch.values()]
            + [pltpu.SemaphoreType.DMA((count,)) for count in (sends, arrivals, 8, 6)],
            compiler_params=pltpu.CompilerParams(
                collective_id=0, has_side_effects=True, vmem_limit_bytes=63 * 2**20
            ),
            name="block",
        )(
            documents,
            prenorm.reshape(1, RW),
            qheads.T,
            qshared.T,
            kheads.T,
            kshared.T,
            vheads.T,
            vshared.T,
            midnorm.reshape(1, RW),
            project,
            gating.T,
            upward.T,
            downward,
            tokens.reshape(y.M, D),
            cotangent.reshape(y.M, D),
        )

        def results(*refs):
            results_kernel(y, *refs)

        large = ((y.M, D), bf16), ((y.M, D), f32), ((256, RW), f32), *[((F, RW), f32)] * 3
        small = [(count, RW) for count in (1, y.HQ, y.SQ, y.HK, y.SK, y.HK, y.SK, 1)]
        held = [((RW, y.FW), f32), ((RW, 256), f32), ((RW, 256), f32), ((y.M, D), bf16), *large]
        outputs = pl.pallas_call(
            results,
            out_shape=[shape(*each) for each in large] + [shape(each, f32) for each in small],
            in_specs=[pl.BlockSpec(memory_space=pl.ANY)] * 5,
            out_specs=[pl.BlockSpec(memory_space=pl.ANY)] * 6 + [vmem] * 8,
            scratch_shapes=[pltpu.VMEM(*each) for each in held] + [pltpu.SemaphoreType.DMA((11,))],
            compiler_params=pltpu.CompilerParams(vmem_limit_bytes=63 * 2**20),
            name="results",
        )(*raw)
        out, tok, pt_back, gate, up, down, pre, qh, qs, kh, ks, vh, vs, mid = outputs
        tokens_like = lambda values: values.reshape(R, T, D)
        return (
            tokens_like(out),
            tokens_like(tok),
            pre.reshape(RW),
            *[each.T for each in (qh, qs, kh, ks, vh, vs)],
            pt_back,
            mid.reshape(RW),
            gate.T,
            up.T,
            down,
        )

    split = P("wide", "narrow")
    flipped = P("narrow", "wide")
    whole = P(None, "wide", None)
    gain = P("wide")
    return jax.shard_map(
        on_device,
        mesh=mesh,
        in_specs=(
            whole,
            P(),
            gain,
            split,
            split,
            split,
            split,
            split,
            split,
            flipped,
            gain,
            split,
            split,
            flipped,
            whole,
        ),
        out_specs=(
            whole,
            whole,
            gain,
            split,
            split,
            split,
            split,
            split,
            split,
            flipped,
            gain,
            split,
            split,
            flipped,
        ),
        check_vma=False,
    )
```

```python
import math
from types import SimpleNamespace

import jax
import jax.numpy as jnp
from jax import lax
from jax.experimental import pallas as pl
from jax.experimental.pallas import tpu as pltpu
from jax.sharding import PartitionSpec as P

DH = 64
QR = 6
KR = 2
VR = 2
LANES = 128

epsilon = 1e-06
masked_score = -1e30
MESH = pl.DeviceIdType.MESH
gather_parts = (((768, False),), ((512, True), (256, False)), ((384, True), (256, False)))
sum_parts = (((512, False), (256, True)), ((512, False), (256, True)), ((640, False),))
chunk_order = (0, 1, 2)
y_first_gathers = ()
z_first_sums = ()
direct_sums = ("wkv", "wqa", "wqb")
f32 = jnp.float32
bf16 = jnp.bfloat16


def dot_nn(a, b):
    return lax.dot_general(a, b, (((1,), (0,)), ((), ())), preferred_element_type=f32)


def dot_nt(a, b):
    return lax.dot_general(a, b, (((1,), (1,)), ((), ())), preferred_element_type=f32)


def dot_tn(a, b):
    return lax.dot_general(a, b, (((0,), (0,)), ((), ())), preferred_element_type=f32)


def lane_iota(rows, cols=LANES):
    return lax.broadcasted_iota(jnp.int32, (rows, cols), 1)


def row_iota(rows, cols=LANES):
    return lax.broadcasted_iota(jnp.int32, (rows, cols), 0)


def place_lanes(pieces):
    rows = pieces[0][0].shape[0]
    lane = lane_iota(rows)
    result = jnp.zeros((rows, LANES), f32)
    for tile, start, to, count in pieces:
        shift = (to - start) % LANES
        moved = pltpu.roll(tile, shift, 1) if shift else tile
        result = jnp.where((lane >= to) & (lane < to + count), moved, result)
    return result


def canonical_pieces(tiles, width, first, count, start, to):
    pieces = []
    while count:
        part, inside = divmod(first, width)
        take = min(count, width - inside)
        pieces.append((tiles[part], start + inside, to, take))
        first, to, count = first + take, to + take, count - take
    return pieces


def swap_quarters(tile):
    low = lane_iota(tile.shape[0]) % DH < DH // 2
    return jnp.where(low, pltpu.roll(tile, LANES - DH // 2, 1), pltpu.roll(tile, DH // 2, 1))


def stack_pair(tile):
    low = lane_iota(tile.shape[0]) < DH
    zero = jnp.zeros_like(tile)
    return jnp.concatenate([jnp.where(low, tile, zero), jnp.where(low, zero, tile)], axis=0)


def unstack_pair(rows):
    half = rows.shape[0] // 2
    low = lane_iota(half) < DH
    return jnp.where(low, rows[:half], rows[half:])


def pack_heads(tile):
    quarter = tile.shape[0] // 4
    low = lane_iota(quarter) < DH
    parts = [tile[i * quarter : (i + 1) * quarter] for i in range(4)]
    pairs = [
        jnp.where(low, parts[i], pltpu.roll(parts[i + 1], DH, 1)) for i in (0, 2)
    ]
    return jnp.concatenate(pairs, axis=1)


def unpack_heads(rows):
    tiles = (rows[:, :LANES], rows[:, LANES:])
    parts = [part for tile in tiles for part in (tile, pltpu.roll(tile, DH, 1))]
    return jnp.concatenate(parts, axis=0)


def fold_halves(tile):
    return tile + pltpu.roll(tile, DH, 1)


def row_scale(values):
    return lax.rsqrt(jnp.mean(values * values, axis=-1, keepdims=True) + epsilon)


def make_layout(W, N, T, D, F, L, heads):
    lay = SimpleNamespace()
    lay.W, lay.N, lay.T, lay.D, lay.F, lay.L, lay.heads = W, N, T, D, F, L, heads
    lay.A = W // 2
    lay.RW = D // W
    lay.M = N * T
    lay.KT = T + T // 4
    lay.FM = F // LANES * LANES
    lay.FP = lay.FM + LANES
    full = lay.FM // 256
    lay.chunks = [(768 * i, 512, 256 * i, 256) for i in range(full)]
    lay.chunks.append((768 * full, 3 * LANES, 256 * full, 256))
    lay.FW = 768 * full + 5 * LANES
    assert lay.FM % 256 == LANES
    lay.pairs = heads // 2
    assert len(lay.chunks) == 3
    lay.KB = L if L <= 1024 else 512
    lay.NB = L // lay.KB
    lay.SQ = QR * DH // N
    lay.SK = KR * DH // N
    lay.HQ = heads * QR // N
    lay.HK = heads * KR // N
    lay.oK, lay.oV = 0, lay.SK
    lay.oq = 2 * lay.SK
    lay.ok = lay.oq + lay.HQ
    lay.ov = lay.ok + lay.HK
    lay.og = lay.ov + lay.HK
    assert N == 4 and W % 8 == 0 and T == LANES and D == heads * DH == 1024
    assert F % LANES == DH and lay.SQ <= LANES and lay.og + 2 <= LANES
    return lay


def scratch_list(y):
    W, N, T, D, L, A, RW, M = y.W, y.N, y.T, y.D, y.L, y.A, y.RW, y.M
    vm = lambda *shape, kind=bf16: pltpu.VMEM(shape, kind)
    GUc = 2 * y.FM + LANES
    return dict(
        PIN=vm(256, RW),
        GIN=vm(y.F, RW),
        UIN=vm(y.F, RW),
        DIN=vm(y.F, RW),
        XIN=vm(M, D),
        CIN=vm(M, D),
        WQ=vm(N, D, 256),
        PT=vm(N, D, 256),
        FW=vm(D, y.FW),
        KVF=vm(L // T * y.KT, 256),
        KP=vm(y.pairs, LANES, y.KB),
        VP=vm(y.pairs, LANES, y.KB),
        EQ=vm(QR, LANES, D),
        SHARED=vm(2, LANES, y.KB, kind=f32),
        HT=vm(y.pairs, 8, y.KB, kind=f32),
        DHT=vm(y.pairs, 8, y.KB, kind=f32),
        BIAS=vm(T, y.KB, kind=f32),
        DOC=vm(T, LANES, kind=f32),
        ROPE=vm(2, T, LANES, kind=f32),
        GAIN=vm(8, D, kind=f32),
        QROT=vm(QR, T, LANES, kind=f32),
        QH=vm(T, 256),
        QP=vm(y.pairs, T, LANES),
        ATT=vm(y.pairs, T, LANES, kind=f32),
        LSE=vm(y.pairs, 2 * T, LANES, kind=f32),
        RUN=vm(y.pairs if y.NB > 1 else 1, 2 * T, LANES, kind=f32),
        MIX=vm(M, D),
        NORM=vm(M, D),
        MID=vm(M, D, kind=f32),
        NM=vm(M, D),
        R2=vm(M, LANES, kind=f32),
        HID=vm(M, y.FP),
        GG=vm(M, GUc),
        MB=vm(M, D),
        MBC=vm(2, T, D),
        MBX=vm(T, D),
        MBS=vm(T, D),
        OP=vm(M, D),
        OPC=vm(2, T, D),
        OPX=vm(T, D),
        OPS=vm(T, D),
        BG=vm(M, D),
        MG=vm(T, D, kind=f32),
        DO=vm(y.pairs, T, LANES),
        QB=vm(y.pairs, T, LANES, kind=f32),
        DST=vm(2, LANES, y.KB, kind=f32),
        DKVY=vm(A * y.KT, 256),
        DKVR=vm((A + 1) * y.KT * (1 + ("wkv" in z_first_sums)), 256),
        DKVO=vm(y.KT, 256, kind=f32),
        QGS=vm(N, T, 256),
        QGR=vm(N, T, 256),
        OUT=vm(M, D),
        TOK=vm(M, D),
        TFW=vm(RW, y.FW, kind=f32),
        TPT=vm(RW, 256, kind=f32),
        TQ=vm(RW, 256, kind=f32),
        GS=vm(8, D, kind=f32),
        GR=vm(3, 8, D, kind=f32),
        YFW=vm(A * RW, y.FW),
        **{
            f"RF{i}{j}": vm((A + 1) * RW * (1 + z_first), lanes)
            for i, parts in enumerate(sum_parts)
            for j, (lanes, z_first) in enumerate(parts)
        },
        PPT=vm(D, 256),
        YPT=vm(A * RW, 256),
        RPT=vm((A + 1) * RW * (1 + ("wpt" in z_first_sums)), 256),
        PQ=vm(D, 256),
        YQ=vm(A * RW, 256),
        RQ0=vm((A + 1) * RW, LANES),
        RQ1=vm((A + 1) * RW, LANES),
    )


def schedule(do):
    return (
        do.prep_wq, do.wf_Ly, do.wq_L, do.prep_pt, do.wq_Ly, do.prep_fw, do.b_Ly, do.wf_L,
        do.pt_L, do.wq_h1, do.fwq_s0, do.wf_h1, do.pt_Ly, do.c2_L, do.fwf_s0, do.wq_h2, do.a_L,
        do.fwq_s1, do.wf_h2, do.fwq_f0, do.wq_h3, do.c2_Ly, do.pt_h1, do.a_Ly, do.consts,
        do.fwq_s2, do.fwq_s3, do.fpt_s0, do.fwf_f0, do.fwq_f1, do.wf_h3, do.a_h1, do.fwf_s1,
        do.fwq_f2, do.pt_h2, do.fwq_f3, do.project, do.c_Ly, do.fpt_s1, do.kv_L, do.fwf_s2,
        do.c2_h1, do.kv_Ly, do.kv_h1, do.fpt_f0, do.pt_h3, do.fpt_s2, do.b2_L, do.fwf_f1,
        do.kv_h2, do.b2_Ly, do.a_h2, do.fwf_f2, do.fwf_s3, do.kv_h3, do.fpt_s3, do.c2_h2,
        do.fpt_f1, do.b2_h1, do.b_L, do.a_y1, do.a_y2, do.fwf_f3, do.queries, do.b2_y1, do.fpt_f2,
        do.at_x, do.at0, do.at1, do.at2, do.b2_h2, do.c2_h3, do.a_h3, do.a_y3, do.at3, do.mix_f0,
        do.b2_y2, do.b_h1, do.c2_y1, do.fpt_f3, do.c_L, do.b2_h3, do.b2_y3, do.mix_f1, do.c2_y2,
        do.mix_f2, do.mix_f3, do.c2_y3, do.middle, do.ff_a, do.g_a, do.wa2_ends, do.b_h2, do.c_h1,
        do.wa_s0, do.b_h3, do.ff_b, do.g_b, do.wb2_ends, do.c_h2, do.c_h3, do.ffCf, do.wb_s0,
        do.wa2_s1, do.mb_pass, do.wa_s1, do.ffCn, do.wa2_s2, do.wb2_s1, do.g_c, do.wb2_s2,
        do.op_start, do.wb_s1, do.mid, do.bq0, do.wc_s0, do.wa_s2, do.bq1, do.bq2, do.op_pass,
        do.wb_s2, do.bq3, do.kvst, do.wc_s1, do.qb, do.qg1, do.wkv_d0, do.bg_f, do.pt_g,
        do.wkv_d1, do.wkv_d2, do.op_res, do.wpt_s0, do.q_g1, do.wc_s2, do.wkv_fin, do.qg, do.fb1,
        do.fb, do.wpt_s1, do.og_f, do.tg_s, do.wqa_d0, do.wa2_fin, do.wqa_d1, do.wa_fin,
        do.wb_fin, do.q_g, do.wb2_fin, do.wqa_d2, do.og_l, do.wpt_s2, do.wqb_d0, do.wc_fin,
        do.wqa_fin, do.wa2_finy, do.wqb_d1, do.wqb_d2, do.tg_f, do.tg_l, do.wb2_finy, do.wpt_fin,
        do.wqb_fin,
    )


def block_kernel(y, names, *refs):
    docs, prenorm, qheads, qshared, kheads, kshared, vheads, vshared, midnorm = refs[:9]
    sources = refs[9:15]
    r_out, r_tok, r_fw, r_pt, r_q = refs[15:20]
    s = SimpleNamespace(**dict(zip(names, refs[20:])))
    ssem, rsem, wsem, lsem = refs[20 + len(names) :]
    o_out, o_tok, o_fw, o_pt, o_q = s.OUT, s.TOK, s.TFW, s.TPT, s.TQ
    written = []

    def write(src, dst):
        copy = pltpu.make_async_copy(src, dst, wsem.at[len(written)])
        copy.start()
        written.append(copy)

    project, gating, upward, downward, tok, cot = s.PIN, s.GIN, s.UIN, s.DIN, s.XIN, s.CIN
    loads = []
    for source, target in zip(sources, (project, gating, upward, downward, tok, cot)):
        loads.append(pltpu.make_async_copy(source, target, lsem.at[len(loads)]))
        loads[-1].start()

    W, N, T, D, F, L, A, RW, M = y.W, y.N, y.T, y.D, y.F, y.L, y.A, y.RW, y.M
    FM, FP, KB, pairs = y.FM, y.FP, y.KB, y.pairs
    w = lax.axis_index("wide")
    n = lax.axis_index("narrow")
    zi, yi = w // 2, w % 2
    xo, co = n // 2, n % 2
    y_peer = (zi * 2 + 1 - yi, n)
    c_peer = (w, xo * 2 + 1 - co)
    x_peer = (w, (1 - xo) * 2 + co)
    d_peer = (w, (1 - xo) * 2 + 1 - co)
    narrow_peers = (c_peer, x_peer, d_peer)
    taken = [0, 0]

    def take(count=1):
        taken[0] += count
        return taken[0] - count

    def take_send(count=1):
        taken[1] += count
        return taken[1] - count

    def remote(src, dst, k, peer, send_k):
        return pltpu.make_async_remote_copy(
            src_ref=src,
            dst_ref=dst,
            send_sem=ssem.at[send_k],
            recv_sem=rsem.at[k],
            device_id=peer,
            device_id_type=MESH,
        )

    def all_sent(ref, send_k):
        remote(ref, ref, 0, y_peer, send_k).wait_send()

    pending = []

    def send(src, dst, k, peer):
        copy = remote(src, dst, k, peer, take_send())
        copy.start()
        pending.append(copy)

    def arrive(dst, k):
        remote(dst, dst, k, y_peer, 0).wait_recv()

    def rows(ref, first, count, lanes=None):
        at = pl.ds(pl.multiple_of(first, 16), count)
        return ref.at[at] if lanes is None else ref.at[at, pl.ds(*lanes)]

    def each_at(distance, act):
        if distance == 0:
            act(zi, None)
            return
        pl.when(zi >= distance)(lambda: act(zi - distance, True))
        pl.when(zi + distance < A)(lambda: act(zi + distance, False))

    right_peer = ((zi + 1) * 2 + yi, n)
    left_peer = ((zi - 1) * 2 + yi, n)

    barrier = pltpu.get_barrier_semaphore()
    z_peers = [(((zi + step) % A) * 2 + yi, n) for step in range(1, A)]
    peers = [y_peer, *narrow_peers, *z_peers]
    for peer in peers:
        pl.semaphore_signal(barrier, inc=1, device_id=peer, device_id_type=MESH)
    pl.semaphore_wait(barrier, len(peers))

    class Gather:
        def __init__(self, ref, count, lanes=None, y_first=False, apart=False):
            self.ref, self.count, self.lanes, self.y_first = ref, count, lanes, y_first
            self.apart = apart and not y_first
            self.kz, self.ky = take(A), take(A if self.apart else 1)
            self.sy, self.sr = take_send(), take_send()
            self.sl = take_send() if y_first else self.sr
            self.next = self.next_y = 1

        def part(self, wide):
            return rows(self.ref, wide * self.count, self.count, self.lanes)

        def block(self, z):
            if self.y_first:
                return rows(self.ref, z * 2 * self.count, 2 * self.count, self.lanes)
            return self.part(z * 2 + yi)

        def along(self, z, to_right):
            block = self.block(z)
            if to_right:
                return remote(block, block, self.kz + z, right_peer, self.sr)
            return remote(block, block, self.kz + z, left_peer, self.sl)

        def across(self, z):
            part = self.part(z * 2 + yi)
            return remote(part, part, self.ky + (z if self.apart else 0), y_peer, self.sy)

        def landed(self, z):
            arrive(self.part(z * 2 + 1 - yi), self.ky + (z if self.apart else 0))

        def launch_y(self):
            self.across(zi).start()

        def launch(self):
            if self.y_first:
                self.landed(zi)
            pl.when(zi < A - 1)(lambda: self.along(zi, True).start())
            pl.when(zi > 0)(lambda: self.along(zi, False).start())

        def hop(self, distance, across):
            def act(z, to_right):
                arrive(self.block(z), self.kz + z)
                more = zi < A - 1 if to_right else zi > 0
                pl.when(more)(lambda: self.along(z, to_right).start())
                if across and not self.y_first:
                    self.across(z).start()

            each_at(distance, act)

        def pump(self, count=A, across=True):
            for _ in range(min(count, A - self.next)):
                self.hop(self.next, across)
                self.next += 1

        def pump_y(self, count=A):
            for _ in range(min(count, self.next - self.next_y)):
                each_at(self.next_y, lambda z, _: self.across(z).start())
                self.next_y += 1

        def landed_all(self):
            if not self.y_first:
                arrive(rows(self.ref, 0, A * self.count, self.lanes), self.ky)

        def sent(self):
            def blocks(count):
                return rows(self.ref, 0, count * self.count, self.lanes)

            all_sent(blocks(1 if self.y_first else A), self.sy)
            if self.y_first:
                for z in range(A - 1):
                    pl.when(zi == z)(lambda: all_sent(blocks(2 * z + 2), self.sr))
                    pl.when(zi == z + 1)(lambda: all_sent(blocks(2 * (A - z - 1)), self.sl))
                return
            inner = (zi > 0) & (zi < A - 1)
            pl.when(inner)(lambda: all_sent(blocks(A + 1), self.sr))
            pl.when(jnp.logical_not(inner))(lambda: all_sent(blocks(1), self.sr))

    class Spread:
        def __init__(self, gather, ref):
            self.gather, self.ref, self.lanes = gather, ref, gather.lanes
            self.next = self.passed = 0
            self.kx, self.kc, self.kd = take(A), take(), take()
            self.sx, self.sc, self.sd = take_send(), take_send(), take_send()

        def part(self, owner, z):
            return rows(self.ref.at[owner], z * 2 * RW, 2 * RW, self.lanes)

        def copies(self, z):
            part = self.part(n, z)
            to_x = remote(part, part, self.kx + z, x_peer, self.sx)
            return to_x, remote(part, part, self.kc, c_peer, self.sc)

        def onward(self, z):
            part = self.part(x_peer[1], z)
            return remote(part, part, self.kd, c_peer, self.sd)

        def start(self, distance):
            def act(z, _):
                if not self.gather.y_first:
                    self.gather.landed(z)
                for copy in self.copies(z):
                    copy.start()

            each_at(distance, act)

        def pump(self, count=A):
            for _ in range(min(count, A - self.next)):
                self.start(self.next)
                self.next += 1

        def pump_forward(self, count=A):
            for _ in range(min(count, A - self.passed)):
                self.forward(self.passed)
                self.passed += 1

        def forward(self, distance):
            def act(z, _):
                arrive(self.part(x_peer[1], z), self.kx + z)
                self.onward(z).start()

            each_at(distance, act)

        def landed(self):
            for peer, k in ((c_peer, self.kc), (d_peer, self.kd)):
                arrive(rows(self.ref.at[peer[1]], 0, D, self.lanes), k)

        def sent(self):
            for k in (self.sx, self.sc, self.sd):
                all_sent(rows(self.ref.at[n], 0, D, self.lanes), k)

    class Share:
        def __init__(self, ref, chunks):
            self.ref, self.chunks = ref, chunks
            self.kx, self.kc, self.kd = take(chunks), take(), take()
            self.width = D // chunks

        def part(self, owner, chunk):
            lanes = pl.ds(pl.multiple_of(chunk * self.width, LANES), self.width)
            return self.ref.at[pl.ds(pl.multiple_of(owner * T, T), T), lanes]

        def start(self, chunk):
            send(self.part(n, chunk), self.part(n, chunk), self.kx + chunk, x_peer)
            send(self.part(n, chunk), self.part(n, chunk), self.kc, c_peer)

        def forward(self, chunk):
            part = self.part(x_peer[1], chunk)
            arrive(part, self.kx + chunk)
            send(part, part, self.kd, c_peer)

        def forward_all(self):
            for chunk in range(self.chunks):
                self.forward(chunk)

        def landed_all(self):
            for peer, k in ((c_peer, self.kc), (d_peer, self.kd)):
                arrive(rows(self.ref, peer[1] * T, T), k)

    class NarrowSum:
        def __init__(self, part_ref, core_ref, x_ref, send_ref):
            self.ref, self.core, self.x, self.out = part_ref, core_ref, x_ref, send_ref
            self.kc, self.kx = take(2), take(1)

        def part(self, owner):
            return rows(self.ref, owner * T, T)

        def start(self, far):
            owner = ((1 - xo) if far else xo) * 2 + 1 - co
            send(self.part(owner), self.core.at[int(far)], self.kc + int(far), c_peer)

        def pass_on(self):
            arrive(self.core.at[1], self.kc + 1)
            total = self.part((1 - xo) * 2 + co)[...].astype(f32) + self.core[1].astype(f32)
            self.out[...] = total.astype(bf16)
            send(self.out, self.x, self.kx, x_peer)

        def result(self):
            arrive(self.core.at[0], self.kc)
            arrive(self.x, self.kx)
            return (
                self.part(n)[...].astype(f32) + self.core[0].astype(f32) + self.x[...].astype(f32)
            )

    class WideSum:
        def __init__(
            self, part_ref, y_ref, z_ref, out_ref, count, lanes=None, z_first=False, straight=False
        ):
            self.ref, self.y, self.z, self.total = part_ref, y_ref, z_ref, out_ref
            self.count, self.lanes, self.z_first = count, lanes, z_first
            self.size = 2 * count if z_first else count
            self.next = 0
            self.z_lanes = lanes and (0, lanes[1])
            self.ky, self.kz = take(1 if z_first else A), take(1 if straight else A + 1)
            self.sy, self.sz = take_send(), take_send()

        def part(self, wide):
            return rows(self.ref, wide * self.count, self.count, self.lanes)

        def block(self, z):
            if self.z_first:
                return rows(self.ref, z * 2 * self.count, 2 * self.count, self.lanes)
            return self.part(z * 2 + yi)

        def got_y(self, z):
            return rows(self.y, z * self.count, self.count, self.lanes)

        def got_z(self, slot):
            return rows(self.z, slot * self.size, self.size, self.z_lanes)

        def across(self, z):
            return remote(self.part(z * 2 + 1 - yi), self.got_y(z), self.ky + z, y_peer, self.sy)

        def along(self, z, to_right):
            block = self.block(z)
            if to_right:
                return remote(block, self.got_z(z), self.kz + z, right_peer, self.sz)
            slot = jnp.where(z == zi - 1, A, z)
            return remote(block, self.got_z(slot), self.kz + slot, left_peer, self.sz)

        def start(self, z):
            if not self.z_first:
                self.across(z).start()

        def gather_y(self, z):
            block = self.block(z)[...].astype(f32)
            if self.z_first:
                return block
            arrive(self.got_y(z), self.ky + z)
            return block + self.got_y(z)[...].astype(f32)

        def stage(self, step):
            def move(z, to_right, joined):
                value = self.gather_y(z)
                if joined:
                    arrive(self.got_z(z), self.kz + z)
                    value = value + self.got_z(z)[...].astype(f32)
                self.block(z)[...] = value.astype(bf16)
                self.along(z, to_right).start()

            right, left = A - 1 - step + zi, step - (A - 1 - zi)
            to_right = (right < A) & (right > zi)
            to_left = (left >= 0) & (left < zi)
            pl.when(to_right & (zi > 0))(lambda: move(right, True, True))
            pl.when(to_left & (zi < A - 1))(lambda: move(left, False, True))
            if not self.z_first:
                pl.when(to_right & (zi == 0))(lambda: move(right, True, False))
                pl.when(to_left & (zi == A - 1))(lambda: move(left, False, False))

        def pump(self, count=A):
            for _ in range(min(count, A - 1 - self.next)):
                self.stage(self.next)
                self.next += 1

        def send_direct(self, count=A):
            for k in range(self.next, min(self.next + count, A - 1)):
                self.next += 1
                z = z_order[k] if A == 4 else (zi + 1 + k) % A
                block = self.block(z)
                block[...] = self.gather_y(z).astype(bf16)
                self.direct(z).start()

        def direct(self, z):
            return remote(
                self.block(z), self.got_z(zi), self.kz, (z * 2 + yi, n), self.sz
            )

        def finish_direct(self):
            total = self.gather_y(zi)
            arrive(rows(self.z, 0, (A - 1) * self.size, self.z_lanes), self.kz)
            for step in range(1, A):
                total = total + self.got_z((zi + step) % A)[...].astype(f32)
            self.total[...] = total

        def start_ends(self):
            @pl.when(zi == 0)
            def _():
                for z in range(A - 1, 0, -1):
                    self.along(z, True).start()

            @pl.when(zi == A - 1)
            def _():
                for z in range(A - 1):
                    self.along(z, False).start()

        def add(self, slot):
            arrive(self.got_z(slot), self.kz + slot)
            got = self.got_z(slot)[...].astype(f32)
            if not self.z_first:
                self.total[...] += got
                return
            block = self.block(zi)
            block[...] = (block[...].astype(f32) + got).astype(bf16)

        def finish(self):
            if not self.z_first:
                self.total[...] = self.gather_y(zi)
            pl.when(zi > 0)(lambda: self.add(zi))
            pl.when(zi < A - 1)(lambda: self.add(A))
            if self.z_first:
                self.last_across().start()

        def last_across(self):
            return remote(self.part(zi * 2 + 1 - yi), self.got_y(0), self.ky, y_peer, self.sy)

        def finish_y(self):
            if self.z_first:
                arrive(self.got_y(0), self.ky)
                mine = self.part(zi * 2 + yi)[...].astype(f32)
                self.total[...] = mine + self.got_y(0)[...].astype(f32)

        def sent(self):
            def parts(count):
                return rows(self.ref, 0, count * self.count, self.lanes)

            all_sent(parts(1 if self.z_first else A), self.sy)
            all_sent(parts((A - 1) * (2 if self.z_first else 1)), self.sz)

    if A == 4:
        z_order = []
        for row in zip((3, 2, 1, 0), (3, 2, 0, 1), (0, 1, 3, 2), (0, 1, 2, 3)):
            z_order.append(sum(jnp.where(zi == at, z, 0) for at, z in enumerate(row)))
    else:
        z_order = range(A)

    chunks = y.chunks
    last = len(chunks) - 1
    cuts = [(base, wide + units) for base, wide, _, units in chunks]
    g_wq = Gather(s.WQ.at[n], RW, (LANES, LANES), "wq" in y_first_gathers, True)
    g_wf = Gather(s.WQ.at[n], RW, (0, LANES), "wf" in y_first_gathers, True)
    g_pt = Gather(s.PT.at[n], RW, y_first="pt" in y_first_gathers, apart=True)
    g_kv = Gather(s.KVF, y.KT, y_first="kv" in y_first_gathers)

    def in_parts(chunk, parts):
        first = cuts[chunk][0]
        for lanes, flag in parts[chunk]:
            yield (first, lanes), flag
            first += lanes

    g_fw = [[Gather(s.FW, RW, *part) for part in in_parts(i, gather_parts)] for i in range(3)]
    f_wq, f_wf, f_pt = Spread(g_wq, s.WQ), Spread(g_wf, s.WQ), Spread(g_pt, s.PT)
    h_mix, h_bg, h_og, h_tg = Share(s.MIX, 4), Share(s.BG, 1), Share(o_out, 1), Share(o_tok, 2)
    n_mb = NarrowSum(s.MB, s.MBC, s.MBX, s.MBS)
    n_op = NarrowSum(s.OP, s.OPC, s.OPX, s.OPS)
    kind_of = lambda name: (name in z_first_sums, name in direct_sums)
    w_kv = WideSum(s.KVF, s.DKVY, s.DKVR, s.DKVO, y.KT, None, *kind_of("wkv"))
    w_fw = [[], [], []]
    for i in range(3):
        for j, (lanes, z_first) in enumerate(in_parts(i, sum_parts)):
            out, got = o_fw.at[:, pl.ds(*lanes)], vars(s)[f"RF{i}{j}"]
            name = f"w{'abc'[chunk_order.index(i)]}{'2' if j else ''}"
            straight = name in direct_sums
            w_fw[i].append(WideSum(s.FW, s.YFW, got, out, RW, lanes, z_first, straight))
    w_pt = WideSum(s.PPT, s.YPT, s.RPT, o_pt, RW, None, *kind_of("wpt"))
    w_q, tiles = [], [(0, LANES), (LANES, LANES)]
    for lanes, got, name in zip(tiles, (s.RQ0, s.RQ1), ("wqa", "wqb")):
        out = o_q.at[:, pl.ds(*lanes)]
        w_q.append(WideSum(s.PQ, s.YQ, got, out, RW, lanes, *kind_of(name)))
    k_a2a, k_gain = (take(3), take(3)), take(3)

    ops = {}

    def op(name):
        def keep(act):
            ops[name] = act
            return act

        return keep

    def gather_ops(name, gather, split):
        ops[f"{name}_L"], ops[f"{name}_Ly"] = gather.launch, gather.launch_y
        for i in range(1, 4):
            count = A if i == 3 else 1
            ops[f"{name}_h{i}"] = lambda count=count: gather.pump(count, not split)
            if split and not gather.y_first:
                ops[f"{name}_y{i}"] = lambda count=count: gather.pump_y(count)

    def spread_ops(name, spread):
        for i in range(4):
            count = A if i == 3 else 1
            ops[f"{name}_s{i}"] = lambda count=count: spread.pump(count)
            ops[f"{name}_f{i}"] = lambda count=count: spread.pump_forward(count)

    def sum_ops(name, exchange, finish):
        for i in range(3):
            count = A if i == 2 else 1
            if name in direct_sums:
                ops[f"{name}_d{i}"] = lambda count=count: exchange.send_direct(count)
            else:
                extra = 1 if exchange.z_first and i == 1 else 0
                ops[f"{name}_s{i}"] = lambda count=count + extra: exchange.pump(count)
        if exchange.z_first:
            ops[f"{name}_ends"] = exchange.start_ends
            ops[f"{name}_finy"] = finish
            ops[f"{name}_fin"] = exchange.finish
        else:
            ops[f"{name}_fin"] = finish

    gather_ops("wq", g_wq, False)
    gather_ops("wf", g_wf, False)
    gather_ops("pt", g_pt, False)
    gather_ops("kv", g_kv, False)
    spread_ops("fwq", f_wq)
    spread_ops("fwf", f_wf)
    spread_ops("fpt", f_pt)

    def chunk_finish(exchange, name):
        if name in direct_sums:
            exchange.finish_direct()
        else:
            (exchange.finish_y if exchange.z_first else exchange.finish)()
        write(exchange.total, r_fw.at[:, pl.ds(*exchange.lanes)])

    for i, name in zip(chunk_order, "abc"):
        for gather, part in zip(g_fw[i], ("", "2")):
            gather_ops(name + part, gather, True)
        for exchange, part in zip(w_fw[i], ("", "2")):
            part = f"w{name}{part}"
            sum_ops(part, exchange, lambda at=exchange, name=part: chunk_finish(at, name))

    def factor_finish(name, exchange, target=None):
        if name in direct_sums:
            exchange.finish_direct()
        else:
            (exchange.finish_y if exchange.z_first else exchange.finish)()
        if target is not None:
            write(exchange.total, target)

    sum_ops("wkv", w_kv, lambda: factor_finish("wkv", w_kv))
    sum_ops("wpt", w_pt, lambda: factor_finish("wpt", w_pt, r_pt))
    for i, name in enumerate(("wqa", "wqb")):
        target = r_q.at[:, pl.ds(*tiles[i])]
        sum_ops(
            name,
            w_q[i],
            lambda i=i, name=name, target=target: factor_finish(name, w_q[i], target),
        )

    own = pl.ds(pl.multiple_of(w * RW, RW), RW)
    own_rows = pl.ds(pl.multiple_of(n * T, T), T)
    blank = lambda count, kind=bf16: jnp.zeros((count, RW), kind)
    held = SimpleNamespace()

    @op("prep_wq")
    def _():
        shared_part = jnp.concatenate([qshared[...].astype(f32), blank(LANES - y.SQ, f32)], axis=0)
        gain_row = row_iota(8, RW)
        gain_part = jnp.where(
            gain_row == 0,
            prenorm[...].astype(f32),
            jnp.where(gain_row == 1, midnorm[...].astype(f32), 0.0),
        )
        second_part = jnp.concatenate(
            [part[...].astype(f32) for part in (kshared, vshared, qheads, kheads, vheads)]
            + [gain_part, blank(LANES - y.og - 8, f32)],
            axis=0,
        )
        s.WQ[n, own, :LANES] = shared_part.T.astype(bf16)
        s.WQ[n, own, LANES:] = second_part.T.astype(bf16)

    @op("prep_pt")
    def _():
        loads[0].wait()
        for first in range(0, 256, LANES):
            s.PT[n, own, first : first + LANES] = project[first : first + LANES, :].T

    @op("prep_fw")
    def _():
        for load in loads[1:4]:
            load.wait()
        for base, wide, unit, _ in chunks[:last]:
            for part, weight in enumerate((gating, upward, downward)):
                for first in range(0, 256, LANES):
                    to = base + part * 256 + first
                    s.FW[own, to : to + LANES] = weight[unit + first : unit + first + LANES, :].T
        base, wide, unit, _ = chunks[last]
        s.FW[own, base : base + LANES] = gating[unit:FM, :].T
        s.FW[own, base + LANES : base + 2 * LANES] = upward[unit:FM, :].T
        s.FW[own, base + 2 * LANES : base + wide] = jnp.concatenate(
            [gating[FM:, :], upward[FM:, :]], axis=0
        ).T
        s.FW[own, base + wide : base + wide + LANES] = downward[unit:FM, :].T
        s.FW[own, base + wide + LANES :] = jnp.concatenate(
            [downward[FM:, :], blank(FP - F)], axis=0
        ).T

    def own_row(values):
        mine = row_iota(N, values.shape[1]) == n
        return jnp.sum(jnp.where(mine, values.astype(f32), 0.0), axis=0, keepdims=True)

    def mask_block(block):
        first = block * KB
        key_docs = own_row(docs[:, pl.ds(pl.multiple_of(first, KB), KB)])
        allowed = (lane_iota(T, KB) + first <= row_iota(T, KB) + w * T) & (
            key_docs == s.DOC[:, :1]
        )
        s.BIAS[...] = jnp.where(allowed, 0.0, masked_score)

    @op("consts")
    def _():
        column, head = row_iota(LANES, D), lane_iota(LANES, D) >> 6
        for r in range(QR):
            s.EQ[r] = jnp.where(column == head * QR + r, 1.0, 0.0).astype(bf16)
        place = (w * T + row_iota(T)).astype(f32)
        lane = lane_iota(T)
        angle = place * jnp.exp((lane % (DH // 2)).astype(f32) * (-math.log(10000.0) / (DH // 2)))
        s.ROPE[0] = jnp.cos(angle)
        s.ROPE[1] = jnp.where(lane % DH < DH // 2, -jnp.sin(angle), jnp.sin(angle))

        own_docs = own_row(docs[:, pl.ds(pl.multiple_of(w * T, T), T)])
        own_docs = jnp.transpose(jnp.broadcast_to(own_docs, (T, T)))
        s.DOC[...] = own_docs

        mask_block(0)

    def rotated(tile, back=False):
        turned = swap_quarters(tile) * s.ROPE[1]
        return tile * s.ROPE[0] - turned if back else tile * s.ROPE[0] + turned

    def collect(start, width):
        pieces = []
        for p in range(N):
            pieces += [(held.second_tiles[p], start, p * width, width)]
        return place_lanes(pieces)

    @op("project")
    def _():
        loads[4].wait()
        f_wq.landed()
        gains = s.WQ[0, :, LANES:].astype(f32).T
        s.GAIN[0:1, :] = gains[y.og : y.og + 1]
        s.GAIN[1:2, :] = gains[y.og + 1 : y.og + 2]

        x_own = tok[own_rows, :].astype(f32)
        r1_own = row_scale(x_own)
        normed_own = (x_own * r1_own * s.GAIN[0:1, :]).astype(bf16)
        held.normed_own = normed_own
        held.second_tiles = [dot_nn(normed_own, s.WQ[p, :, LANES:]) for p in range(N)]

        kv_own = pl.ds(pl.multiple_of(w * T, T), T)
        kv_own = pl.multiple_of(w * y.KT, 32)
        s.KVF[pl.ds(kv_own, T), 0:128] = rotated(collect(y.oK, y.SK)).astype(bf16)
        s.KVF[pl.ds(kv_own, T), 128:256] = collect(y.oV, y.SK).astype(bf16)
        heads = place_lanes(
            [(held.second_tiles[p], y.ok, p * y.HK, y.HK) for p in range(N)]
            + [(held.second_tiles[p], y.ov, (N + p) * y.HK, y.HK) for p in range(N)]
        )
        s.KVF[pl.ds(kv_own + T, T // 4), :] = pack_heads(heads).astype(bf16)

    def spread_heads(r):
        return dot_nn(s.QH[:, :LANES], s.EQ[r]) + dot_nn(s.QH[:, LANES:], s.EQ[r])

    @op("queries")
    def _():
        f_wf.landed()
        held.first_tiles = [dot_nn(held.normed_own, s.WQ[p, :, :LANES]) for p in range(N)]
        query_heads = collect(y.oq, y.HQ)
        heads_high = query_heads.astype(bf16)
        s.QH[:, :LANES] = heads_high
        s.QH[:, LANES:] = (query_heads - heads_high.astype(f32)).astype(bf16)

        queries = jnp.zeros((T, D), f32)
        for r in range(QR):
            pieces = canonical_pieces(held.first_tiles, y.SQ, r * DH, DH, 0, 0)
            pieces += canonical_pieces(held.first_tiles, y.SQ, r * DH, DH, 0, DH)
            turned = rotated(place_lanes(pieces))
            s.QROT[r] = turned
            queries = queries + spread_heads(r) * jnp.concatenate([turned] * pairs, axis=1)
        for i in range(pairs):
            tile = (queries[:, i * LANES : (i + 1) * LANES] * (1.0 / QR)).astype(bf16)
            s.QP[i] = tile * jnp.asarray(DH**-0.5, bf16)

        def norm_rows(block, _):
            at = pl.ds(pl.multiple_of(block * T, T), T)
            values = tok[at, :].astype(f32)
            s.NORM[at, :] = (values * row_scale(values) * s.GAIN[0:1, :]).astype(bf16)
            return 0

        lax.fori_loop(0, N, norm_rows, 0)

    def expand_block(block):
        tiles = []
        for t in range(KB // T):
            first = pl.multiple_of((block * (KB // T) + t) * y.KT, 32)
            lanes = slice(t * T, (t + 1) * T)
            for kind in range(2):
                shared = s.KVF[pl.ds(first, T), kind * 128 : kind * 128 + 128]
                s.SHARED[kind, :, lanes] = shared.astype(f32).T
            tiles.append(unpack_heads(s.KVF[pl.ds(first + T, T // 4), :].astype(f32)).T)
        heads = jnp.concatenate(tiles, axis=1)
        for i in range(pairs):
            for kind in range(2):
                first = kind * y.heads * KR + 4 * i
                s.HT[i, 4 * kind : 4 * kind + 4, :] = heads[first : first + 4]

        def expand(i, _):
            for kind, ref in enumerate((s.KP, s.VP)):
                one, two = s.SHARED[kind, :DH, :], s.SHARED[kind, DH:, :]
                for half in range(2):
                    row = 4 * kind + 2 * half
                    joined = s.HT[i, row : row + 1, :] * one + s.HT[i, row + 1 : row + 2, :] * two
                    ref[i, half * DH : (half + 1) * DH, :] = (joined * 0.5).astype(bf16)
            return 0

        lax.fori_loop(0, pairs, expand, 0)

    def pair_bias():
        bias = s.BIAS[...]
        return jnp.concatenate([bias, bias], axis=0)

    def forward_pair(i):
        scores = dot_nn(stack_pair(s.QP[i]), s.KP[i]) + pair_bias()
        top = jnp.max(scores, axis=1, keepdims=True)
        if y.NB > 1:
            old_top = s.LSE[i][:, :1]
            top = jnp.maximum(top, old_top)
        weights = jnp.exp(scores - top)
        total = jnp.sum(weights, axis=1, keepdims=True)
        rows_out = dot_nt(weights.astype(bf16), s.VP[i])
        if y.NB > 1:
            factor = jnp.exp(old_top - top)
            total = total + s.RUN[i][:, :1] * factor
            s.LSE[i] = jnp.broadcast_to(top, (2 * T, LANES))
            s.RUN[i] = jnp.broadcast_to(total, (2 * T, LANES))
            keep = stack_pair(s.ATT[i]) * factor
            s.ATT[i] = unstack_pair(rows_out + keep)
        return top, total, rows_out

    def store_mixture(i, attended, top, total):
        s.ATT[i] = attended
        s.LSE[i] = jnp.broadcast_to(top + jnp.log(total), (2 * T, LANES))
        s.MIX[own_rows, pl.ds(pl.multiple_of(i * LANES, LANES), LANES)] = attended.astype(bf16)

    def forward_step(i, _):
        top, total, rows_out = forward_pair(i)
        store_mixture(i, unstack_pair(rows_out / total), top, total)
        return 0

    @op("at_x")
    def _():
        g_kv.landed_all()
        if y.NB == 1:
            expand_block(0)
            return
        s.LSE[...] = jnp.full(s.LSE.shape, masked_score, f32)
        s.RUN[...] = jnp.zeros(s.RUN.shape, f32)
        s.ATT[...] = jnp.zeros(s.ATT.shape, f32)

        def forward_block(block, _):
            mask_block(block)
            expand_block(block)

            def step(i, _):
                forward_pair(i)
                return 0

            lax.fori_loop(0, pairs, step, 0)
            return 0

        lax.fori_loop(0, y.NB, forward_block, 0)

        def finish_step(i, _):
            total = s.RUN[i][:, :1]
            store_mixture(i, unstack_pair(stack_pair(s.ATT[i]) / total), s.LSE[i][:, :1], total)
            return 0

        lax.fori_loop(0, pairs, finish_step, 0)

    def forward_chunk(chunk):
        per = pairs // h_mix.chunks
        if y.NB == 1:
            lax.fori_loop(chunk * per, (chunk + 1) * per, forward_step, 0)
        h_mix.start(chunk)

    for i in range(h_mix.chunks):
        ops[f"at{i}"] = lambda i=i: forward_chunk(i)
        ops[f"mix_f{i}"] = lambda i=i: h_mix.forward(i)

    @op("middle")
    def _():
        loads[5].wait()
        h_mix.landed_all()
        f_pt.landed()
        def middle_rows(block, _):
            at = pl.ds(pl.multiple_of(block * 2 * T, 2 * T), 2 * T)
            values = tok[at, :].astype(f32)
            for p in range(N):
                values = values + dot_nt(s.MIX[at, p * 256 : (p + 1) * 256], s.PT[p])
            scale = row_scale(values)
            s.MID[at, :] = values
            s.R2[at, :] = jnp.broadcast_to(scale, (2 * T, LANES))
            s.NM[at, :] = (values * scale * s.GAIN[1:2, :]).astype(bf16)
            return 0

        lax.fori_loop(0, 2, middle_rows, 0)

    def gates(gate, up, pushed):
        chance = 1.0 / (1.0 + jnp.exp(-gate))
        silu = gate * chance
        back = pushed * up * chance * (1.0 + gate * (1.0 - chance))
        return silu * up, back, pushed * silu

    tail_low = lane_iota(2 * T) < DH

    def dense_rows(chunk, far):
        base, wide, unit, units = chunks[chunk]
        first = sum(part[1] for part in chunks[:chunk])
        block = (1 - xo) if far else xo
        at = pl.ds(pl.multiple_of(block * 2 * T, 2 * T), 2 * T)
        both = dot_nn(s.NM[at, :], s.FW[:, base : base + wide])
        back = dot_nn(cot[at, :], s.FW[:, base + wide : base + wide + units])
        width = 256 if chunk < last else LANES
        hidden, gate_back, up_back = gates(
            both[:, :width], both[:, width : 2 * width], back[:, :width]
        )
        s.HID[at, unit : unit + width] = hidden.astype(bf16)
        s.GG[at, first : first + width] = gate_back.astype(bf16)
        s.GG[at, first + width : first + 2 * width] = up_back.astype(bf16)
        if chunk == last:
            tail = both[:, 2 * width :]
            hidden, gate_back, up_back = gates(tail, pltpu.roll(tail, DH, 1), back[:, width:])
            s.HID[at, unit + width :] = jnp.where(tail_low, hidden, 0.0).astype(bf16)
            up_back = pltpu.roll(up_back, DH, 1)
            s.GG[at, first + 2 * width :] = jnp.where(tail_low, gate_back, up_back).astype(bf16)
        mid = dot_nt(s.GG[at, first : first + wide], s.FW[:, base : base + wide])
        out = dot_nt(s.HID[at, unit : unit + units], s.FW[:, base + wide : base + wide + units])
        if chunk != chunk_order[0]:
            mid = mid + s.MB[at, :].astype(f32)
            out = out + s.OP[at, :].astype(f32)
        s.MB[at, :] = mid.astype(bf16)
        s.OP[at, :] = out.astype(bf16)

    def grad_blocks(target, to, left, right, lanes, exchange, begin):
        per = A // 4
        for j in range(4):
            block = z_order[j] if A == 4 else j
            at = pl.ds(pl.multiple_of(block * 256, 256), 256)
            value = dot_tn(left[:, at], right[:, lanes]).astype(bf16)
            target[at, to : to + value.shape[1]] = value
            if begin and not exchange.z_first:
                for q in range(per):
                    exchange.start(block * per + q)

    def dense_grads(chunk):
        base, wide, unit, units = chunks[chunk]
        first = sum(part[1] for part in chunks[:chunk])
        for gather in g_fw[chunk]:
            gather.sent()
        one, two = w_fw[chunk][0], w_fw[chunk][-1]
        grad_blocks(s.FW, base, s.NM, s.GG, slice(first, first + wide), one, one is not two)
        grad_blocks(s.FW, base + wide, cot, s.HID, slice(unit, unit + units), two, True)

    def dense_chunk(chunk):
        for gather in g_fw[chunk]:
            gather.landed_all()
        dense_rows(chunk, True)
        dense_rows(chunk, False)

    for i, name in zip(chunk_order, "abc"):
        ops["ff_" + name] = lambda i=i: dense_chunk(i)
        ops["g_" + name] = lambda i=i: dense_grads(i)

    def last_dense(far):
        if far:
            for gather in g_fw[chunk_order[-1]]:
                gather.landed_all()
        dense_rows(chunk_order[-1], far)
        n_mb.start(far)

    ops["ffCf"] = lambda: last_dense(True)
    ops["ffCn"] = lambda: last_dense(False)
    ops["mb_pass"] = n_mb.pass_on

    @op("op_start")
    def _():
        n_op.start(True)
        n_op.start(False)

    ops["op_pass"] = n_op.pass_on

    @op("mid")
    def _():
        mid_back = n_mb.result()
        mid_own = s.MID[own_rows, :]
        r2_own = s.R2[own_rows, :][:, :1]
        scaled = mid_back * s.GAIN[1:2, :]
        s.GS[1:2, :] = jnp.sum(mid_back * mid_own * r2_own, axis=0, keepdims=True)
        middle_gradient = (
            cot[own_rows, :].astype(f32)
            + r2_own * scaled
            - mid_own * (r2_own * r2_own * r2_own) * jnp.mean(scaled * mid_own, axis=-1, keepdims=True)
        )
        s.MG[...] = middle_gradient
        branch = middle_gradient.astype(bf16)
        s.BG[own_rows, :] = branch
        h_bg.start(0)
        for p in range(N):
            part = dot_nn(branch, s.PT[p]).astype(bf16)
            s.DO[2 * p] = part[:, :LANES]
            s.DO[2 * p + 1] = part[:, LANES:]

    def backward_part(block, part):
        if part == 0:
            s.DST[...] = jnp.zeros(s.DST.shape, f32)

        def step(i, _):
            query, pushed = s.QP[i], s.DO[i]
            query2, pushed2 = stack_pair(query), stack_pair(pushed)
            product = pushed.astype(f32) * s.ATT[i]
            delta = jnp.sum(stack_pair(product), axis=1, keepdims=True)
            scores = dot_nn(query2, s.KP[i]) + pair_bias()
            chance = jnp.exp(scores - jnp.concatenate([s.LSE[i]] * (KB // LANES), axis=1))
            gradient = (chance * (dot_nn(pushed2, s.VP[i]) - delta)).astype(bf16)
            s.QB[i] = s.QB[i] + unstack_pair(dot_nt(gradient, s.KP[i])) * DH**-0.5
            key_back = dot_tn(query2, gradient)
            value_back = dot_tn(pushed2, chance.astype(bf16))
            for kind, back in enumerate((key_back, value_back)):
                for r in range(KR):
                    shared = slice(r * DH, (r + 1) * DH)
                    found = s.DST[kind, shared, :]
                    for half in range(2):
                        mine = back[half * DH : (half + 1) * DH]
                        row = 4 * kind + 2 * half + r
                        found = found + s.HT[i, row : row + 1, :] * mine
                        s.DHT[i, row : row + 1, :] = jnp.sum(
                            mine * s.SHARED[kind, shared, :], axis=0, keepdims=True
                        )
                    s.DST[kind, shared, :] = found
            return 0

        quarter = pairs // 4
        lax.fori_loop(part * quarter, (part + 1) * quarter, step, 0)
        if part < 3:
            return
        at = pl.ds(pl.multiple_of(block * KB, KB), KB)
        heads = [s.DHT[i, 4 * kind : 4 * kind + 4, :] for kind in range(2) for i in range(pairs)]
        heads.append(jnp.zeros((LANES - 8 * pairs, KB), f32))
        heads = jnp.concatenate(heads, axis=0) * 0.5
        for t in range(KB // T):
            first = pl.multiple_of((block * (KB // T) + t) * y.KT, 32)
            lanes = slice(t * T, (t + 1) * T)
            for kind in range(2):
                shared = (s.DST[kind, :, lanes] * 0.5).T
                s.KVF[pl.ds(first, T), kind * 128 : kind * 128 + 128] = shared.astype(bf16)
            s.KVF[pl.ds(first + T, T // 4), :] = pack_heads(heads[:, lanes].T).astype(bf16)

    def backward_quarter(part):
        if part == 0:
            s.QB[...] = jnp.zeros(s.QB.shape, f32)
            g_kv.sent()
        if y.NB == 1:
            backward_part(0, part)
        elif part == 0:

            def backward_step(block, _):
                mask_block(block)
                expand_block(block)
                for each in range(4):
                    backward_part(block, each)
                return 0

            lax.fori_loop(0, y.NB, backward_step, 0)

    for i in range(4):
        ops[f"bq{i}"] = lambda i=i: backward_quarter(i)

    @op("kvst")
    def _():
        for z in z_order:
            w_kv.start(z)

    ops["bg_f"] = h_bg.forward_all

    @op("pt_g")
    def _():
        h_bg.landed_all()
        mine = pl.ds(pl.multiple_of(n * 256, 256), 256)
        grad_blocks(s.PPT, 0, s.BG, s.MIX, mine, w_pt, True)

    @op("qb")
    def _():
        query_back = jnp.concatenate([s.QB[i] for i in range(pairs)], axis=1)
        heads_back = jnp.zeros((T, LANES), f32)
        shared_back = []
        for r in range(QR):
            turned = s.QROT[r]
            product = (query_back * jnp.concatenate([turned] * pairs, axis=1)).astype(bf16)
            heads_back = heads_back + dot_nt(product, s.EQ[r])
            product = spread_heads(r) * query_back
            total = product[:, :LANES]
            for i in range(1, pairs):
                total = total + product[:, i * LANES : (i + 1) * LANES]
            shared_back.append(fold_halves(total))
        low = lane_iota(T) < DH
        held.shared_tiles = [
            rotated(jnp.where(low, shared_back[2 * t], shared_back[2 * t + 1]), back=True) * (1.0 / QR)
            for t in range(QR // 2)
        ]
        held.heads_back = heads_back * (1.0 / QR)

    @op("op_res")
    def _():
        o_out[own_rows, :] = (s.MID[own_rows, :] + n_op.result()).astype(bf16)
        h_og.start(0)

    ops["og_f"] = h_og.forward_all

    @op("og_l")
    def _():
        h_og.landed_all()
        write(o_out, r_out)

    ops["tg_f"] = h_tg.forward_all

    @op("tg_l")
    def _():
        h_tg.landed_all()
        write(o_tok, r_tok)

    def exchange_factors(tile):
        lanes = pl.ds(*tiles[tile])
        for k, peer in enumerate(narrow_peers):
            to = s.QGR.at[n, :, lanes]
            send(s.QGS.at[peer[1], :, lanes], to, k_a2a[tile] + k, peer)
        s.QGR[n, :, lanes] = s.QGS[n, :, lanes]

    def factors_through(tile):
        lanes = pl.ds(*tiles[tile])
        total = jnp.zeros((T, D), f32)
        for p in range(N):
            total = total + dot_nt(s.QGS[p, :, lanes], s.WQ[p, :, lanes])
        return total

    def factor_gradients(tile):
        lanes = pl.ds(*tiles[tile])
        for k, peer in enumerate(narrow_peers):
            arrive(s.QGR.at[peer[1], :, lanes], k_a2a[tile] + k)
        for j in range(4):
            block = pl.ds(pl.multiple_of(j * 256, 256), 256)
            value = jnp.zeros((256, LANES), f32)
            for p in range(N):
                value = value + dot_tn(s.NORM[p * T : (p + 1) * T, block], s.QGR[p, :, lanes])
            s.PQ[block, lanes] = value.astype(bf16)

    @op("qg1")
    def _():
        for p in range(N):
            s.QGS[p, :, :LANES] = place_lanes(
                canonical_pieces(held.shared_tiles, LANES, p * y.SQ, y.SQ, 0, 0)
            ).astype(bf16)
        exchange_factors(0)

    @op("fb1")
    def _():
        held.first_back = factors_through(0)

    @op("q_g1")
    def _():
        factor_gradients(0)
        for z in z_order:
            w_q[0].start(z)

    @op("qg")
    def _():
        key_shared = rotated(s.DKVO[:T, 0:128], back=True)
        value_shared = s.DKVO[:T, 128:256]
        head_tile = unpack_heads(s.DKVO[T:, :])
        for p in range(N):
            s.QGS[p, :, LANES:] = place_lanes(
                [
                    (key_shared, p * y.SK, y.oK, y.SK),
                    (value_shared, p * y.SK, y.oV, y.SK),
                    (held.heads_back, p * y.HQ, y.oq, y.HQ),
                    (head_tile, p * y.HK, y.ok, y.HK),
                    (head_tile, (N + p) * y.HK, y.ov, y.HK),
                ]
            ).astype(bf16)
        exchange_factors(1)

    @op("fb")
    def _():
        first_back = held.first_back = held.first_back + factors_through(1)
        x_own = tok[own_rows, :].astype(f32)
        r1_own = row_scale(x_own)
        s.GS[0:1, :] = jnp.sum(first_back * x_own * r1_own, axis=0, keepdims=True)
        for k, peer in enumerate(narrow_peers):
            send(s.GS, s.GR.at[k], k_gain + k, peer)

    @op("tg_s")
    def _():
        first_back = held.first_back
        x_own = tok[own_rows, :].astype(f32)
        r1_own = row_scale(x_own)
        scaled = first_back * s.GAIN[0:1, :]
        tokens_gradient = (
            s.MG[...]
            + r1_own * scaled
            - x_own * (r1_own * r1_own * r1_own) * jnp.mean(scaled * x_own, axis=-1, keepdims=True)
        )
        o_tok[own_rows, :] = tokens_gradient.astype(bf16)
        for chunk in range(h_tg.chunks):
            h_tg.start(chunk)

    @op("q_g")
    def _():
        for k in range(3):
            arrive(s.GR.at[k], k_gain + k)
        factor_gradients(1)
        gain_rows = s.GS[...]
        for k in range(3):
            gain_rows = gain_rows + s.GR[k]
        lane_row = row_iota(LANES, D)
        spread = jnp.where(
            lane_row == y.og,
            gain_rows[0:1],
            jnp.where(lane_row == y.og + 1, gain_rows[1:2], 0.0),
        )
        gain_columns = spread.T
        s.PQ[:, LANES:] = (s.PQ[:, LANES:].astype(f32) + gain_columns).astype(bf16)
        for z in z_order:
            w_q[1].start(z)

    for act in schedule(SimpleNamespace(**ops)):
        act()

    for exchange in (g_wq, g_wf, g_pt, f_wq, f_wf, f_pt, *sum(w_fw, []), w_kv, w_pt, *w_q):
        exchange.sent()
    assert (taken[0], taken[1]) == (rsem.shape[0], ssem.shape[0]), taken
    for copy in pending:
        copy.wait_send()
    for copy in written:
        copy.wait()


def results_kernel(y, *refs):
    sources, targets, sems = refs[:5], refs[5:19], refs[-1]
    held = refs[19:-1]
    in_q, in_pt, in_fw, in_tok, in_out = held[:5]
    o_tok, o_pt, o_gate, o_up, o_down, o_pre, o_qh, o_qs, o_kh, o_ks, o_vh, o_vs, o_mid = held[5:]
    FM, F, half = y.FM, y.F, y.F - y.FM
    loads = [pltpu.make_async_copy(*pair, sems.at[i]) for i, pair in enumerate(zip(sources, held))]
    for load in loads:
        load.start()
    used = []

    def give(ref):
        place = len(used)
        used.append(pltpu.make_async_copy(ref, targets[place], sems.at[5 + place]))
        used[-1].start()

    loads[0].wait()
    o_qs[...] = in_q[:, :LANES].T[: y.SQ]
    second = in_q[:, LANES:].T
    o_ks[...] = second[y.oK : y.oK + y.SK]
    o_vs[...] = second[y.oV : y.oV + y.SK]
    o_qh[...] = second[y.oq : y.oq + y.HQ]
    o_kh[...] = second[y.ok : y.ok + y.HK]
    o_vh[...] = second[y.ov : y.ov + y.HK]
    o_pre[...] = second[y.og : y.og + 1]
    o_mid[...] = second[y.og + 1 : y.og + 2]
    for ref in (o_pre, o_qh, o_qs, o_kh, o_ks, o_vh, o_vs, o_mid):
        give(ref)
    loads[1].wait()
    for first in range(0, 256, LANES):
        o_pt[first : first + LANES, :] = in_pt[:, first : first + LANES].T
    give(o_pt)
    loads[2].wait()
    *whole_chunks, (base, wide, unit, _) = y.chunks
    for part, target in enumerate((o_gate, o_up, o_down)):
        for at, _, first_unit, _ in whole_chunks:
            for first in range(0, 256, LANES):
                place = at + part * 256 + first
                to = first_unit + first
                target[to : to + LANES, :] = in_fw[:, place : place + LANES].T
        place = base + (wide if part == 2 else part * LANES)
        target[unit:FM, :] = in_fw[:, place : place + LANES].T
        tail = base + (wide + LANES if part == 2 else 2 * LANES)
        tail = in_fw[:, tail : tail + LANES].T
        target[FM:, :] = tail[half:] if part == 1 else tail[:half]
        give(target)
    loads[3].wait()
    o_tok[...] = in_tok[...].astype(f32)
    give(o_tok)
    loads[4].wait()
    give(in_out)
    for copy in used:
        copy.wait()


def solution(mesh):
    W, N = mesh.shape["wide"], mesh.shape["narrow"]

    def on_device(
        tokens,
        documents,
        prenorm,
        qheads,
        qshared,
        kheads,
        kshared,
        vheads,
        vshared,
        project,
        midnorm,
        gating,
        upward,
        downward,
        cotangent,
    ):
        R, T, D = tokens.shape
        L = documents.shape[1]
        RW, F = gating.shape
        y = make_layout(W, N, T, D, F, L, N * kheads.shape[1] // KR)
        assert R == N
        scratch = scratch_list(y)
        gathers = [flag for parts in gather_parts for _, flag in parts]
        sums = [flag for parts in sum_parts for _, flag in parts]
        y_first, z_first = sum(gathers) + len(y_first_gathers), sum(sums) + len(z_first_sums)
        gathers, sums = 4 + len(gathers), 4 + len(sums)
        arrivals = gathers * (y.A + 1) + (3 - len(y_first_gathers)) * (y.A - 1)
        arrivals += 3 * (y.A + 2) + (8 + 4 * 2) + 6 + 9
        arrivals += z_first * (y.A + 2) + (sums - z_first) * (2 * y.A + 1)
        arrivals -= len(direct_sums) * y.A
        sends = 2 * gathers + y_first + 2 * sums + 48
        vmem = pl.BlockSpec(memory_space=pltpu.VMEM)

        def kernel(*refs):
            block_kernel(y, tuple(scratch), *refs)

        shape = jax.ShapeDtypeStruct
        raw = pl.pallas_call(
            kernel,
            out_shape=(
                shape((y.M, D), bf16),
                shape((y.M, D), bf16),
                shape((RW, y.FW), f32),
                shape((RW, 256), f32),
                shape((RW, 256), f32),
            ),
            in_specs=[vmem] * 9 + [pl.BlockSpec(memory_space=pl.ANY)] * 6,
            out_specs=[pl.BlockSpec(memory_space=pl.ANY)] * 5,
            scratch_shapes=[*scratch.values()]
            + [pltpu.SemaphoreType.DMA((count,)) for count in (sends, arrivals, sums + 1, 6)],
            compiler_params=pltpu.CompilerParams(
                collective_id=0, has_side_effects=True, vmem_limit_bytes=63 * 2**20
            ),
            name="block",
        )(
            documents,
            prenorm.reshape(1, RW),
            qheads.T,
            qshared.T,
            kheads.T,
            kshared.T,
            vheads.T,
            vshared.T,
            midnorm.reshape(1, RW),
            project,
            gating.T,
            upward.T,
            downward,
            tokens.reshape(y.M, D),
            cotangent.reshape(y.M, D),
        )

        def results(*refs):
            results_kernel(y, *refs)

        large = [((256, RW), f32), *[((F, RW), f32)] * 3, ((y.M, D), f32), ((y.M, D), bf16)]
        small = [((count, RW), f32) for count in (1, y.HQ, y.SQ, y.HK, y.SK, y.HK, y.SK, 1)]
        held = [((RW, 256), f32), ((RW, 256), f32), ((RW, y.FW), f32), *[((y.M, D), bf16)] * 2]
        held += [large[4], *large[:4], *small]
        anywhere = pl.BlockSpec(memory_space=pl.ANY)
        outputs = pl.pallas_call(
            results,
            out_shape=[shape(*each) for each in small + large],
            in_specs=[anywhere] * 5,
            out_specs=[anywhere] * 14,
            scratch_shapes=[pltpu.VMEM(*each) for each in held] + [pltpu.SemaphoreType.DMA((19,))],
            compiler_params=pltpu.CompilerParams(vmem_limit_bytes=63 * 2**20),
            name="results",
        )(*raw[::-1])
        pre, qh, qs, kh, ks, vh, vs, mid, pt_back, gate, up, down, tok, out = outputs
        tokens_like = lambda values: values.reshape(R, T, D)
        return (
            tokens_like(out),
            tokens_like(tok),
            pre.reshape(RW),
            *[each.T for each in (qh, qs, kh, ks, vh, vs)],
            pt_back,
            mid.reshape(RW),
            gate.T,
            up.T,
            down,
        )

    split = P("wide", "narrow")
    flipped = P("narrow", "wide")
    whole = P(None, "wide", None)
    gain = P("wide")
    return jax.shard_map(
        on_device,
        mesh=mesh,
        in_specs=(
            whole,
            P(),
            gain,
            split,
            split,
            split,
            split,
            split,
            split,
            flipped,
            gain,
            split,
            split,
            flipped,
            whole,
        ),
        out_specs=(
            whole,
            whole,
            gain,
            split,
            split,
            split,
            split,
            split,
            split,
            flipped,
            gain,
            split,
            split,
            flipped,
        ),
        check_vma=False,
    )
```

```python
import math
from types import SimpleNamespace

import jax
import jax.numpy as jnp
from jax import lax
from jax.experimental import pallas as pl
from jax.experimental.pallas import tpu as pltpu
from jax.sharding import PartitionSpec as P

DH = 64
QR = 6
KR = 2
VR = 2
LANES = 128

epsilon = 1e-06
masked_score = -1e30
MESH = pl.DeviceIdType.MESH
gather_parts = (((768, False),), ((512, True), (256, False)), ((384, True), (256, False)))
sum_parts = (((512, False), (256, True)), ((512, False), (256, True)), ((640, False),))
chunk_order = (0, 1, 2)
y_first_gathers = ()
z_first_sums = ()
direct_sums = ("wkv", "wqa", "wqb")
f32 = jnp.float32
bf16 = jnp.bfloat16


def dot_nn(a, b):
    return lax.dot_general(a, b, (((1,), (0,)), ((), ())), preferred_element_type=f32)


def dot_nt(a, b):
    return lax.dot_general(a, b, (((1,), (1,)), ((), ())), preferred_element_type=f32)


def dot_tn(a, b):
    return lax.dot_general(a, b, (((0,), (0,)), ((), ())), preferred_element_type=f32)


def lane_iota(rows, cols=LANES):
    return lax.broadcasted_iota(jnp.int32, (rows, cols), 1)


def row_iota(rows, cols=LANES):
    return lax.broadcasted_iota(jnp.int32, (rows, cols), 0)


def place_lanes(pieces):
    rows = pieces[0][0].shape[0]
    lane = lane_iota(rows)
    result = jnp.zeros((rows, LANES), f32)
    for tile, start, to, count in pieces:
        shift = (to - start) % LANES
        moved = pltpu.roll(tile, shift, 1) if shift else tile
        result = jnp.where((lane >= to) & (lane < to + count), moved, result)
    return result


def canonical_pieces(tiles, width, first, count, start, to):
    pieces = []
    while count:
        part, inside = divmod(first, width)
        take = min(count, width - inside)
        pieces.append((tiles[part], start + inside, to, take))
        first, to, count = first + take, to + take, count - take
    return pieces


def swap_quarters(tile):
    low = lane_iota(tile.shape[0]) % DH < DH // 2
    return jnp.where(low, pltpu.roll(tile, LANES - DH // 2, 1), pltpu.roll(tile, DH // 2, 1))


def stack_pair(tile):
    low = lane_iota(tile.shape[0]) < DH
    zero = jnp.zeros_like(tile)
    return jnp.concatenate([jnp.where(low, tile, zero), jnp.where(low, zero, tile)], axis=0)


def unstack_pair(rows):
    half = rows.shape[0] // 2
    low = lane_iota(half) < DH
    return jnp.where(low, rows[:half], rows[half:])


def pack_heads(tile):
    quarter = tile.shape[0] // 4
    low = lane_iota(quarter) < DH
    parts = [tile[i * quarter : (i + 1) * quarter] for i in range(4)]
    pairs = [
        jnp.where(low, parts[i], pltpu.roll(parts[i + 1], DH, 1)) for i in (0, 2)
    ]
    return jnp.concatenate(pairs, axis=1)


def unpack_heads(rows):
    tiles = (rows[:, :LANES], rows[:, LANES:])
    parts = [part for tile in tiles for part in (tile, pltpu.roll(tile, DH, 1))]
    return jnp.concatenate(parts, axis=0)


def fold_halves(tile):
    return tile + pltpu.roll(tile, DH, 1)


def row_scale(values):
    return lax.rsqrt(jnp.mean(values * values, axis=-1, keepdims=True) + epsilon)


def make_layout(W, N, T, D, F, L, heads):
    lay = SimpleNamespace()
    lay.W, lay.N, lay.T, lay.D, lay.F, lay.L, lay.heads = W, N, T, D, F, L, heads
    lay.A = W // 2
    lay.RW = D // W
    lay.M = N * T
    lay.KT = T + T // 4
    lay.FM = F // LANES * LANES
    lay.FP = lay.FM + LANES
    full = lay.FM // 256
    lay.chunks = [(768 * i, 512, 256 * i, 256) for i in range(full)]
    lay.chunks.append((768 * full, 3 * LANES, 256 * full, 256))
    lay.FW = 768 * full + 5 * LANES
    assert lay.FM % 256 == LANES
    lay.pairs = heads // 2
    assert len(lay.chunks) == 3
    lay.KB = L if L <= 1024 else 512
    lay.NB = L // lay.KB
    lay.SQ = QR * DH // N
    lay.SK = KR * DH // N
    lay.HQ = heads * QR // N
    lay.HK = heads * KR // N
    lay.oK, lay.oV = 0, lay.SK
    lay.oq = 2 * lay.SK
    lay.ok = lay.oq + lay.HQ
    lay.ov = lay.ok + lay.HK
    lay.og = lay.ov + lay.HK
    assert N == 4 and W % 8 == 0 and T == LANES and D == heads * DH == 1024
    assert F % LANES == DH and lay.SQ <= LANES and lay.og + 2 <= LANES
    return lay


def scratch_list(y):
    W, N, T, D, L, A, RW, M = y.W, y.N, y.T, y.D, y.L, y.A, y.RW, y.M
    vm = lambda *shape, kind=bf16: pltpu.VMEM(shape, kind)
    GUc = 2 * y.FM + LANES
    return dict(
        PIN=vm(256, RW),
        GIN=vm(y.F, RW),
        UIN=vm(y.F, RW),
        DIN=vm(y.F, RW),
        XIN=vm(M, D),
        CIN=vm(M, D),
        WQ=vm(N, D, 256),
        PT=vm(N, D, 256),
        FW=vm(D, y.FW),
        KVF=vm(L // T * y.KT, 256),
        KP=vm(y.pairs, LANES, y.KB),
        VP=vm(y.pairs, LANES, y.KB),
        EQ=vm(QR, LANES, D),
        SHARED=vm(2, LANES, y.KB, kind=f32),
        HT=vm(y.pairs, 8, y.KB, kind=f32),
        DHT=vm(y.pairs, 8, y.KB, kind=f32),
        BIAS=vm(T, y.KB, kind=f32),
        DOC=vm(T, LANES, kind=f32),
        ROPE=vm(2, T, LANES, kind=f32),
        GAIN=vm(8, D, kind=f32),
        QROT=vm(QR, T, LANES, kind=f32),
        QH=vm(T, 256),
        QP=vm(y.pairs, T, LANES),
        ATT=vm(y.pairs, T, LANES, kind=f32),
        LSE=vm(y.pairs, 2 * T, LANES, kind=f32),
        RUN=vm(y.pairs if y.NB > 1 else 1, 2 * T, LANES, kind=f32),
        MIX=vm(M, D),
        NORM=vm(M, D),
        MID=vm(M, D, kind=f32),
        NM=vm(M, D),
        R2=vm(M, LANES, kind=f32),
        HID=vm(M, y.FP),
        GG=vm(M, GUc),
        MB=vm(M, D),
        MBC=vm(2, T, D),
        MBX=vm(T, D),
        MBS=vm(T, D),
        OP=vm(M, D),
        OPC=vm(2, T, D),
        OPX=vm(T, D),
        OPS=vm(T, D),
        BG=vm(M, D),
        MG=vm(T, D, kind=f32),
        DO=vm(y.pairs, T, LANES),
        QB=vm(y.pairs, T, LANES, kind=f32),
        DST=vm(2, LANES, y.KB, kind=f32),
        DKVY=vm(A * y.KT, 256),
        DKVR=vm((A + 1) * y.KT * (1 + ("wkv" in z_first_sums)), 256),
        DKVO=vm(y.KT, 256, kind=f32),
        QGS=vm(N, T, 256),
        QGR=vm(N, T, 256),
        OUT=vm(M, D),
        TOK=vm(M, D),
        TFW=vm(RW, y.FW, kind=f32),
        TPT=vm(RW, 256, kind=f32),
        TQ=vm(RW, 256, kind=f32),
        GC=vm(D, LANES, kind=f32),
        GS=vm(8, D // 4, kind=f32),
        GR=vm(3, 8, D // 4, kind=f32),
        YFW=vm(A * RW, y.FW),
        **{
            f"RF{i}{j}": vm((A + 1) * RW * (1 + z_first), lanes)
            for i, parts in enumerate(sum_parts)
            for j, (lanes, z_first) in enumerate(parts)
        },
        PPT=vm(D, 256),
        YPT=vm(A * RW, 256),
        RPT=vm((A + 1) * RW * (1 + ("wpt" in z_first_sums)), 256),
        PQ=vm(D, 256),
        YQ=vm(A * RW, 256),
        RQ0=vm((A + 1) * RW, LANES),
        RQ1=vm((A + 1) * RW, LANES),
    )


def schedule(do):
    return (
        do.prep_wq, do.wf_Ly, do.wq_L, do.prep_pt, do.wq_Ly, do.prep_fw, do.b_Ly, do.wf_L,
        do.pt_L, do.wq_h1, do.fwq_s0, do.wf_h1, do.pt_Ly, do.c2_L, do.fwf_s0, do.wq_h2, do.a_L,
        do.fwq_s1, do.wf_h2, do.fwq_f0, do.wq_h3, do.c2_Ly, do.pt_h1, do.a_Ly, do.consts,
        do.fwq_s2, do.fwq_s3, do.fpt_s0, do.fwf_f0, do.fwq_f1, do.wf_h3, do.a_h1, do.fwf_s1,
        do.fwq_f2, do.pt_h2, do.fwq_f3, do.project, do.c_Ly, do.fpt_s1, do.kv_L, do.fwf_s2,
        do.c2_h1, do.kv_Ly, do.kv_h1, do.fpt_f0, do.pt_h3, do.fpt_s2, do.b2_L, do.fwf_f1,
        do.kv_h2, do.b2_Ly, do.a_h2, do.fwf_f2, do.fwf_s3, do.kv_h3, do.fpt_s3, do.c2_h2,
        do.fpt_f1, do.b2_h1, do.b_L, do.a_y1, do.a_y2, do.fwf_f3, do.queries, do.b2_y1, do.fpt_f2,
        do.at_x, do.at0, do.at1, do.at2, do.b2_h2, do.c2_h3, do.a_h3, do.a_y3, do.at3, do.mix_f0,
        do.b2_y2, do.b_h1, do.c2_y1, do.fpt_f3, do.c_L, do.b2_h3, do.b2_y3, do.mix_f1, do.c2_y2,
        do.mix_f2, do.mix_f3, do.c2_y3, do.middle, do.ff_a, do.g_a, do.g_a2, do.wa2_ends, do.b_h2,
        do.c_h1, do.wa_s0, do.b_h3, do.ff_b, do.g_b, do.g_b2, do.wb2_ends, do.c_h2, do.c_h3,
        do.ffCf, do.wb_s0, do.wa2_s1, do.mb_pass, do.wa_s1, do.ffCn, do.wa2_s2, do.wb2_s1, do.g_c,
        do.wb2_s2, do.op_start, do.wb_s1, do.mid, do.bq0, do.wc_s0, do.wa_s2, do.bq1, do.bq2,
        do.op_pass, do.wb_s2, do.bq3, do.kvst, do.wc_s1, do.qb, do.qg1, do.wkv_d0, do.bg_f,
        do.pt_g, do.wkv_d1, do.wkv_d2, do.op_res, do.wpt_s0, do.q_g1, do.wc_s2, do.wkv_fin, do.qg,
        do.fb1, do.fb, do.wpt_s1, do.og_f, do.tg_s, do.wqa_d0, do.wa2_fin, do.wqa_d1, do.wa_fin,
        do.wb_fin, do.q_g, do.wb2_fin, do.wqa_d2, do.og_l, do.wpt_s2, do.wqb_d0, do.wc_fin,
        do.wqa_fin, do.wa2_finy, do.wqb_d1, do.wqb_d2, do.tg_f, do.tg_l, do.wb2_finy, do.wpt_fin,
        do.wqb_fin,
    )


def block_kernel(y, names, *refs):
    docs, prenorm, qheads, qshared, kheads, kshared, vheads, vshared, midnorm = refs[:9]
    sources = refs[9:15]
    r_out, r_tok, r_fw, r_pt, r_q = refs[15:20]
    s = SimpleNamespace(**dict(zip(names, refs[20:])))
    ssem, rsem, wsem, lsem = refs[20 + len(names) :]
    o_out, o_tok, o_fw, o_pt, o_q = s.OUT, s.TOK, s.TFW, s.TPT, s.TQ
    written = []

    def write(src, dst):
        copy = pltpu.make_async_copy(src, dst, wsem.at[len(written)])
        copy.start()
        written.append(copy)

    project, gating, upward, downward, tok, cot = s.PIN, s.GIN, s.UIN, s.DIN, s.XIN, s.CIN
    loads = []
    for source, target in zip(sources, (project, gating, upward, downward, tok, cot)):
        loads.append(pltpu.make_async_copy(source, target, lsem.at[len(loads)]))
        loads[-1].start()

    W, N, T, D, F, L, A, RW, M = y.W, y.N, y.T, y.D, y.F, y.L, y.A, y.RW, y.M
    FM, FP, KB, pairs = y.FM, y.FP, y.KB, y.pairs
    w = lax.axis_index("wide")
    n = lax.axis_index("narrow")
    zi, yi = w // 2, w % 2
    xo, co = n // 2, n % 2
    y_peer = (zi * 2 + 1 - yi, n)
    c_peer = (w, xo * 2 + 1 - co)
    x_peer = (w, (1 - xo) * 2 + co)
    d_peer = (w, (1 - xo) * 2 + 1 - co)
    narrow_peers = (c_peer, x_peer, d_peer)
    taken = [0, 0]

    def take(count=1):
        taken[0] += count
        return taken[0] - count

    def take_send(count=1):
        taken[1] += count
        return taken[1] - count

    def remote(src, dst, k, peer, send_k):
        return pltpu.make_async_remote_copy(
            src_ref=src,
            dst_ref=dst,
            send_sem=ssem.at[send_k],
            recv_sem=rsem.at[k],
            device_id=peer,
            device_id_type=MESH,
        )

    def all_sent(ref, send_k):
        remote(ref, ref, 0, y_peer, send_k).wait_send()

    pending = []

    def send(src, dst, k, peer):
        copy = remote(src, dst, k, peer, take_send())
        copy.start()
        pending.append(copy)

    def arrive(dst, k):
        remote(dst, dst, k, y_peer, 0).wait_recv()

    def rows(ref, first, count, lanes=None):
        at = pl.ds(pl.multiple_of(first, 16), count)
        return ref.at[at] if lanes is None else ref.at[at, pl.ds(*lanes)]

    def each_at(distance, act):
        if distance == 0:
            act(zi, None)
            return
        pl.when(zi >= distance)(lambda: act(zi - distance, True))
        pl.when(zi + distance < A)(lambda: act(zi + distance, False))

    right_peer = ((zi + 1) * 2 + yi, n)
    left_peer = ((zi - 1) * 2 + yi, n)

    barrier = pltpu.get_barrier_semaphore()
    z_peers = [(((zi + step) % A) * 2 + yi, n) for step in range(1, A)]
    peers = [y_peer, *narrow_peers, *z_peers]
    for peer in peers:
        pl.semaphore_signal(barrier, inc=1, device_id=peer, device_id_type=MESH)
    pl.semaphore_wait(barrier, len(peers))

    class Gather:
        def __init__(self, ref, count, lanes=None, y_first=False, apart=False):
            self.ref, self.count, self.lanes, self.y_first = ref, count, lanes, y_first
            self.apart = apart and not y_first
            self.kz, self.ky = take(A), take(A if self.apart else 1)
            self.sy, self.sr = take_send(), take_send()
            self.sl = take_send() if y_first else self.sr
            self.next = self.next_y = 1

        def part(self, wide):
            return rows(self.ref, wide * self.count, self.count, self.lanes)

        def block(self, z):
            if self.y_first:
                return rows(self.ref, z * 2 * self.count, 2 * self.count, self.lanes)
            return self.part(z * 2 + yi)

        def along(self, z, to_right):
            block = self.block(z)
            if to_right:
                return remote(block, block, self.kz + z, right_peer, self.sr)
            return remote(block, block, self.kz + z, left_peer, self.sl)

        def across(self, z):
            part = self.part(z * 2 + yi)
            return remote(part, part, self.ky + (z if self.apart else 0), y_peer, self.sy)

        def landed(self, z):
            arrive(self.part(z * 2 + 1 - yi), self.ky + (z if self.apart else 0))

        def launch_y(self):
            self.across(zi).start()

        def launch(self):
            if self.y_first:
                self.landed(zi)
            pl.when(zi < A - 1)(lambda: self.along(zi, True).start())
            pl.when(zi > 0)(lambda: self.along(zi, False).start())

        def hop(self, distance, across):
            def act(z, to_right):
                arrive(self.block(z), self.kz + z)
                more = zi < A - 1 if to_right else zi > 0
                pl.when(more)(lambda: self.along(z, to_right).start())
                if across and not self.y_first:
                    self.across(z).start()

            each_at(distance, act)

        def pump(self, count=A, across=True):
            for _ in range(min(count, A - self.next)):
                self.hop(self.next, across)
                self.next += 1

        def pump_y(self, count=A):
            for _ in range(min(count, self.next - self.next_y)):
                each_at(self.next_y, lambda z, _: self.across(z).start())
                self.next_y += 1

        def landed_all(self):
            if not self.y_first:
                arrive(rows(self.ref, 0, A * self.count, self.lanes), self.ky)

        def sent(self):
            def blocks(count):
                return rows(self.ref, 0, count * self.count, self.lanes)

            all_sent(blocks(1 if self.y_first else A), self.sy)
            if self.y_first:
                for z in range(A - 1):
                    pl.when(zi == z)(lambda: all_sent(blocks(2 * z + 2), self.sr))
                    pl.when(zi == z + 1)(lambda: all_sent(blocks(2 * (A - z - 1)), self.sl))
                return
            inner = (zi > 0) & (zi < A - 1)
            pl.when(inner)(lambda: all_sent(blocks(A + 1), self.sr))
            pl.when(jnp.logical_not(inner))(lambda: all_sent(blocks(1), self.sr))

    class Spread:
        def __init__(self, gather, ref):
            self.gather, self.ref, self.lanes = gather, ref, gather.lanes
            self.next = self.passed = 0
            self.kx, self.kc, self.kd = take(A), take(), take()
            self.sx, self.sc, self.sd = take_send(), take_send(), take_send()

        def part(self, owner, z):
            return rows(self.ref.at[owner], z * 2 * RW, 2 * RW, self.lanes)

        def copies(self, z):
            part = self.part(n, z)
            to_x = remote(part, part, self.kx + z, x_peer, self.sx)
            return to_x, remote(part, part, self.kc, c_peer, self.sc)

        def onward(self, z):
            part = self.part(x_peer[1], z)
            return remote(part, part, self.kd, c_peer, self.sd)

        def start(self, distance):
            def act(z, _):
                if not self.gather.y_first:
                    self.gather.landed(z)
                for copy in self.copies(z):
                    copy.start()

            each_at(distance, act)

        def pump(self, count=A):
            for _ in range(min(count, A - self.next)):
                self.start(self.next)
                self.next += 1

        def pump_forward(self, count=A):
            for _ in range(min(count, A - self.passed)):
                self.forward(self.passed)
                self.passed += 1

        def forward(self, distance):
            def act(z, _):
                arrive(self.part(x_peer[1], z), self.kx + z)
                self.onward(z).start()

            each_at(distance, act)

        def landed(self):
            for peer, k in ((c_peer, self.kc), (d_peer, self.kd)):
                arrive(rows(self.ref.at[peer[1]], 0, D, self.lanes), k)

        def sent(self):
            for k in (self.sx, self.sc, self.sd):
                all_sent(rows(self.ref.at[n], 0, D, self.lanes), k)

    class Share:
        def __init__(self, ref, chunks):
            self.ref, self.chunks = ref, chunks
            self.kx, self.kc, self.kd = take(chunks), take(), take()
            self.width = D // chunks

        def part(self, owner, chunk):
            lanes = pl.ds(pl.multiple_of(chunk * self.width, LANES), self.width)
            return self.ref.at[pl.ds(pl.multiple_of(owner * T, T), T), lanes]

        def start(self, chunk):
            send(self.part(n, chunk), self.part(n, chunk), self.kx + chunk, x_peer)
            send(self.part(n, chunk), self.part(n, chunk), self.kc, c_peer)

        def forward(self, chunk):
            part = self.part(x_peer[1], chunk)
            arrive(part, self.kx + chunk)
            send(part, part, self.kd, c_peer)

        def forward_all(self):
            for chunk in range(self.chunks):
                self.forward(chunk)

        def landed_all(self):
            for peer, k in ((c_peer, self.kc), (d_peer, self.kd)):
                arrive(rows(self.ref, peer[1] * T, T), k)

    class NarrowSum:
        def __init__(self, part_ref, core_ref, x_ref, send_ref):
            self.ref, self.core, self.x, self.out = part_ref, core_ref, x_ref, send_ref
            self.kc, self.kx = take(2), take(1)

        def part(self, owner):
            return rows(self.ref, owner * T, T)

        def start(self, far):
            owner = ((1 - xo) if far else xo) * 2 + 1 - co
            send(self.part(owner), self.core.at[int(far)], self.kc + int(far), c_peer)

        def pass_on(self):
            arrive(self.core.at[1], self.kc + 1)
            total = self.part((1 - xo) * 2 + co)[...].astype(f32) + self.core[1].astype(f32)
            self.out[...] = total.astype(bf16)
            send(self.out, self.x, self.kx, x_peer)

        def result(self):
            arrive(self.core.at[0], self.kc)
            arrive(self.x, self.kx)
            return (
                self.part(n)[...].astype(f32) + self.core[0].astype(f32) + self.x[...].astype(f32)
            )

    class WideSum:
        def __init__(
            self, part_ref, y_ref, z_ref, out_ref, count, lanes=None, z_first=False, straight=False
        ):
            self.ref, self.y, self.z, self.total = part_ref, y_ref, z_ref, out_ref
            self.count, self.lanes, self.z_first = count, lanes, z_first
            self.size = 2 * count if z_first else count
            self.next = 0
            self.z_lanes = lanes and (0, lanes[1])
            self.ky, self.kz = take(1 if z_first else A), take(1 if straight else A + 1)
            self.sy, self.sz = take_send(), take_send()

        def part(self, wide):
            return rows(self.ref, wide * self.count, self.count, self.lanes)

        def block(self, z):
            if self.z_first:
                return rows(self.ref, z * 2 * self.count, 2 * self.count, self.lanes)
            return self.part(z * 2 + yi)

        def got_y(self, z):
            return rows(self.y, z * self.count, self.count, self.lanes)

        def got_z(self, slot):
            return rows(self.z, slot * self.size, self.size, self.z_lanes)

        def across(self, z):
            return remote(self.part(z * 2 + 1 - yi), self.got_y(z), self.ky + z, y_peer, self.sy)

        def along(self, z, to_right):
            block = self.block(z)
            if to_right:
                return remote(block, self.got_z(z), self.kz + z, right_peer, self.sz)
            slot = jnp.where(z == zi - 1, A, z)
            return remote(block, self.got_z(slot), self.kz + slot, left_peer, self.sz)

        def start(self, z):
            if not self.z_first:
                self.across(z).start()

        def gather_y(self, z):
            block = self.block(z)[...].astype(f32)
            if self.z_first:
                return block
            arrive(self.got_y(z), self.ky + z)
            return block + self.got_y(z)[...].astype(f32)

        def stage(self, step):
            def move(z, to_right, joined):
                value = self.gather_y(z)
                if joined:
                    arrive(self.got_z(z), self.kz + z)
                    value = value + self.got_z(z)[...].astype(f32)
                self.block(z)[...] = value.astype(bf16)
                self.along(z, to_right).start()

            right, left = A - 1 - step + zi, step - (A - 1 - zi)
            to_right = (right < A) & (right > zi)
            to_left = (left >= 0) & (left < zi)
            pl.when(to_right & (zi > 0))(lambda: move(right, True, True))
            pl.when(to_left & (zi < A - 1))(lambda: move(left, False, True))
            if not self.z_first:
                pl.when(to_right & (zi == 0))(lambda: move(right, True, False))
                pl.when(to_left & (zi == A - 1))(lambda: move(left, False, False))

        def pump(self, count=A):
            for _ in range(min(count, A - 1 - self.next)):
                self.stage(self.next)
                self.next += 1

        def send_direct(self, count=A):
            for k in range(self.next, min(self.next + count, A - 1)):
                self.next += 1
                z = z_order[k] if A == 4 else (zi + 1 + k) % A
                block = self.block(z)
                block[...] = self.gather_y(z).astype(bf16)
                self.direct(z).start()

        def direct(self, z):
            return remote(
                self.block(z), self.got_z(zi), self.kz, (z * 2 + yi, n), self.sz
            )

        def finish_direct(self):
            total = self.gather_y(zi)
            arrive(rows(self.z, 0, (A - 1) * self.size, self.z_lanes), self.kz)
            for step in range(1, A):
                total = total + self.got_z((zi + step) % A)[...].astype(f32)
            self.total[...] = total

        def start_ends(self):
            @pl.when(zi == 0)
            def _():
                for z in range(A - 1, 0, -1):
                    self.along(z, True).start()

            @pl.when(zi == A - 1)
            def _():
                for z in range(A - 1):
                    self.along(z, False).start()

        def add(self, slot):
            arrive(self.got_z(slot), self.kz + slot)
            got = self.got_z(slot)[...].astype(f32)
            if not self.z_first:
                self.total[...] += got
                return
            block = self.block(zi)
            block[...] = (block[...].astype(f32) + got).astype(bf16)

        def finish(self):
            if not self.z_first:
                self.total[...] = self.gather_y(zi)
            pl.when(zi > 0)(lambda: self.add(zi))
            pl.when(zi < A - 1)(lambda: self.add(A))
            if self.z_first:
                self.last_across().start()

        def last_across(self):
            return remote(self.part(zi * 2 + 1 - yi), self.got_y(0), self.ky, y_peer, self.sy)

        def finish_y(self):
            if self.z_first:
                arrive(self.got_y(0), self.ky)
                mine = self.part(zi * 2 + yi)[...].astype(f32)
                self.total[...] = mine + self.got_y(0)[...].astype(f32)

        def sent(self):
            def parts(count):
                return rows(self.ref, 0, count * self.count, self.lanes)

            all_sent(parts(1 if self.z_first else A), self.sy)
            all_sent(parts((A - 1) * (2 if self.z_first else 1)), self.sz)

    if A == 4:
        z_order = []
        for row in zip((3, 2, 1, 0), (3, 2, 0, 1), (0, 1, 3, 2), (0, 1, 2, 3)):
            z_order.append(sum(jnp.where(zi == at, z, 0) for at, z in enumerate(row)))
    else:
        z_order = range(A)

    chunks = y.chunks
    last = len(chunks) - 1
    cuts = [(base, wide + units) for base, wide, _, units in chunks]
    g_wq = Gather(s.WQ.at[n], RW, (LANES, LANES), "wq" in y_first_gathers, True)
    g_wf = Gather(s.WQ.at[n], RW, (0, LANES), "wf" in y_first_gathers, True)
    g_pt = Gather(s.PT.at[n], RW, y_first="pt" in y_first_gathers, apart=True)
    g_kv = Gather(s.KVF, y.KT, y_first="kv" in y_first_gathers)

    def in_parts(chunk, parts):
        first = cuts[chunk][0]
        for lanes, flag in parts[chunk]:
            yield (first, lanes), flag
            first += lanes

    g_fw = [[Gather(s.FW, RW, *part) for part in in_parts(i, gather_parts)] for i in range(3)]
    f_wq, f_wf, f_pt = Spread(g_wq, s.WQ), Spread(g_wf, s.WQ), Spread(g_pt, s.PT)
    h_mix, h_bg, h_og, h_tg = Share(s.MIX, 4), Share(s.BG, 1), Share(o_out, 1), Share(o_tok, 2)
    n_mb = NarrowSum(s.MB, s.MBC, s.MBX, s.MBS)
    n_op = NarrowSum(s.OP, s.OPC, s.OPX, s.OPS)
    kind_of = lambda name: (name in z_first_sums, name in direct_sums)
    w_kv = WideSum(s.KVF, s.DKVY, s.DKVR, s.DKVO, y.KT, None, *kind_of("wkv"))
    w_fw = [[], [], []]
    for i in range(3):
        for j, (lanes, z_first) in enumerate(in_parts(i, sum_parts)):
            out, got = o_fw.at[:, pl.ds(*lanes)], vars(s)[f"RF{i}{j}"]
            name = f"w{'abc'[chunk_order.index(i)]}{'2' if j else ''}"
            straight = name in direct_sums
            w_fw[i].append(WideSum(s.FW, s.YFW, got, out, RW, lanes, z_first, straight))
    w_pt = WideSum(s.PPT, s.YPT, s.RPT, o_pt, RW, None, *kind_of("wpt"))
    w_q, tiles = [], [(0, LANES), (LANES, LANES)]
    for lanes, got, name in zip(tiles, (s.RQ0, s.RQ1), ("wqa", "wqb")):
        out = o_q.at[:, pl.ds(*lanes)]
        w_q.append(WideSum(s.PQ, s.YQ, got, out, RW, lanes, *kind_of(name)))
    k_a2a, k_gain = (take(3), take(3)), take(3)

    ops = {}

    def op(name):
        def keep(act):
            ops[name] = act
            return act

        return keep

    def gather_ops(name, gather, split):
        ops[f"{name}_L"], ops[f"{name}_Ly"] = gather.launch, gather.launch_y
        for i in range(1, 4):
            count = A if i == 3 else 1
            ops[f"{name}_h{i}"] = lambda count=count: gather.pump(count, not split)
            if split and not gather.y_first:
                ops[f"{name}_y{i}"] = lambda count=count: gather.pump_y(count)

    def spread_ops(name, spread):
        for i in range(4):
            count = A if i == 3 else 1
            ops[f"{name}_s{i}"] = lambda count=count: spread.pump(count)
            ops[f"{name}_f{i}"] = lambda count=count: spread.pump_forward(count)

    def sum_ops(name, exchange, finish):
        for i in range(3):
            count = A if i == 2 else 1
            if name in direct_sums:
                ops[f"{name}_d{i}"] = lambda count=count: exchange.send_direct(count)
            else:
                extra = 1 if exchange.z_first and i == 1 else 0
                ops[f"{name}_s{i}"] = lambda count=count + extra: exchange.pump(count)
        if exchange.z_first:
            ops[f"{name}_ends"] = exchange.start_ends
            ops[f"{name}_finy"] = finish
            ops[f"{name}_fin"] = exchange.finish
        else:
            ops[f"{name}_fin"] = finish

    gather_ops("wq", g_wq, False)
    gather_ops("wf", g_wf, False)
    gather_ops("pt", g_pt, False)
    gather_ops("kv", g_kv, False)
    spread_ops("fwq", f_wq)
    spread_ops("fwf", f_wf)
    spread_ops("fpt", f_pt)

    def chunk_finish(exchange, name):
        if name in direct_sums:
            exchange.finish_direct()
        else:
            (exchange.finish_y if exchange.z_first else exchange.finish)()
        write(exchange.total, r_fw.at[:, pl.ds(*exchange.lanes)])

    for i, name in zip(chunk_order, "abc"):
        for gather, part in zip(g_fw[i], ("", "2")):
            gather_ops(name + part, gather, True)
        for exchange, part in zip(w_fw[i], ("", "2")):
            part = f"w{name}{part}"
            sum_ops(part, exchange, lambda at=exchange, name=part: chunk_finish(at, name))

    def factor_finish(name, exchange, target=None):
        if name in direct_sums:
            exchange.finish_direct()
        else:
            (exchange.finish_y if exchange.z_first else exchange.finish)()
        if target is not None:
            write(exchange.total, target)

    sum_ops("wkv", w_kv, lambda: factor_finish("wkv", w_kv))
    sum_ops("wpt", w_pt, lambda: factor_finish("wpt", w_pt, r_pt))
    for i, name in enumerate(("wqa", "wqb")):
        target = r_q.at[:, pl.ds(*tiles[i])]
        sum_ops(
            name,
            w_q[i],
            lambda i=i, name=name, target=target: factor_finish(name, w_q[i], target),
        )

    own = pl.ds(pl.multiple_of(w * RW, RW), RW)
    own_rows = pl.ds(pl.multiple_of(n * T, T), T)
    blank = lambda count, kind=bf16: jnp.zeros((count, RW), kind)
    held = SimpleNamespace()

    @op("prep_wq")
    def _():
        shared_part = jnp.concatenate([qshared[...].astype(f32), blank(LANES - y.SQ, f32)], axis=0)
        gain_row = row_iota(8, RW)
        gain_part = jnp.where(
            gain_row == 0,
            prenorm[...].astype(f32),
            jnp.where(gain_row == 1, midnorm[...].astype(f32), 0.0),
        )
        second_part = jnp.concatenate(
            [part[...].astype(f32) for part in (kshared, vshared, qheads, kheads, vheads)]
            + [gain_part, blank(LANES - y.og - 8, f32)],
            axis=0,
        )
        s.WQ[n, own, :LANES] = shared_part.T.astype(bf16)
        s.WQ[n, own, LANES:] = second_part.T.astype(bf16)

    @op("prep_pt")
    def _():
        loads[0].wait()
        for first in range(0, 256, LANES):
            s.PT[n, own, first : first + LANES] = project[first : first + LANES, :].T

    @op("prep_fw")
    def _():
        for load in loads[1:4]:
            load.wait()
        for base, wide, unit, _ in chunks[:last]:
            for part, weight in enumerate((gating, upward, downward)):
                for first in range(0, 256, LANES):
                    to = base + part * 256 + first
                    s.FW[own, to : to + LANES] = weight[unit + first : unit + first + LANES, :].T
        base, wide, unit, _ = chunks[last]
        s.FW[own, base : base + LANES] = gating[unit:FM, :].T
        s.FW[own, base + LANES : base + 2 * LANES] = upward[unit:FM, :].T
        s.FW[own, base + 2 * LANES : base + wide] = jnp.concatenate(
            [gating[FM:, :], upward[FM:, :]], axis=0
        ).T
        s.FW[own, base + wide : base + wide + LANES] = downward[unit:FM, :].T
        s.FW[own, base + wide + LANES :] = jnp.concatenate(
            [downward[FM:, :], blank(FP - F)], axis=0
        ).T

    def own_row(values):
        mine = row_iota(N, values.shape[1]) == n
        return jnp.sum(jnp.where(mine, values.astype(f32), 0.0), axis=0, keepdims=True)

    def mask_block(block):
        first = block * KB
        key_docs = own_row(docs[:, pl.ds(pl.multiple_of(first, KB), KB)])
        allowed = (lane_iota(T, KB) + first <= row_iota(T, KB) + w * T) & (
            key_docs == s.DOC[:, :1]
        )
        s.BIAS[...] = jnp.where(allowed, 0.0, masked_score)

    @op("consts")
    def _():
        column, head = row_iota(LANES, D), lane_iota(LANES, D) >> 6
        for r in range(QR):
            s.EQ[r] = jnp.where(column == head * QR + r, 1.0, 0.0).astype(bf16)
        place = (w * T + row_iota(T)).astype(f32)
        lane = lane_iota(T)
        angle = place * jnp.exp((lane % (DH // 2)).astype(f32) * (-math.log(10000.0) / (DH // 2)))
        s.ROPE[0] = jnp.cos(angle)
        s.ROPE[1] = jnp.where(lane % DH < DH // 2, -jnp.sin(angle), jnp.sin(angle))

        own_docs = own_row(docs[:, pl.ds(pl.multiple_of(w * T, T), T)])
        own_docs = jnp.transpose(jnp.broadcast_to(own_docs, (T, T)))
        s.DOC[...] = own_docs

        mask_block(0)

    def rotated(tile, back=False):
        turned = swap_quarters(tile) * s.ROPE[1]
        return tile * s.ROPE[0] - turned if back else tile * s.ROPE[0] + turned

    def collect(start, width):
        pieces = []
        for p in range(N):
            pieces += [(held.second_tiles[p], start, p * width, width)]
        return place_lanes(pieces)

    @op("project")
    def _():
        loads[4].wait()
        f_wq.landed()
        gains = s.WQ[0, :, LANES:].astype(f32).T
        s.GAIN[0:1, :] = gains[y.og : y.og + 1]
        s.GAIN[1:2, :] = gains[y.og + 1 : y.og + 2]

        x_own = tok[own_rows, :].astype(f32)
        r1_own = row_scale(x_own)
        normed_own = (x_own * r1_own * s.GAIN[0:1, :]).astype(bf16)
        held.normed_own = normed_own
        held.second_tiles = [dot_nn(normed_own, s.WQ[p, :, LANES:]) for p in range(N)]

        kv_own = pl.ds(pl.multiple_of(w * T, T), T)
        kv_own = pl.multiple_of(w * y.KT, 32)
        s.KVF[pl.ds(kv_own, T), 0:128] = rotated(collect(y.oK, y.SK)).astype(bf16)
        s.KVF[pl.ds(kv_own, T), 128:256] = collect(y.oV, y.SK).astype(bf16)
        heads = place_lanes(
            [(held.second_tiles[p], y.ok, p * y.HK, y.HK) for p in range(N)]
            + [(held.second_tiles[p], y.ov, (N + p) * y.HK, y.HK) for p in range(N)]
        )
        s.KVF[pl.ds(kv_own + T, T // 4), :] = pack_heads(heads).astype(bf16)

    def spread_heads(r):
        return dot_nn(s.QH[:, :LANES], s.EQ[r]) + dot_nn(s.QH[:, LANES:], s.EQ[r])

    @op("queries")
    def _():
        f_wf.landed()
        held.first_tiles = [dot_nn(held.normed_own, s.WQ[p, :, :LANES]) for p in range(N)]
        query_heads = collect(y.oq, y.HQ)
        heads_high = query_heads.astype(bf16)
        s.QH[:, :LANES] = heads_high
        s.QH[:, LANES:] = (query_heads - heads_high.astype(f32)).astype(bf16)

        queries = jnp.zeros((T, D), f32)
        for r in range(QR):
            pieces = canonical_pieces(held.first_tiles, y.SQ, r * DH, DH, 0, 0)
            pieces += canonical_pieces(held.first_tiles, y.SQ, r * DH, DH, 0, DH)
            turned = rotated(place_lanes(pieces))
            s.QROT[r] = turned
            queries = queries + spread_heads(r) * jnp.concatenate([turned] * pairs, axis=1)
        for i in range(pairs):
            tile = (queries[:, i * LANES : (i + 1) * LANES] * (1.0 / QR)).astype(bf16)
            s.QP[i] = tile * jnp.asarray(DH**-0.5, bf16)

        def norm_rows(block, _):
            at = pl.ds(pl.multiple_of(block * T, T), T)
            values = tok[at, :].astype(f32)
            s.NORM[at, :] = (values * row_scale(values) * s.GAIN[0:1, :]).astype(bf16)
            return 0

        lax.fori_loop(0, N, norm_rows, 0)

    def expand_block(block):
        tiles = []
        for t in range(KB // T):
            first = pl.multiple_of((block * (KB // T) + t) * y.KT, 32)
            lanes = slice(t * T, (t + 1) * T)
            for kind in range(2):
                shared = s.KVF[pl.ds(first, T), kind * 128 : kind * 128 + 128]
                s.SHARED[kind, :, lanes] = shared.astype(f32).T
            tiles.append(unpack_heads(s.KVF[pl.ds(first + T, T // 4), :].astype(f32)).T)
        heads = jnp.concatenate(tiles, axis=1)
        for i in range(pairs):
            for kind in range(2):
                first = kind * y.heads * KR + 4 * i
                s.HT[i, 4 * kind : 4 * kind + 4, :] = heads[first : first + 4]

        def expand(i, _):
            for kind, ref in enumerate((s.KP, s.VP)):
                one, two = s.SHARED[kind, :DH, :], s.SHARED[kind, DH:, :]
                for half in range(2):
                    row = 4 * kind + 2 * half
                    joined = s.HT[i, row : row + 1, :] * one + s.HT[i, row + 1 : row + 2, :] * two
                    ref[i, half * DH : (half + 1) * DH, :] = (joined * 0.5).astype(bf16)
            return 0

        lax.fori_loop(0, pairs, expand, 0)

    def pair_bias():
        bias = s.BIAS[...]
        return jnp.concatenate([bias, bias], axis=0)

    def forward_pair(i):
        scores = dot_nn(stack_pair(s.QP[i]), s.KP[i]) + pair_bias()
        top = jnp.max(scores, axis=1, keepdims=True)
        if y.NB > 1:
            old_top = s.LSE[i][:, :1]
            top = jnp.maximum(top, old_top)
        weights = jnp.exp(scores - top)
        total = jnp.sum(weights, axis=1, keepdims=True)
        rows_out = dot_nt(weights.astype(bf16), s.VP[i])
        if y.NB > 1:
            factor = jnp.exp(old_top - top)
            total = total + s.RUN[i][:, :1] * factor
            s.LSE[i] = jnp.broadcast_to(top, (2 * T, LANES))
            s.RUN[i] = jnp.broadcast_to(total, (2 * T, LANES))
            keep = stack_pair(s.ATT[i]) * factor
            s.ATT[i] = unstack_pair(rows_out + keep)
        return top, total, rows_out

    def store_mixture(i, attended, top, total):
        s.ATT[i] = attended
        s.LSE[i] = jnp.broadcast_to(top + jnp.log(total), (2 * T, LANES))
        s.MIX[own_rows, pl.ds(pl.multiple_of(i * LANES, LANES), LANES)] = attended.astype(bf16)

    def forward_step(i, _):
        top, total, rows_out = forward_pair(i)
        store_mixture(i, unstack_pair(rows_out / total), top, total)
        return 0

    @op("at_x")
    def _():
        g_kv.landed_all()
        if y.NB == 1:
            expand_block(0)
            return
        s.LSE[...] = jnp.full(s.LSE.shape, masked_score, f32)
        s.RUN[...] = jnp.zeros(s.RUN.shape, f32)
        s.ATT[...] = jnp.zeros(s.ATT.shape, f32)

        def forward_block(block, _):
            mask_block(block)
            expand_block(block)

            def step(i, _):
                forward_pair(i)
                return 0

            lax.fori_loop(0, pairs, step, 0)
            return 0

        lax.fori_loop(0, y.NB, forward_block, 0)

        def finish_step(i, _):
            total = s.RUN[i][:, :1]
            store_mixture(i, unstack_pair(stack_pair(s.ATT[i]) / total), s.LSE[i][:, :1], total)
            return 0

        lax.fori_loop(0, pairs, finish_step, 0)

    def forward_chunk(chunk):
        per = pairs // h_mix.chunks
        if y.NB == 1:
            lax.fori_loop(chunk * per, (chunk + 1) * per, forward_step, 0)
        h_mix.start(chunk)

    for i in range(h_mix.chunks):
        ops[f"at{i}"] = lambda i=i: forward_chunk(i)
        ops[f"mix_f{i}"] = lambda i=i: h_mix.forward(i)

    @op("middle")
    def _():
        loads[5].wait()
        h_mix.landed_all()
        f_pt.landed()
        def middle_rows(block, _):
            at = pl.ds(pl.multiple_of(block * 2 * T, 2 * T), 2 * T)
            values = tok[at, :].astype(f32)
            for p in range(N):
                values = values + dot_nt(s.MIX[at, p * 256 : (p + 1) * 256], s.PT[p])
            scale = row_scale(values)
            s.MID[at, :] = values
            s.R2[at, :] = jnp.broadcast_to(scale, (2 * T, LANES))
            s.NM[at, :] = (values * scale * s.GAIN[1:2, :]).astype(bf16)
            return 0

        lax.fori_loop(0, 2, middle_rows, 0)

    def gates(gate, up, pushed):
        chance = 1.0 / (1.0 + jnp.exp(-gate))
        silu = gate * chance
        back = pushed * up * chance * (1.0 + gate * (1.0 - chance))
        return silu * up, back, pushed * silu

    tail_low = lane_iota(2 * T) < DH

    def dense_rows(chunk, far):
        base, wide, unit, units = chunks[chunk]
        first = sum(part[1] for part in chunks[:chunk])
        block = (1 - xo) if far else xo
        at = pl.ds(pl.multiple_of(block * 2 * T, 2 * T), 2 * T)
        both = dot_nn(s.NM[at, :], s.FW[:, base : base + wide])
        back = dot_nn(cot[at, :], s.FW[:, base + wide : base + wide + units])
        width = 256 if chunk < last else LANES
        hidden, gate_back, up_back = gates(
            both[:, :width], both[:, width : 2 * width], back[:, :width]
        )
        s.HID[at, unit : unit + width] = hidden.astype(bf16)
        s.GG[at, first : first + width] = gate_back.astype(bf16)
        s.GG[at, first + width : first + 2 * width] = up_back.astype(bf16)
        if chunk == last:
            tail = both[:, 2 * width :]
            hidden, gate_back, up_back = gates(tail, pltpu.roll(tail, DH, 1), back[:, width:])
            s.HID[at, unit + width :] = jnp.where(tail_low, hidden, 0.0).astype(bf16)
            up_back = pltpu.roll(up_back, DH, 1)
            s.GG[at, first + 2 * width :] = jnp.where(tail_low, gate_back, up_back).astype(bf16)
        mid = dot_nt(s.GG[at, first : first + wide], s.FW[:, base : base + wide])
        out = dot_nt(s.HID[at, unit : unit + units], s.FW[:, base + wide : base + wide + units])
        if chunk != chunk_order[0]:
            mid = mid + s.MB[at, :].astype(f32)
            out = out + s.OP[at, :].astype(f32)
        s.MB[at, :] = mid.astype(bf16)
        s.OP[at, :] = out.astype(bf16)

    def grad_blocks(target, to, left, right, lanes, exchange, begin):
        per = A // 4
        for j in range(4):
            block = z_order[j] if A == 4 else j
            at = pl.ds(pl.multiple_of(block * 256, 256), 256)
            value = dot_tn(left[:, at], right[:, lanes]).astype(bf16)
            target[at, to : to + value.shape[1]] = value
            if begin and not exchange.z_first:
                for q in range(per):
                    exchange.start(block * per + q)

    def dense_grads(chunk, part):
        base, wide, unit, units = chunks[chunk]
        first = sum(part[1] for part in chunks[:chunk])
        one, two = w_fw[chunk][0], w_fw[chunk][-1]
        if part == 0:
            for gather in g_fw[chunk]:
                gather.sent()
            grad_blocks(s.FW, base, s.NM, s.GG, slice(first, first + wide), one, one is not two)
        if part == 1 or one is two:
            units = slice(unit, unit + units)
            grad_blocks(s.FW, base + wide, cot, s.HID, units, two, True)

    def dense_chunk(chunk):
        for gather in g_fw[chunk]:
            gather.landed_all()
        dense_rows(chunk, True)
        dense_rows(chunk, False)

    for i, name in zip(chunk_order, "abc"):
        ops["ff_" + name] = lambda i=i: dense_chunk(i)
        for part, end in enumerate(("", "2")[: len(w_fw[i])]):
            ops["g_" + name + end] = lambda i=i, part=part: dense_grads(i, part)

    def last_dense(far):
        if far:
            for gather in g_fw[chunk_order[-1]]:
                gather.landed_all()
        dense_rows(chunk_order[-1], far)
        n_mb.start(far)

    ops["ffCf"] = lambda: last_dense(True)
    ops["ffCn"] = lambda: last_dense(False)
    ops["mb_pass"] = n_mb.pass_on

    @op("op_start")
    def _():
        n_op.start(True)
        n_op.start(False)

    ops["op_pass"] = n_op.pass_on

    def keep_gain(which, row):
        for i in range(4):
            place = 4 * which + i
            s.GS[place : place + 1, :] = row[:, i * (D // 4) : (i + 1) * (D // 4)]

    @op("mid")
    def _():
        mid_back = n_mb.result()
        mid_own = s.MID[own_rows, :]
        r2_own = s.R2[own_rows, :][:, :1]
        scaled = mid_back * s.GAIN[1:2, :]
        keep_gain(1, jnp.sum(mid_back * mid_own * r2_own, axis=0, keepdims=True))
        middle_gradient = (
            cot[own_rows, :].astype(f32)
            + r2_own * scaled
            - mid_own * (r2_own * r2_own * r2_own) * jnp.mean(scaled * mid_own, axis=-1, keepdims=True)
        )
        s.MG[...] = middle_gradient
        branch = middle_gradient.astype(bf16)
        s.BG[own_rows, :] = branch
        h_bg.start(0)
        for p in range(N):
            part = dot_nn(branch, s.PT[p]).astype(bf16)
            s.DO[2 * p] = part[:, :LANES]
            s.DO[2 * p + 1] = part[:, LANES:]

    def backward_part(block, part):
        if part == 0:
            s.DST[...] = jnp.zeros(s.DST.shape, f32)

        def step(i, _):
            query, pushed = s.QP[i], s.DO[i]
            query2, pushed2 = stack_pair(query), stack_pair(pushed)
            product = pushed.astype(f32) * s.ATT[i]
            delta = jnp.sum(stack_pair(product), axis=1, keepdims=True)
            scores = dot_nn(query2, s.KP[i]) + pair_bias()
            chance = jnp.exp(scores - jnp.concatenate([s.LSE[i]] * (KB // LANES), axis=1))
            gradient = (chance * (dot_nn(pushed2, s.VP[i]) - delta)).astype(bf16)
            s.QB[i] = s.QB[i] + unstack_pair(dot_nt(gradient, s.KP[i])) * DH**-0.5
            key_back = dot_tn(query2, gradient)
            value_back = dot_tn(pushed2, chance.astype(bf16))
            for kind, back in enumerate((key_back, value_back)):
                for r in range(KR):
                    shared = slice(r * DH, (r + 1) * DH)
                    found = s.DST[kind, shared, :]
                    for half in range(2):
                        mine = back[half * DH : (half + 1) * DH]
                        row = 4 * kind + 2 * half + r
                        found = found + s.HT[i, row : row + 1, :] * mine
                        s.DHT[i, row : row + 1, :] = jnp.sum(
                            mine * s.SHARED[kind, shared, :], axis=0, keepdims=True
                        )
                    s.DST[kind, shared, :] = found
            return 0

        quarter = pairs // 4
        lax.fori_loop(part * quarter, (part + 1) * quarter, step, 0)
        if part < 3:
            return
        at = pl.ds(pl.multiple_of(block * KB, KB), KB)
        heads = [s.DHT[i, 4 * kind : 4 * kind + 4, :] for kind in range(2) for i in range(pairs)]
        heads.append(jnp.zeros((LANES - 8 * pairs, KB), f32))
        heads = jnp.concatenate(heads, axis=0) * 0.5
        for t in range(KB // T):
            first = pl.multiple_of((block * (KB // T) + t) * y.KT, 32)
            lanes = slice(t * T, (t + 1) * T)
            for kind in range(2):
                shared = (s.DST[kind, :, lanes] * 0.5).T
                s.KVF[pl.ds(first, T), kind * 128 : kind * 128 + 128] = shared.astype(bf16)
            s.KVF[pl.ds(first + T, T // 4), :] = pack_heads(heads[:, lanes].T).astype(bf16)

    def backward_quarter(part):
        if part == 0:
            s.QB[...] = jnp.zeros(s.QB.shape, f32)
            g_kv.sent()
        if y.NB == 1:
            backward_part(0, part)
        elif part == 0:

            def backward_step(block, _):
                mask_block(block)
                expand_block(block)
                for each in range(4):
                    backward_part(block, each)
                return 0

            lax.fori_loop(0, y.NB, backward_step, 0)

    for i in range(4):
        ops[f"bq{i}"] = lambda i=i: backward_quarter(i)

    @op("kvst")
    def _():
        for z in z_order:
            w_kv.start(z)

    ops["bg_f"] = h_bg.forward_all

    @op("pt_g")
    def _():
        h_bg.landed_all()
        mine = pl.ds(pl.multiple_of(n * 256, 256), 256)
        grad_blocks(s.PPT, 0, s.BG, s.MIX, mine, w_pt, True)

    @op("qb")
    def _():
        query_back = jnp.concatenate([s.QB[i] for i in range(pairs)], axis=1)
        heads_back = jnp.zeros((T, LANES), f32)
        shared_back = []
        for r in range(QR):
            turned = s.QROT[r]
            product = (query_back * jnp.concatenate([turned] * pairs, axis=1)).astype(bf16)
            heads_back = heads_back + dot_nt(product, s.EQ[r])
            product = spread_heads(r) * query_back
            total = product[:, :LANES]
            for i in range(1, pairs):
                total = total + product[:, i * LANES : (i + 1) * LANES]
            shared_back.append(fold_halves(total))
        low = lane_iota(T) < DH
        held.shared_tiles = [
            rotated(jnp.where(low, shared_back[2 * t], shared_back[2 * t + 1]), back=True) * (1.0 / QR)
            for t in range(QR // 2)
        ]
        held.heads_back = heads_back * (1.0 / QR)

    @op("op_res")
    def _():
        o_out[own_rows, :] = (s.MID[own_rows, :] + n_op.result()).astype(bf16)
        h_og.start(0)

    ops["og_f"] = h_og.forward_all

    @op("og_l")
    def _():
        h_og.landed_all()
        write(o_out, r_out)

    ops["tg_f"] = h_tg.forward_all

    @op("tg_l")
    def _():
        h_tg.landed_all()
        write(o_tok, r_tok)

    def exchange_factors(tile):
        lanes = pl.ds(*tiles[tile])
        for k, peer in enumerate(narrow_peers):
            to = s.QGR.at[n, :, lanes]
            send(s.QGS.at[peer[1], :, lanes], to, k_a2a[tile] + k, peer)
        s.QGR[n, :, lanes] = s.QGS[n, :, lanes]

    def factors_through(tile):
        lanes = pl.ds(*tiles[tile])
        total = jnp.zeros((T, D), f32)
        for p in range(N):
            total = total + dot_nt(s.QGS[p, :, lanes], s.WQ[p, :, lanes])
        return total

    def factor_gradients(tile, added=None):
        lanes = pl.ds(*tiles[tile])
        for k, peer in enumerate(narrow_peers):
            arrive(s.QGR.at[peer[1], :, lanes], k_a2a[tile] + k)
        for j in range(4):
            at = pl.ds(j * 256, 256)
            value = jnp.zeros((256, LANES), f32)
            for p in range(N):
                value = value + dot_tn(s.NORM[p * T : (p + 1) * T, at], s.QGR[p, :, lanes])
            if added is not None:
                value = value + added[at, :]
            s.PQ[at, lanes] = value.astype(bf16)
        for z in z_order:
            w_q[tile].start(z)

    @op("qg1")
    def _():
        for p in range(N):
            s.QGS[p, :, :LANES] = place_lanes(
                canonical_pieces(held.shared_tiles, LANES, p * y.SQ, y.SQ, 0, 0)
            ).astype(bf16)
        exchange_factors(0)

    @op("fb1")
    def _():
        held.first_back = factors_through(0)

    @op("q_g1")
    def _():
        factor_gradients(0)

    @op("qg")
    def _():
        key_shared = rotated(s.DKVO[:T, 0:128], back=True)
        value_shared = s.DKVO[:T, 128:256]
        head_tile = unpack_heads(s.DKVO[T:, :])
        for p in range(N):
            s.QGS[p, :, LANES:] = place_lanes(
                [
                    (key_shared, p * y.SK, y.oK, y.SK),
                    (value_shared, p * y.SK, y.oV, y.SK),
                    (held.heads_back, p * y.HQ, y.oq, y.HQ),
                    (head_tile, p * y.HK, y.ok, y.HK),
                    (head_tile, (N + p) * y.HK, y.ov, y.HK),
                ]
            ).astype(bf16)
        exchange_factors(1)

    @op("fb")
    def _():
        first_back = held.first_back = held.first_back + factors_through(1)
        x_own = tok[own_rows, :].astype(f32)
        r1_own = row_scale(x_own)
        keep_gain(0, jnp.sum(first_back * x_own * r1_own, axis=0, keepdims=True))
        for k, peer in enumerate(narrow_peers):
            send(s.GS, s.GR.at[k], k_gain + k, peer)

    @op("tg_s")
    def _():
        first_back = held.first_back
        x_own = tok[own_rows, :].astype(f32)
        r1_own = row_scale(x_own)
        scaled = first_back * s.GAIN[0:1, :]
        tokens_gradient = (
            s.MG[...]
            + r1_own * scaled
            - x_own * (r1_own * r1_own * r1_own) * jnp.mean(scaled * x_own, axis=-1, keepdims=True)
        )
        o_tok[own_rows, :] = tokens_gradient.astype(bf16)
        for chunk in range(h_tg.chunks):
            h_tg.start(chunk)

    @op("q_g")
    def _():
        for k in range(3):
            arrive(s.GR.at[k], k_gain + k)
        packed = s.GS[...]
        for k in range(3):
            packed = packed + s.GR[k]
        gain_rows = [
            jnp.concatenate([packed[i : i + 1] for i in range(first, first + 4)], axis=1)
            for first in (0, 4)
        ]
        lane_row = row_iota(LANES, D)
        spread = jnp.where(
            lane_row == y.og,
            gain_rows[0],
            jnp.where(lane_row == y.og + 1, gain_rows[1], 0.0),
        )
        s.GC[...] = spread.T
        factor_gradients(1, s.GC)

    for act in schedule(SimpleNamespace(**ops)):
        act()

    for exchange in (g_wq, g_wf, g_pt, f_wq, f_wf, f_pt, *sum(w_fw, []), w_kv, w_pt, *w_q):
        exchange.sent()
    assert (taken[0], taken[1]) == (rsem.shape[0], ssem.shape[0]), taken
    for copy in pending:
        copy.wait_send()
    for copy in written:
        copy.wait()


def results_kernel(y, *refs):
    sources, targets, sems = refs[:5], refs[5:19], refs[-1]
    held = refs[19:-1]
    in_q, in_pt, in_fw, in_tok, in_out = held[:5]
    o_tok, o_pt, o_gate, o_up, o_down, o_pre, o_qh, o_qs, o_kh, o_ks, o_vh, o_vs, o_mid = held[5:]
    FM, F, half = y.FM, y.F, y.F - y.FM
    loads = [pltpu.make_async_copy(*pair, sems.at[i]) for i, pair in enumerate(zip(sources, held))]
    for load in loads:
        load.start()
    used = []

    def give(ref):
        place = len(used)
        used.append(pltpu.make_async_copy(ref, targets[place], sems.at[5 + place]))
        used[-1].start()

    loads[0].wait()
    o_qs[...] = in_q[:, :LANES].T[: y.SQ]
    second = in_q[:, LANES:].T
    o_ks[...] = second[y.oK : y.oK + y.SK]
    o_vs[...] = second[y.oV : y.oV + y.SK]
    o_qh[...] = second[y.oq : y.oq + y.HQ]
    o_kh[...] = second[y.ok : y.ok + y.HK]
    o_vh[...] = second[y.ov : y.ov + y.HK]
    o_pre[...] = second[y.og : y.og + 1]
    o_mid[...] = second[y.og + 1 : y.og + 2]
    for ref in (o_pre, o_qh, o_qs, o_kh, o_ks, o_vh, o_vs, o_mid):
        give(ref)
    loads[1].wait()
    for first in range(0, 256, LANES):
        o_pt[first : first + LANES, :] = in_pt[:, first : first + LANES].T
    give(o_pt)
    loads[2].wait()
    *whole_chunks, (base, wide, unit, _) = y.chunks
    for part, target in enumerate((o_gate, o_up, o_down)):
        for at, _, first_unit, _ in whole_chunks:
            for first in range(0, 256, LANES):
                place = at + part * 256 + first
                to = first_unit + first
                target[to : to + LANES, :] = in_fw[:, place : place + LANES].T
        place = base + (wide if part == 2 else part * LANES)
        target[unit:FM, :] = in_fw[:, place : place + LANES].T
        tail = base + (wide + LANES if part == 2 else 2 * LANES)
        tail = in_fw[:, tail : tail + LANES].T
        target[FM:, :] = tail[half:] if part == 1 else tail[:half]
        give(target)
    loads[3].wait()
    o_tok[...] = in_tok[...].astype(f32)
    give(o_tok)
    loads[4].wait()
    give(in_out)
    for copy in used:
        copy.wait()


def solution(mesh):
    W, N = mesh.shape["wide"], mesh.shape["narrow"]

    def on_device(
        tokens,
        documents,
        prenorm,
        qheads,
        qshared,
        kheads,
        kshared,
        vheads,
        vshared,
        project,
        midnorm,
        gating,
        upward,
        downward,
        cotangent,
    ):
        R, T, D = tokens.shape
        L = documents.shape[1]
        RW, F = gating.shape
        y = make_layout(W, N, T, D, F, L, N * kheads.shape[1] // KR)
        assert R == N
        scratch = scratch_list(y)
        gathers = [flag for parts in gather_parts for _, flag in parts]
        sums = [flag for parts in sum_parts for _, flag in parts]
        y_first, z_first = sum(gathers) + len(y_first_gathers), sum(sums) + len(z_first_sums)
        gathers, sums = 4 + len(gathers), 4 + len(sums)
        arrivals = gathers * (y.A + 1) + (3 - len(y_first_gathers)) * (y.A - 1)
        arrivals += 3 * (y.A + 2) + (8 + 4 * 2) + 6 + 9
        arrivals += z_first * (y.A + 2) + (sums - z_first) * (2 * y.A + 1)
        arrivals -= len(direct_sums) * y.A
        sends = 2 * gathers + y_first + 2 * sums + 48
        vmem = pl.BlockSpec(memory_space=pltpu.VMEM)

        def kernel(*refs):
            block_kernel(y, tuple(scratch), *refs)

        shape = jax.ShapeDtypeStruct
        raw = pl.pallas_call(
            kernel,
            out_shape=(
                shape((y.M, D), bf16),
                shape((y.M, D), bf16),
                shape((RW, y.FW), f32),
                shape((RW, 256), f32),
                shape((RW, 256), f32),
            ),
            in_specs=[vmem] * 9 + [pl.BlockSpec(memory_space=pl.ANY)] * 6,
            out_specs=[pl.BlockSpec(memory_space=pl.ANY)] * 5,
            scratch_shapes=[*scratch.values()]
            + [pltpu.SemaphoreType.DMA((count,)) for count in (sends, arrivals, sums + 1, 6)],
            compiler_params=pltpu.CompilerParams(
                collective_id=0, has_side_effects=True, vmem_limit_bytes=63 * 2**20
            ),
            name="block",
        )(
            documents,
            prenorm.reshape(1, RW),
            qheads.T,
            qshared.T,
            kheads.T,
            kshared.T,
            vheads.T,
            vshared.T,
            midnorm.reshape(1, RW),
            project,
            gating.T,
            upward.T,
            downward,
            tokens.reshape(y.M, D),
            cotangent.reshape(y.M, D),
        )

        def results(*refs):
            results_kernel(y, *refs)

        large = [((256, RW), f32), *[((F, RW), f32)] * 3, ((y.M, D), f32), ((y.M, D), bf16)]
        small = [((count, RW), f32) for count in (1, y.HQ, y.SQ, y.HK, y.SK, y.HK, y.SK, 1)]
        held = [((RW, 256), f32), ((RW, 256), f32), ((RW, y.FW), f32), *[((y.M, D), bf16)] * 2]
        held += [large[4], *large[:4], *small]
        anywhere = pl.BlockSpec(memory_space=pl.ANY)
        outputs = pl.pallas_call(
            results,
            out_shape=[shape(*each) for each in small + large],
            in_specs=[anywhere] * 5,
            out_specs=[anywhere] * 14,
            scratch_shapes=[pltpu.VMEM(*each) for each in held] + [pltpu.SemaphoreType.DMA((19,))],
            compiler_params=pltpu.CompilerParams(vmem_limit_bytes=63 * 2**20),
            name="results",
        )(*raw[::-1])
        pre, qh, qs, kh, ks, vh, vs, mid, pt_back, gate, up, down, tok, out = outputs
        tokens_like = lambda values: values.reshape(R, T, D)
        return (
            tokens_like(out),
            tokens_like(tok),
            pre.reshape(RW),
            *[each.T for each in (qh, qs, kh, ks, vh, vs)],
            pt_back,
            mid.reshape(RW),
            gate.T,
            up.T,
            down,
        )

    split = P("wide", "narrow")
    flipped = P("narrow", "wide")
    whole = P(None, "wide", None)
    gain = P("wide")
    return jax.shard_map(
        on_device,
        mesh=mesh,
        in_specs=(
            whole,
            P(),
            gain,
            split,
            split,
            split,
            split,
            split,
            split,
            flipped,
            gain,
            split,
            split,
            flipped,
            whole,
        ),
        out_specs=(
            whole,
            whole,
            gain,
            split,
            split,
            split,
            split,
            split,
            split,
            flipped,
            gain,
            split,
            split,
            flipped,
        ),
        check_vma=False,
    )
```
